256 devices in a mesh: gx: 8 (over z), gy: 4 (over x), gz: 8 (over y, core).
Axes of the slice: x: 4, y: 4, z: 8, core: 2. Of those that a mesh axis runs over, the one named last changes fastest.
Arguments:
- rhs: float32 [128, 512, 512], P('gx', 'gz', 'gy'), may hold values from -6 to 6
- mobility: float32 [128, 512, 512], P('gx', 'gz', 'gy'), may hold values from 0.1 to 1
- labels: int32 [128, 512, 512], P('gx', 'gz', 'gy'), may hold values from 0 to 15
- coarse_inverse: float32 [4096, 4096], P(('gx', 'gy', 'gz'))
Outputs:
- solution_field: float32 [128, 512, 512], P('gx', 'gz', 'gy')
- residual: float32 [128, 512, 512], P('gx', 'gz', 'gy')
The draws below stay inside these ranges and needn't reach their ends.
All inputs are finite; a program needn't handle non-finite values.
Results may differ from the reference program's by a relative error of at most 0.0003.
Values sent between devices are 32-bit elements; how exact they have to be, the bound alone decides.
A program may use at most 128 MiB of HBM per device.

```python
import math
import jax
import jax.numpy as jnp
from jax import lax

CX = 16
CY = 64
CZ = 128
DEFL = 16
ITERS = 3
NX = 128
NY = 512
NZ = 512
COARSE = 4096
N_GY = 4
N_GZ = 8


def draw_labels(key, part):
    key = jax.random.fold_in(key, 7)
    first, second = jax.random.split(key)
    along_x = (jnp.arange(NX, dtype=jnp.int32) % CX * 2 // CX)[:, None, None]
    along_z = (jnp.arange(NZ, dtype=jnp.int32) % CZ * (DEFL // 2) // CZ)[None, None, :]
    base = along_x * (DEFL // 2) + along_z + jnp.zeros((1, NY, 1), jnp.int32)
    flips = jax.random.randint(first, (NX, NY, NZ), 0, 8) == 0
    others = jax.random.randint(second, (NX, NY, NZ), 0, DEFL)
    return jnp.where(flips, others, base).astype(jnp.int32)


def draw_coarse_inverse(key, part):
    key = jax.random.fold_in(key, 11)
    first, second = jax.random.split(key)
    noise = jax.random.normal(first, (COARSE, COARSE), jnp.float32)
    spread = jnp.exp(jax.random.uniform(second, (COARSE,), jnp.float32, jnp.log(0.5), jnp.log(4.0)))
    scale = 1.0 / (CX * CY)
    twin = (noise + noise.T) * 0.70710678
    matrix = scale * (0.5 / jnp.sqrt(float(COARSE))) * twin + scale * jnp.diag(spread)
    return matrix.astype(jnp.float32)


def shard_levels(rng, dims, cuts, smallest, largest):
    gain = 1.0
    for dim, shards_of in cuts:
        steps = jax.random.uniform(jax.random.fold_in(jax.random.fold_in(rng, 6), dim), (shards_of,), jnp.float32, smallest / len(cuts), largest / len(cuts))
        gain = gain * jnp.repeat(jnp.exp(steps), dims[dim] // shards_of).reshape((-1,) + (1,) * (len(dims) - 1 - dim))
    return gain


def bell_draw(key, extent, scale, bound, pieces=(), held_as=jnp.bfloat16):
    level = shard_levels(key, extent, pieces, -0.22, 0.18) if pieces else 1.0
    array = jax.random.normal(key, extent, jnp.float32) * scale * level
    return jnp.minimum(jnp.maximum(array, -bound), bound).astype(held_as)


def setup_inputs(seed: int = 0) -> dict:
    arg_keys = jax.random.split(jax.random.key(seed), 5)
    rhs = bell_draw(arg_keys[0], (NX, NY, NZ), 1.0, 6.0, ((0, 8), (1, 8), (2, 4)), jnp.float32)
    mobility = jnp.clip(jnp.exp(math.log(1.0) - 2.3025851 * jax.random.uniform(arg_keys[1], (NX, NY, NZ), jnp.float32) ** shard_levels(arg_keys[1], (NX, NY, NZ), ((0, 8), (1, 8), (2, 4)), -0.2, 0.2)), 0.1, 1.0)
    labels = draw_labels(jax.random.fold_in(arg_keys[4], 71), 0)
    coarse_inverse = draw_coarse_inverse(jax.random.fold_in(arg_keys[4], 71), 0)
    return dict(rhs=rhs, mobility=mobility, labels=labels, coarse_inverse=coarse_inverse)


def faces(mobility):
    padded = jnp.pad(mobility, 1)
    face_x = 0.5 * (padded[1:, 1:-1, 1:-1] + padded[:-1, 1:-1, 1:-1])
    face_y = 0.5 * (padded[1:-1, 1:, 1:-1] + padded[1:-1, :-1, 1:-1])
    face_z = 0.5 * (padded[1:-1, 1:-1, 1:] + padded[1:-1, 1:-1, :-1])
    return face_x, face_y, face_z


def apply_operator(padded, field, face_x, face_y, face_z):
    total = face_x[1:] * (field - padded[2:, 1:-1, 1:-1]) + face_x[:-1] * (field - padded[:-2, 1:-1, 1:-1])
    total = total + face_y[:, 1:] * (field - padded[1:-1, 2:, 1:-1]) + face_y[:, :-1] * (field - padded[1:-1, :-2, 1:-1])
    total = total + face_z[:, :, 1:] * (field - padded[1:-1, 1:-1, 2:]) + face_z[:, :, :-1] * (field - padded[1:-1, 1:-1, :-2])
    return total


def reference(rhs, mobility, labels, coarse_inverse):
    face_x, face_y, face_z = faces(mobility)
    diag = face_x[1:] + face_x[:-1] + face_y[:, 1:] + face_y[:, :-1] + face_z[:, :, 1:] + face_z[:, :, :-1]
    block_x = (jnp.arange(NX, dtype=jnp.int32) // CX)[:, None, None]
    block_y = (jnp.arange(NY, dtype=jnp.int32) // CY)[None, :, None]
    block_z = (jnp.arange(NZ, dtype=jnp.int32) // CZ)[None, None, :]
    unknown = (labels + DEFL * ((block_x * N_GY + block_z) * N_GZ + block_y)).astype(jnp.int32)
    flat_unknown = unknown.reshape(-1)

    def correct(field):
        sums = jax.ops.segment_sum(field.reshape(-1), flat_unknown, num_segments=COARSE)
        coarse = jnp.dot(coarse_inverse, sums, precision=lax.Precision.HIGHEST)
        return coarse[unknown]

    def operate(field):
        return apply_operator(jnp.pad(field, 1), field, face_x, face_y, face_z)

    solution_field = correct(rhs)
    residual = rhs - operate(solution_field)
    precond = residual / diag
    norm_now = jnp.sum(residual * precond)
    direction = precond - correct(operate(precond))
    for step in range(ITERS):
        image = operate(direction)
        alpha = norm_now / jnp.sum(direction * image)
        solution_field = solution_field + alpha * direction
        residual = residual - alpha * image
        if step + 1 < ITERS:
            precond = residual / diag
            norm_next = jnp.sum(residual * precond)
            direction = (precond + (norm_next / norm_now) * direction) - correct(operate(precond))
            norm_now = norm_next
    return solution_field, residual
```

```python
import functools

import jax
import jax.numpy as jnp
from jax import lax
from jax.experimental import pallas as pl
from jax.experimental.pallas import tpu as pltpu
from jax.sharding import PartitionSpec as P

MESH = pl.DeviceIdType.MESH
F32 = jnp.float32
LOOP = 5
VMEM_BYTES = 64 * 1024 * 1024 - 256 * 1024

Y0, Z0, Z1, MOB, LAB, INV = range(6)


def farthest_first(n):
    return sorted(range(n), key=lambda k: -min(k, n - k))


def kernel(
    nx,
    ny,
    nz,
    rhs_hbm,
    mob_hbm,
    lab_hbm,
    inv_hbm,
    x_hbm,
    p_hbm,
    r_hbm,
    w_hbm,
    step_out,
    mob,
    x0,
    y0,
    z0,
    z1,
    p0,
    p1,
    p2,
    rhs,
    lab,
    inv,
    inv_far,
    fx,
    fy,
    fz,
    dinv,
    rim,
    bits,
    fyb,
    fzp,
    xs,
    rs,
    ws,
    xh,
    ys,
    yh,
    zs,
    zh,
    lxh,
    lys,
    lyh,
    lzs,
    lzh,
    lzf,
    yrim_y,
    yrim_z,
    prim_y,
    prim_z,
    zt,
    lt,
    et,
    ey,
    G1_first,
    G2_first,
    G1,
    G2,
    G1_last,
    G2_last,
    in_sem,
    out_sem,
    hs_sem,
    hr_sem,
    gs_sem,
    gr_sem,
):
    cx = rhs.shape[0]
    gx, gy, gz = lax.axis_index("gx"), lax.axis_index("gy"), lax.axis_index("gz")
    sides = (
        ("gx", gx > 0, gx - 1),
        ("gx", gx < nx - 1, gx + 1),
        ("gz", gz > 0, gz - 1),
        ("gz", gz < nz - 1, gz + 1),
        ("gy", gy > 0, gy - 1),
        ("gy", gy < ny - 1, gy + 1),
    )
    fields = {Y0: y0, Z0: z0, Z1: z1, MOB: mob}

    loads = [
        pltpu.make_async_copy(rhs_hbm, rhs, in_sem.at[0]),
        pltpu.make_async_copy(lab_hbm, lab, in_sem.at[1]),
        pltpu.make_async_copy(mob_hbm, mob.at[pl.ds(1, cx)], in_sem.at[2]),
        pltpu.make_async_copy(inv_hbm, inv, in_sem.at[3]),
    ]
    for load in loads:
        load.start()

    def clear(ref, *index):
        ref[index] = jnp.zeros(ref.shape[len(index) :], ref.dtype)

    for low in range(2):

        @pl.when(gx == (nx - 1 if low else 0))
        def _():
            clear(mob, cx + 1 if low else 0)
            clear(lxh, low)
            for e in (Y0, Z0, Z1):
                clear(xh, e, low)

        @pl.when(gz == (nz - 1 if low else 0))
        def _():
            clear(lyh, low)
            for e in (Y0, Z0, Z1, MOB):
                clear(yh, e, low)

        @pl.when(gy == (ny - 1 if low else 0))
        def _():
            clear(lzh, low)
            for e in (Y0, Z0, Z1, MOB):
                clear(zh, e, low)

    barrier = pltpu.get_barrier_semaphore()
    plane_peers = [
        {"gy": lax.rem(gy + j, ny), "gz": lax.rem(gz + k, nz)}
        for j in farthest_first(ny)
        for k in farthest_first(nz)
        if j or k
    ]
    line_peers = [{"gx": lax.rem(gx + k, nx)} for k in farthest_first(nx) if k]
    phases = ((gy * nz + gz, plane_peers), (gx, line_peers))
    partners = plane_peers + line_peers
    for partner in partners:
        pl.semaphore_signal(barrier, inc=1, device_id=partner, device_id_type=MESH)

    for field in (y0, z0, z1):
        clear(field, 0)
        clear(field, cx + 1)

    lane8 = lax.broadcasted_iota(jnp.int32, (8, 128), 1)
    row8 = lax.broadcasted_iota(jnp.int32, (8, 128), 0)
    lane16 = lax.broadcasted_iota(jnp.int32, (16, 128), 1)
    row16 = lax.broadcasted_iota(jnp.int32, (16, 128), 0)
    pair = ((lane8 + 1) >> 1) & 63
    ends = (lane8 == 0) | (lane8 == 127)
    even = (lane8 & 1) == 0
    zero = jnp.zeros((8, 128), F32)

    def fold(plane):
        tiles = [plane[k : k + 8] for k in range(0, plane.shape[0], 8)]
        while len(tiles) > 1:
            tiles = [a + b for a, b in zip(tiles[::2], tiles[1::2])]
        return tiles[0]

    def halo_copy(e, side):
        axis, _, index = sides[side]
        low, other = side & 1, 1 - (side & 1)
        if e == INV:
            src, dst = inv, inv_far.at[side ^ 1]
        elif e == LAB:
            if axis == "gx":
                src, dst = lab.at[cx - 1 if low else 0], lxh.at[other]
            elif axis == "gz":
                src, dst = lys.at[low], lyh.at[other]
            else:
                src, dst = lzs, lzh.at[other]
        elif axis == "gx":
            src = fields[e].at[cx if low else 1]
            dst = mob.at[0 if low else cx + 1] if e == MOB else xh.at[e, other]
        elif axis == "gz":
            src, dst = ys.at[e, low], yh.at[e, other]
        else:
            src, dst = zs.at[e], zh.at[e, other]
        return pltpu.make_async_remote_copy(
            src_ref=src,
            dst_ref=dst,
            send_sem=hs_sem.at[e, side],
            recv_sem=hr_sem.at[e, side ^ 1],
            device_id={axis: index},
            device_id_type=MESH,
        )

    def halo_landed(e, side):
        low = side & 1
        if e == INV:
            ref = inv_far.at[side]
        elif e == LAB:
            ref = (lxh, lyh, lzh)[side // 2].at[low]
        elif side < 2:
            ref = mob.at[cx + 1 if low else 0] if e == MOB else xh.at[e, low]
        else:
            ref = (yh, zh)[side // 2 - 1].at[e, low]
        return pltpu.make_async_copy(ref, ref, hr_sem.at[e, side])

    def exchange_start(e):
        for side in (0, 1, 4, 5, 2, 3):

            @pl.when(sides[side][1])
            def _():
                halo_copy(e, side).start()

    def exchange_wait(e):
        for side in range(6):

            @pl.when(sides[side][1])
            def _():
                halo_landed(e, side).wait()
                halo_copy(e, side).wait_send()

    def stage_rows(rows, x, plane):
        rows[0, pl.ds(x, 1), :] = plane[0:1]
        rows[1, pl.ds(x, 1), :] = plane[63:64]

    def pack_plane(plane):
        packed = plane[0:8]
        for k in range(1, 8):
            packed = jnp.where(pair == k, pltpu.roll(plane[8 * k : 8 * k + 8], 2 * k, 1), packed)
        return jnp.where(pair < 8, packed, jnp.zeros_like(packed))

    def pack_end(tiles, half):
        total = tiles[8 * half]
        for k in range(1, 8):
            total = total + pltpu.roll(tiles[8 * half + k], 16 * k, 1)
        return total

    def stage_plane(e, x, plane):
        stage_rows(ys.at[e], x, plane)
        zt[x] = pack_plane(plane)

    def stage_end(e):
        for half in range(2):
            zs[e, half] = pack_end(zt, half)

    def far(received, half):
        return jnp.where(
            even, pltpu.roll(received[0, half], 1, 1), pltpu.roll(received[1, half], 127, 1)
        )

    def spread(packed, half):
        et[8 * half] = packed
        for k in range(1, 8):
            et[8 * half + k] = pltpu.roll(packed, 128 - 16 * k, 1)

    def edge_part(x, v):
        return edge_tiles(x)

    def edge_tiles(x):
        tile = et[x]
        tiles = [
            jnp.where(ends, tile if k == 0 else pltpu.roll(tile, 128 - 2 * k, 1), 0.0)
            for k in range(8)
        ]
        first, last = ey[0, pl.ds(x, 1), :], ey[1, pl.ds(x, 1), :]
        tiles[0] = tiles[0] + jnp.where(row8 == 0, first, 0.0)
        tiles[7] = tiles[7] + jnp.where(row8 == 7, last, 0.0)
        return jnp.concatenate(tiles, axis=0)

    def apply_all(field, body, init, outer, make=None):
        def step(x, carry, above_v):
            below, v, rest = carry
            above = fx[x + 1] * (above_v - v)
            flux_y = fy[x] * (pltpu.roll(v, 63, 0) - v)
            flux_z = fz[x] * (pltpu.roll(v, 127, 1) - v)
            out = (
                (below - above)
                + (pltpu.roll(flux_y, 1, 0) - flux_y)
                + (pltpu.roll(flux_z, 1, 1) - flux_z)
                + outer(x, v)
            )
            return above, above_v, body(x, v, out, rest)

        if make is None:

            def make(x):
                return field[x + 1]

        v = make(0)
        carry = (fx[0] * (v - field[0]), v, init)
        carry = lax.fori_loop(
            0, cx - 1, lambda x, c: step(x, c, make(x + 1)), carry, unroll=LOOP
        )
        return step(cx - 1, carry, field[cx + 1])[2]

    def subset_sums(values, bits):
        terms = [values]
        for bit in bits:
            terms = terms + [term * bit for term in terms]
        return [fold(term) for term in terms]

    def label_sums(sums):
        sums = list(sums)
        for i in range(4):
            for value in range(16):
                if not value >> i & 1:
                    sums[value] = sums[value] - sums[value | 1 << i]
        return sums

    def bits_of(labels):
        return [((labels >> i) & 1).astype(F32) for i in range(4)]

    def by_label(labels, values):
        return label_sums(subset_sums(values, bits_of(labels)))

    def restrict_plane(x, plane, sums):
        more = subset_sums(plane, [bits[i, x] for i in range(4)])
        return tuple(total + extra for total, extra in zip(sums, more))

    def restrict_rhs(x, sums):
        planes = bits_of(lab[x])
        for i in range(4):
            bits[i, x] = planes[i]
        return tuple(total + extra for total, extra in zip(sums, subset_sums(rhs[x], planes)))

    no_sums = (zero,) * 16

    def rows_of(tiles):
        for shift in (4, 2, 1):
            low = (row8 & shift) == 0
            half = len(tiles) // 2
            merged = []
            for a, b in zip(tiles[:half], tiles[half:]):
                kept, moved = jnp.where(low, a, b), jnp.where(low, b, a)
                if shift == 4:
                    moved = pltpu.roll(moved, 4, 0)
                else:
                    moved = jnp.where(
                        low, pltpu.roll(moved, 8 - shift, 0), pltpu.roll(moved, shift, 0)
                    )
                merged.append(kept + moved)
            tiles = merged
        return tiles[0]

    def placed(sums, block):
        rows = jnp.concatenate([rows_of(list(sums[:8])), rows_of(list(sums[8:]))], axis=0)
        column = jnp.sum(rows, axis=1, keepdims=True)
        return fold(jnp.where(lane16 == 16 * block + row16, column, 0.0))

    def make_tile(sums, parts, dots):
        tiles = [placed(sums, gz) + placed(parts[2], gz - 1) + placed(parts[3], gz + 1)]
        for side in (4, 5, 0, 1):
            tiles.append(placed(parts[side], gz))
        narrow = []
        for dot in dots:
            dot = dot + pltpu.roll(dot, 64, 1)
            narrow.append(dot + pltpu.roll(dot, 32, 1))
        joined = zero
        for k, dot in enumerate(narrow):
            joined = jnp.where(lane8 >> 5 == k, dot, joined)
        return rows_of(tiles + [joined, zero, zero])[:6]

    def neighbour_parts(e, field):
        parts = [
            by_label(lxh[0], -(fx[0] * field[1])),
            by_label(lxh[1], -(fx[cx] * field[cx])),
        ]
        for low in range(2):
            parts.append(by_label(lyh[low], -(fyb[low] * ys[e, low])))
        for keep in (even, ~even):
            halves = [
                by_label(lzf[half], jnp.where(keep, -(fzp[half] * zs[e, half]), 0.0))
                for half in range(2)
            ]
            parts.append([a + b for a, b in zip(*halves)])
        return parts

    def coarse_right_side(e, field):
        sums = apply_all(
            field, lambda x, v, out, s: restrict_plane(x, out, s), no_sums, lambda x, v: rim[x] * v
        )
        return label_sums(sums), neighbour_parts(e, field)

    def slots_of(g, ph):
        if g == 0:
            return (G1_first, G2_first)[ph]
        if g == 4:
            return (G1_last, G2_last)[ph]
        return (G1, G2)[ph].at[g - 1]

    def phase_start(g, ph):
        me, peers = phases[ph]
        slot = slots_of(g, ph).at[me]
        for peer in peers:
            pltpu.make_async_remote_copy(
                src_ref=slot,
                dst_ref=slot,
                send_sem=gs_sem.at[g, ph],
                recv_sem=gr_sem.at[g, ph],
                device_id=peer,
                device_id_type=MESH,
            ).start()

    def phase_wait(g, ph):
        part = slots_of(g, ph).at[pl.ds(0, len(phases[ph][1]))]
        pltpu.make_async_copy(part, part, gr_sem.at[g, ph]).wait()
        pltpu.make_async_copy(part, part, gs_sem.at[g, ph]).wait()

    def shift_down(rows):
        return jnp.concatenate([jnp.zeros((1, 128), F32), rows[: ny - 1]], axis=0)

    def shift_up(rows):
        return jnp.concatenate([rows[1:], jnp.zeros((1, 128), F32)], axis=0)

    def line_sums(slots):
        return [jnp.sum(slots[j * nz : (j + 1) * nz], axis=0) for j in range(ny)]

    def gather(g, tile):
        G1[g - 1, gy * nz + gz] = tile
        phase_start(g, 0)
        phase_wait(g, 0)
        lines = line_sums(G1[g - 1])

        def pick(row):
            return jnp.concatenate([line[row : row + 1] for line in lines], axis=0)

        G2[g - 1, gx, 0:ny] = pick(0) + shift_down(pick(2)) + shift_up(pick(1))
        G2[g - 1, gx, ny : 2 * ny] = pick(3)
        G2[g - 1, gx, 2 * ny : 3 * ny] = pick(4)
        G2[g - 1, gx, 3 * ny : 3 * ny + 1] = sum(lines[1:], lines[0])[5:6]
        phase_start(g, 1)
        phase_wait(g, 1)

    def dots_of(g):
        row = jnp.sum(G2[g - 1, :, 3 * ny : 3 * ny + 1], axis=0)
        lane = lax.broadcasted_iota(jnp.int32, (1, 128), 1)
        return [
            jnp.broadcast_to(
                jnp.sum(jnp.where(lane >> 5 == k, row, 0.0), axis=1, keepdims=True), (1, 128)
            )
            for k in range(3)
        ]

    def right_side(g):
        if g == 0:
            return [G2_first[i] for i in range(nx)]
        blocks = []
        for i in range(nx):
            rows = G2[g - 1, i, 0:ny]
            if i + 1 < nx:
                rows = rows + G2[g - 1, i + 1, ny : 2 * ny]
            if i > 0:
                rows = rows + G2[g - 1, i - 1, 2 * ny : 3 * ny]
            blocks.append(rows)
        return blocks

    def coarse(g):
        accs = [jnp.zeros((16, 128), F32) for _ in range(7)]
        for i, rows in enumerate(right_side(g)):
            for j in range(ny):
                columns = slice((i * ny + j) * 128, (i * ny + j + 1) * 128)
                row = rows[j : j + 1]
                accs[6] = accs[6] + inv[:, columns] * row
                for side in range(6):
                    accs[side] = accs[side] + inv_far[side, :, columns] * row
        lines = []
        for side in range(7):
            total = jnp.sum(accs[side], axis=1, keepdims=True)
            line = jnp.sum(jnp.where(lane16 == row16, total, 0.0), axis=0, keepdims=True)
            if side < 6:
                index = lax.broadcasted_iota(jnp.int32, (1, 128), 1) * 0 + (gx, gz, gy)[side // 2]
                edge = (0, (nx, nz, ny)[side // 2] - 1)[side & 1]
                line = jnp.where(index == edge, 0.0, line)
            lines.append(line)
        return lines

    def take(line, labels):
        return jnp.take_along_axis(
            jnp.broadcast_to(line, labels.shape), labels, axis=1, mode="promise_in_bounds"
        )

    def rim_of(lines):
        x_far = [take(lines[low], lxh[low]) for low in range(2)]
        y_own = [take(lines[6], lys[low]) for low in range(2)]
        y_far = [take(lines[2 + low], lyh[low]) for low in range(2)]
        z_own = [take(lines[6], lzs[half]) for half in range(2)]
        z_far = [
            jnp.where(even, take(lines[4], lzf[half]), take(lines[5], lzf[half]))
            for half in range(2)
        ]
        return x_far, y_own, y_far, z_own, z_far

    def outer_faces(y_own, y_far, z_own, z_far):
        for low in range(2):
            ey[low] = fyb[low] * (y_own[low] - y_far[low])
        for half in range(2):
            spread(fzp[half] * (z_own[half] - z_far[half]), half)

    loads[0].wait()
    loads[1].wait()
    sums = lax.fori_loop(0, cx, restrict_rhs, no_sums, unroll=4)
    line = jnp.sum(placed(label_sums(sums), gz), axis=0, keepdims=True)
    pl.semaphore_wait(barrier, len(partners))
    G1_first[gy * nz + gz] = line
    phase_start(0, 0)
    loads[2].wait()

    def stage_static(x, carry):
        stage_plane(MOB, x, mob[x + 1])
        labels = lab[x]
        stage_rows(lys, x, labels)
        lt[x] = pack_plane(labels)
        return carry

    lax.fori_loop(0, cx, stage_static, 0, unroll=4)
    stage_end(MOB)
    for half in range(2):
        lzs[half] = pack_end(lt, half)
    exchange_start(MOB)
    exchange_start(LAB)
    loads[3].wait()
    exchange_start(INV)

    def faces():
        exchange_wait(MOB)
        exchange_wait(LAB)
        for half in range(2):
            lzf[half] = far(lzh, half)
            fzp[half] = 0.5 * (zs[MOB, half] + far(zh.at[MOB], half))
            spread(fzp[half], half)
        for low in range(2):
            fyb[low] = 0.5 * (ys[MOB, low] + yh[MOB, low])
            ey[low] = fyb[low]
        fx[0] = 0.5 * (mob[1] + mob[0])
        row = lax.broadcasted_iota(jnp.int32, (64, 128), 0)
        lane = lax.broadcasted_iota(jnp.int32, (64, 128), 1)

        def step(x, below):
            m = mob[x + 1]
            above = 0.5 * (mob[x + 2] + m)
            face_y = jnp.where(row == 63, 0.0, 0.5 * (pltpu.roll(m, 63, 0) + m))
            face_z = jnp.where(lane == 127, 0.0, 0.5 * (pltpu.roll(m, 127, 1) + m))
            edges = edge_tiles(x)
            diag = (
                (below + above)
                + (pltpu.roll(face_y, 1, 0) + face_y)
                + (pltpu.roll(face_z, 1, 1) + face_z)
                + edges
            )
            rim[x] = edges
            fx[x + 1] = above
            fy[x] = face_y
            fz[x] = face_z
            dinv[x] = 1.0 / diag
            return above

        lax.fori_loop(0, cx, step, fx[0], unroll=4)

    phase_wait(0, 0)
    for j, row in enumerate(line_sums(G1_first)):
        G2_first[gx, j : j + 1] = row
    phase_start(0, 1)
    faces()
    phase_wait(0, 1)

    exchange_wait(INV)
    lines = coarse(0)

    def first_iterate(x):
        plane = take(lines[6], lab[x])
        x0[x + 1] = plane
        return plane

    x_far, *rest = rim_of(lines)
    x0[0] = x_far[0]
    x0[cx + 1] = x_far[1]
    outer_faces(*rest)

    def first_residual(x, v, out, dot):
        residual = rhs[x] - out
        precond = residual * dinv[x]
        rs[x] = residual
        y0[x + 1] = precond
        stage_plane(Y0, x, precond)
        return dot + fold(residual * precond)

    ry_part = apply_all(x0, first_residual, zero, edge_part, first_iterate)
    stage_end(Y0)
    exchange_start(Y0)
    sums, parts = coarse_right_side(Y0, y0)
    gather(1, make_tile(sums, parts, (ry_part,)))
    lines = coarse(1)
    ry = dots_of(1)[0]

    def first_direction(x):
        plane = y0[x + 1] - take(line_here, lab[x])
        p0[x + 1] = plane
        return plane

    line_here = lines[6]
    direction = first_direction
    exchange_wait(Y0)
    x_far, y_own, y_far, z_own, z_far = rim_of(lines)
    for low in range(2):
        p0[cx + 1 if low else 0] = xh[Y0, low] - x_far[low]
        yrim_y[low] = ys[Y0, low]
        yrim_y[2 + low] = yh[Y0, low]
        yrim_z[low] = zs[Y0, low]
        yrim_z[2 + low] = far(zh.at[Y0], low)
    for k, (y_part, z_part) in enumerate(zip(y_own + y_far, z_own + z_far)):
        prim_y[k] = yrim_y[k] - y_part
        prim_z[k] = yrim_z[k] - z_part

    def prim_faces():
        outer_faces(
            [prim_y[0], prim_y[1]],
            [prim_y[2], prim_y[3]],
            [prim_z[0], prim_z[1]],
            [prim_z[2], prim_z[3]],
        )

    prim_faces()

    alphas = []
    for g, here, scaled, e, after in ((2, p0, z0, Z0, p1), (3, p1, z1, Z1, p2)):

        def image(x, v, out, dots):
            z = out * dinv[x]
            ws[x] = out
            scaled[x + 1] = z
            stage_plane(e, x, z)
            return (
                dots[0] + fold(v * out),
                dots[1] + fold(rs[x] * z),
                dots[2] + fold(out * z),
            )

        dots = apply_all(here, image, (zero, zero, zero), edge_part, direction)
        stage_end(e)
        exchange_start(e)
        sums, parts = coarse_right_side(e, scaled)
        gather(g, make_tile(sums, parts, dots))
        more = coarse(g)
        pw, rz, wz = dots_of(g)
        alpha = ry / pw
        alphas.append(alpha)
        ry_next = ry + alpha * (alpha * wz - 2.0 * rz)
        beta = ry_next / ry
        ry = ry_next
        lines = [line - alpha * extra for line, extra in zip(lines, more)]

        def next_direction(x, here=here, after=after, alpha=alpha, beta=beta, line=lines[6]):
            p = here[x + 1]
            residual = rs[x] - alpha * ws[x]
            rs[x] = residual
            plane = (residual * dinv[x] + beta * p) - take(line, lab[x])
            after[x + 1] = plane
            return plane

        direction = next_direction
        exchange_wait(e)
        x_far, y_own, y_far, z_own, z_far = rim_of(lines)
        for low in range(2):
            outer = cx + 1 if low else 0
            layer = xh[Y0, low] - alpha * xh[e, low]
            xh[Y0, low] = layer
            after[outer] = (layer + beta * here[outer]) - x_far[low]
        z_rows = [ys[e, 0], ys[e, 1], yh[e, 0], yh[e, 1]]
        z_packs = [zs[e, 0], zs[e, 1], far(zh.at[e], 0), far(zh.at[e], 1)]
        for k, (y_part, z_part) in enumerate(zip(y_own + y_far, z_own + z_far)):
            rows = yrim_y[k] - alpha * z_rows[k]
            packs = yrim_z[k] - alpha * z_packs[k]
            yrim_y[k] = rows
            yrim_z[k] = packs
            prim_y[k] = (rows + beta * prim_y[k]) - y_part
            prim_z[k] = (packs + beta * prim_z[k]) - z_part
        prim_faces()

    stores = [
        pltpu.make_async_copy(xs, x_hbm, out_sem.at[0]),
        pltpu.make_async_copy(p2.at[pl.ds(1, cx)], p_hbm, out_sem.at[1]),
        pltpu.make_async_copy(rs, r_hbm, out_sem.at[2]),
        pltpu.make_async_copy(ws, w_hbm, out_sem.at[3]),
    ]

    def last_image(x, v, out, dot):
        ws[x] = out
        return dot + fold(v * out)

    part = apply_all(p2, last_image, zero, edge_part, direction)
    last_tile = jnp.sum(part, axis=0, keepdims=True)
    G1_last[gy * nz + gz] = last_tile
    phase_start(4, 0)
    for store in stores[1:]:
        store.start()

    def join_iterate(x, carry):
        xs[x] = (x0[x + 1] + alphas[0] * p0[x + 1]) + alphas[1] * p1[x + 1]
        return carry

    lax.fori_loop(0, cx, join_iterate, 0, unroll=4)
    stores[0].start()
    phase_wait(4, 0)
    G2_last[gx] = jnp.sum(G1_last[...], axis=0)
    phase_start(4, 1)
    phase_wait(4, 1)
    total = jnp.sum(jnp.sum(G2_last[...], axis=0), axis=1, keepdims=True)
    step_out[...] = jnp.broadcast_to(ry / total, step_out.shape)
    for store in stores:
        store.wait()


def solution(mesh):
    nx, ny, nz = mesh.shape["gx"], mesh.shape["gy"], mesh.shape["gz"]

    def per_device(rhs, mobility, labels, coarse_inverse):
        cx, cy, cz = rhs.shape
        hbm = pl.BlockSpec(memory_space=pl.ANY)

        def vmem(*shape, dtype=F32):
            return pltpu.VMEM(shape, dtype)

        i32 = jnp.int32
        xs, p, rs, w, alpha = pl.pallas_call(
            functools.partial(kernel, nx, ny, nz),
            out_shape=[jax.ShapeDtypeStruct(rhs.shape, F32)] * 4
            + [jax.ShapeDtypeStruct((cy, cz), F32)],
            in_specs=[hbm] * 4,
            out_specs=[hbm] * 4 + [pl.BlockSpec(memory_space=pltpu.VMEM)],
            scratch_shapes=[
                *[vmem(cx + 2, cy, cz) for _ in range(8)],
                vmem(cx, cy, cz),
                vmem(cx, cy, cz, dtype=i32),
                vmem(*coarse_inverse.shape),
                vmem(6, *coarse_inverse.shape),
                vmem(cx + 1, cy, cz),
                *[vmem(cx, cy, cz) for _ in range(4)],
                vmem(4, cx, cy, cz),
                vmem(2, cx, cz),
                vmem(2, 8, 128),
                *[vmem(cx, cy, cz) for _ in range(3)],
                vmem(3, 2, cy, cz),
                vmem(4, 2, cx, cz),
                vmem(4, 2, cx, cz),
                vmem(4, 2, 8, 128),
                vmem(4, 2, 2, 8, 128),
                vmem(2, cy, cz, dtype=i32),
                vmem(2, cx, cz, dtype=i32),
                vmem(2, cx, cz, dtype=i32),
                vmem(2, 8, 128, dtype=i32),
                vmem(2, 2, 8, 128, dtype=i32),
                vmem(2, 8, 128, dtype=i32),
                vmem(4, cx, cz),
                vmem(4, 8, 128),
                vmem(4, cx, cz),
                vmem(4, 8, 128),
                vmem(cx, 8, 128),
                vmem(cx, 8, 128, dtype=i32),
                vmem(cx, 8, 128),
                vmem(2, cx, cz),
                vmem(ny * nz, 1, 128),
                vmem(nx, ny, 128),
                vmem(3, ny * nz, 6, 128),
                vmem(3, nx, 3 * ny + 1, 128),
                vmem(ny * nz, 1, 128),
                vmem(nx, 1, 128),
                pltpu.SemaphoreType.DMA((4,)),
                pltpu.SemaphoreType.DMA((4,)),
                pltpu.SemaphoreType.DMA((6, 6)),
                pltpu.SemaphoreType.DMA((6, 6)),
                pltpu.SemaphoreType.DMA((5, 2)),
                pltpu.SemaphoreType.DMA((5, 2)),
            ],
            compiler_params=pltpu.CompilerParams(
                collective_id=0, has_side_effects=True, vmem_limit_bytes=VMEM_BYTES
            ),
            name="deflated_cg",
        )(rhs, mobility, labels, coarse_inverse)
        return xs + alpha * p, rs - alpha * w

    spec = P("gx", "gz", "gy")
    return jax.shard_map(
        per_device,
        mesh=mesh,
        in_specs=(spec, spec, spec, P(("gx", "gy", "gz"), None)),
        out_specs=(spec, spec),
        check_vma=False,
    )
```

```python
import functools

import jax
import jax.numpy as jnp
from jax import lax
from jax.experimental import pallas as pl
from jax.experimental.pallas import tpu as pltpu
from jax.sharding import PartitionSpec as P

MESH = pl.DeviceIdType.MESH
F32 = jnp.float32
LOOP = 5
VMEM_BYTES = 64 * 1024 * 1024 - 256 * 1024

STEPS = 3
MOB, LAB, INV = range(STEPS, STEPS + 3)


def farthest_first(n):
    return sorted(range(n), key=lambda k: -min(k, n - k))


def kernel(
    nx,
    ny,
    nz,
    rhs_hbm,
    mob_hbm,
    lab_hbm,
    inv_hbm,
    x_hbm,
    p_hbm,
    r_hbm,
    w_hbm,
    step_out,
    mob,
    x0,
    field,
    direction,
    history,
    rhs,
    lab,
    inv_in,
    inv,
    inv_far,
    fx,
    fy,
    fz,
    dinv,
    rim,
    bits,
    fyb,
    fzp,
    xs,
    rs,
    ws,
    xh,
    ys,
    yh,
    zs,
    zh,
    lxh,
    lys,
    lyh,
    lzs,
    lzh,
    lzf,
    yrim_x,
    yrim_y,
    yrim_z,
    prim_y,
    prim_z,
    zt,
    lt,
    et,
    ey,
    G1_first,
    G2_first,
    G1,
    G2,
    G1_last,
    G2_last,
    in_sem,
    out_sem,
    hs_sem,
    hr_sem,
    gs_sem,
    gr_sem,
):
    cx = rhs.shape[0]
    gx, gy, gz = lax.axis_index("gx"), lax.axis_index("gy"), lax.axis_index("gz")
    sides = (
        ("gx", gx > 0, gx - 1),
        ("gx", gx < nx - 1, gx + 1),
        ("gz", gz > 0, gz - 1),
        ("gz", gz < nz - 1, gz + 1),
        ("gy", gy > 0, gy - 1),
        ("gy", gy < ny - 1, gy + 1),
    )

    loads = [
        pltpu.make_async_copy(rhs_hbm, rhs, in_sem.at[0]),
        pltpu.make_async_copy(lab_hbm, lab, in_sem.at[1]),
        pltpu.make_async_copy(mob_hbm, mob.at[pl.ds(1, cx)], in_sem.at[2]),
        pltpu.make_async_copy(inv_hbm, inv_in, in_sem.at[3]),
    ]
    for load in loads:
        load.start()

    def clear(ref, *index):
        ref[index or Ellipsis] = jnp.zeros(ref.shape[len(index) :], ref.dtype)

    for low in range(2):

        @pl.when(gx == (nx - 1 if low else 0))
        def _():
            clear(mob, cx + 1 if low else 0)
            clear(lxh, low)
            for e in range(STEPS):
                clear(xh, e, low)

        @pl.when(gz == (nz - 1 if low else 0))
        def _():
            clear(lyh, low)
            for e in range(STEPS + 1):
                clear(yh, e, low)

        @pl.when(gy == (ny - 1 if low else 0))
        def _():
            clear(lzh, low)
            for e in range(STEPS + 1):
                clear(zh, e, low)

    barrier = pltpu.get_barrier_semaphore()
    plane_peers = [
        {"gx": lax.rem(gx + k, nx), "gy": lax.rem(gy + j, ny)}
        for k in farthest_first(nx)
        for j in farthest_first(ny)
        if j or k
    ]
    line_peers = [{"gz": lax.rem(gz + k, nz)} for k in farthest_first(nz) if k]
    phases = ((gy * nx + gx, plane_peers), (gz, line_peers))
    partners = plane_peers + line_peers
    for partner in partners:
        pl.semaphore_signal(barrier, inc=1, device_id=partner, device_id_type=MESH)

    clear(field, 0)
    clear(field, cx + 1)

    lane8 = lax.broadcasted_iota(jnp.int32, (8, 128), 1)
    row8 = lax.broadcasted_iota(jnp.int32, (8, 128), 0)
    lane16 = lax.broadcasted_iota(jnp.int32, (16, 128), 1)
    row16 = lax.broadcasted_iota(jnp.int32, (16, 128), 0)
    pair = ((lane8 + 1) >> 1) & 63
    ends = (lane8 == 0) | (lane8 == 127)
    even = (lane8 & 1) == 0
    zero = jnp.zeros((8, 128), F32)

    def fold(plane):
        tiles = [plane[k : k + 8] for k in range(0, plane.shape[0], 8)]
        while len(tiles) > 1:
            tiles = [a + b for a, b in zip(tiles[::2], tiles[1::2])]
        return tiles[0]

    def halo_copy(e, side):
        axis, _, index = sides[side]
        low, other = side & 1, 1 - (side & 1)
        kind = e if isinstance(e, int) else 0
        if kind == INV:
            src, dst = inv, inv_far.at[side ^ 1]
        elif kind == LAB:
            if axis == "gx":
                src, dst = lab.at[cx - 1 if low else 0], lxh.at[other]
            elif axis == "gz":
                src, dst = lys.at[low], lyh.at[other]
            else:
                src, dst = lzs, lzh.at[other]
        elif axis == "gx":
            src = (mob if kind == MOB else field).at[cx if low else 1]
            dst = mob.at[0 if low else cx + 1] if kind == MOB else xh.at[e, other]
        elif axis == "gz":
            src, dst = ys.at[e, low], yh.at[e, other]
        else:
            src, dst = zs.at[e], zh.at[e, other]
        return pltpu.make_async_remote_copy(
            src_ref=src,
            dst_ref=dst,
            send_sem=hs_sem.at[e, side],
            recv_sem=hr_sem.at[e, side ^ 1],
            device_id={axis: index},
            device_id_type=MESH,
        )

    def halo_landed(e, side):
        low = side & 1
        kind = e if isinstance(e, int) else 0
        if kind == INV:
            ref = inv_far.at[side]
        elif kind == LAB:
            ref = (lxh, lyh, lzh)[side // 2].at[low]
        elif side < 2:
            ref = mob.at[cx + 1 if low else 0] if kind == MOB else xh.at[e, low]
        else:
            ref = (yh, zh)[side // 2 - 1].at[e, low]
        return pltpu.make_async_copy(ref, ref, hr_sem.at[e, side])

    def exchange_start(e):
        for side in (0, 1, 4, 5, 2, 3):

            @pl.when(sides[side][1])
            def _():
                halo_copy(e, side).start()

    def exchange_wait(e):
        for side in range(6):

            @pl.when(sides[side][1])
            def _():
                halo_landed(e, side).wait()
                halo_copy(e, side).wait_send()

    def stage_rows(rows, x, plane):
        rows[0, pl.ds(x, 1), :] = plane[0:1]
        rows[1, pl.ds(x, 1), :] = plane[63:64]

    def pack_plane(plane):
        packed = plane[0:8]
        for k in range(1, 8):
            packed = jnp.where(pair == k, pltpu.roll(plane[8 * k : 8 * k + 8], 2 * k, 1), packed)
        return jnp.where(pair < 8, packed, jnp.zeros_like(packed))

    def pack_end(tiles, half):
        total = tiles[8 * half]
        for k in range(1, 8):
            total = total + pltpu.roll(tiles[8 * half + k], 16 * k, 1)
        return total

    def stage_plane(e, x, plane):
        stage_rows(ys.at[e], x, plane)
        zt[x] = pack_plane(plane)

    def stage_end(e):
        for half in range(2):
            zs[e, half] = pack_end(zt, half)

    def far(received, half):
        return jnp.where(
            even, pltpu.roll(received[0, half], 1, 1), pltpu.roll(received[1, half], 127, 1)
        )

    def spread(packed, half):
        et[8 * half] = packed
        for k in range(1, 8):
            et[8 * half + k] = pltpu.roll(packed, 128 - 16 * k, 1)

    def edge_part(x, v):
        return edge_tiles(x)

    def edge_tiles(x):
        tile = et[x]
        tiles = [
            jnp.where(ends, tile if k == 0 else pltpu.roll(tile, 128 - 2 * k, 1), 0.0)
            for k in range(8)
        ]
        first, last = ey[0, pl.ds(x, 1), :], ey[1, pl.ds(x, 1), :]
        tiles[0] = tiles[0] + jnp.where(row8 == 0, first, 0.0)
        tiles[7] = tiles[7] + jnp.where(row8 == 7, last, 0.0)
        return jnp.concatenate(tiles, axis=0)

    def apply_all(values, body, init, outer, make=None):
        def step(x, carry, above_v):
            below, v, rest = carry
            above = fx[x + 1] * (above_v - v)
            flux_y = fy[x] * (pltpu.roll(v, 63, 0) - v)
            flux_z = fz[x] * (pltpu.roll(v, 127, 1) - v)
            out = (
                (below - above)
                + (pltpu.roll(flux_y, 1, 0) - flux_y)
                + (pltpu.roll(flux_z, 1, 1) - flux_z)
                + outer(x, v)
            )
            return above, above_v, body(x, v, out, rest)

        if make is None:

            def make(x):
                return values[x + 1]

        v = make(0)
        carry = (fx[0] * (v - values[0]), v, init)
        carry = lax.fori_loop(
            0, cx - 1, lambda x, c: step(x, c, make(x + 1)), carry, unroll=LOOP
        )
        return step(cx - 1, carry, values[cx + 1])[2]

    def subset_sums(values, bits):
        terms = [values]
        for bit in bits:
            terms = terms + [term * bit for term in terms]
        return [fold(term) for term in terms]

    def label_sums(sums):
        sums = list(sums)
        for i in range(4):
            for value in range(16):
                if not value >> i & 1:
                    sums[value] = sums[value] - sums[value | 1 << i]
        return sums

    def bits_of(labels):
        return [((labels >> i) & 1).astype(F32) for i in range(4)]

    def by_label(labels, values):
        return label_sums(subset_sums(values, bits_of(labels)))

    def restrict_plane(x, plane, sums):
        more = subset_sums(plane, [bits[i, x] for i in range(4)])
        return tuple(total + extra for total, extra in zip(sums, more))

    def restrict_rhs(x, sums):
        planes = bits_of(lab[x])
        for i in range(4):
            bits[i, x] = planes[i]
        return tuple(total + extra for total, extra in zip(sums, subset_sums(rhs[x], planes)))

    no_sums = (zero,) * 16

    def rows_of(tiles):
        for shift in (4, 2, 1):
            low = (row8 & shift) == 0
            half = len(tiles) // 2
            merged = []
            for a, b in zip(tiles[:half], tiles[half:]):
                kept, moved = jnp.where(low, a, b), jnp.where(low, b, a)
                if shift == 4:
                    moved = pltpu.roll(moved, 4, 0)
                else:
                    moved = jnp.where(
                        low, pltpu.roll(moved, 8 - shift, 0), pltpu.roll(moved, shift, 0)
                    )
                merged.append(kept + moved)
            tiles = merged
        return tiles[0]

    def message(groups, dots):
        tiles = []
        for sums in groups:
            tiles += [rows_of(list(sums[:8])), rows_of(list(sums[8:]))]
        if dots:
            tiles.append(rows_of(list(dots) + [zero] * (8 - len(dots))))
        line = zero
        for k, tile in enumerate(tiles):
            column = jnp.sum(tile, axis=1, keepdims=True)
            line = line + jnp.where(lane8 == 8 * k + row8, column, 0.0)
        return jnp.sum(line, axis=0, keepdims=True)

    def transpose_groups(tile):
        for s in (4, 2, 1):
            group = (lane8 >> 4) & s
            up = pltpu.roll(pltpu.roll(tile, 8 - s, 0), 16 * s, 1)
            down = pltpu.roll(pltpu.roll(tile, s, 0), 128 - 16 * s, 1)
            tile = jnp.where((row8 & s) == group, tile, jnp.where(group != 0, up, down))
        return tile

    def neighbour_parts(e):
        parts = [
            by_label(lxh[0], -(fx[0] * field[1])),
            by_label(lxh[1], -(fx[cx] * field[cx])),
        ]
        for low in range(2):
            parts.append(by_label(lyh[low], -(fyb[low] * ys[e, low])))
        for keep in (even, ~even):
            halves = [
                by_label(lzf[half], jnp.where(keep, -(fzp[half] * zs[e, half]), 0.0))
                for half in range(2)
            ]
            parts.append([a + b for a, b in zip(*halves)])
        return parts

    def coarse_right_side(e):
        sums = apply_all(
            field, lambda x, v, out, s: restrict_plane(x, out, s), no_sums, lambda x, v: rim[x] * v
        )
        return label_sums(sums), neighbour_parts(e)

    def slots_of(g, ph):
        if isinstance(g, int):
            return ((G1_first, G2_first), (G1_last, G2_last))[g != 0][ph]
        return (G1, G2)[ph].at[g - 1]

    def phase_slots(g, ph, first, count):
        slots = slots_of(g, ph)
        return slots.at[pl.ds(first, count)]

    def phase_start(g, ph):
        me, peers = phases[ph]
        slot = phase_slots(g, ph, me, 1)
        for peer in peers:
            pltpu.make_async_remote_copy(
                src_ref=slot,
                dst_ref=slot,
                send_sem=gs_sem.at[g, ph],
                recv_sem=gr_sem.at[g, ph],
                device_id=peer,
                device_id_type=MESH,
            ).start()

    def phase_wait(g, ph):
        part = phase_slots(g, ph, 0, len(phases[ph][1]))
        pltpu.make_async_copy(part, part, gr_sem.at[g, ph]).wait()
        pltpu.make_async_copy(part, part, gs_sem.at[g, ph]).wait()

    def shift_down(rows):
        return jnp.concatenate([jnp.zeros((1, 128), F32), rows[: ny - 1]], axis=0)

    def shift_up(rows):
        return jnp.concatenate([rows[1:], jnp.zeros((1, 128), F32)], axis=0)

    def group_lines(slots):
        tiles = [transpose_groups(slots[nx * j : nx * (j + 1)]) for j in range(ny)]

        def pick(group):
            return jnp.concatenate([tile[group : group + 1] for tile in tiles], axis=0)

        return pick

    lane4 = lax.broadcasted_iota(jnp.int32, (ny, 128), 1)

    def gather(g, line, started, between):
        G1[g - 1, pl.ds(gy * nx + gx, 1), :] = line
        phase_start(g, 0)
        started()
        phase_wait(g, 0)
        pick = group_lines(G1.at[g - 1])
        own = pick(0)
        own = own + jnp.where(lane4 < 112, pltpu.roll(pick(1), 112, 1), 0.0)
        own = own + jnp.where(lane4 >= 16, pltpu.roll(pick(2), 16, 1), 0.0)
        own = own + shift_up(pick(3)) + shift_down(pick(4))
        G2[g - 1, gz, 0:ny] = own
        G2[g - 1, gz, ny : 2 * ny] = pick(5)
        G2[g - 1, gz, 2 * ny : 3 * ny] = pick(6)
        G2[g - 1, gz, 3 * ny : 3 * ny + 1] = jnp.sum(pick(7), axis=0, keepdims=True)
        phase_start(g, 1)
        between()
        phase_wait(g, 1)

    def dots_of(g):
        row = jnp.sum(G2[g - 1, :, 3 * ny : 3 * ny + 1], axis=0)
        lane = lax.broadcasted_iota(jnp.int32, (1, 128), 1)
        return [
            jnp.broadcast_to(
                jnp.sum(jnp.where(lane & 15 == k, row, 0.0), axis=1, keepdims=True), (1, 128)
            )
            for k in range(3)
        ]

    def right_side(g):
        if isinstance(g, int):
            return [G2_first[i] for i in range(nz)]
        blocks = []
        for i in range(nz):
            rows = G2[g - 1, i, 0:ny]
            if i + 1 < nz:
                rows = rows + G2[g - 1, i + 1, ny : 2 * ny]
            if i > 0:
                rows = rows + G2[g - 1, i - 1, 2 * ny : 3 * ny]
            blocks.append(rows)
        return blocks

    def coarse(g):
        accs = [jnp.zeros((16, 128), F32) for _ in range(7)]
        for i, rows in enumerate(right_side(g)):
            for j in range(ny):
                columns = slice((i * ny + j) * 128, (i * ny + j + 1) * 128)
                row = rows[j : j + 1]
                accs[6] = accs[6] + inv[:, columns] * row
                for side in range(6):
                    accs[side] = accs[side] + inv_far[side, :, columns] * row
        lines = []
        for side in range(7):
            total = jnp.sum(accs[side], axis=1, keepdims=True)
            line = jnp.sum(jnp.where(lane16 == row16, total, 0.0), axis=0, keepdims=True)
            if side < 6:
                index = lax.broadcasted_iota(jnp.int32, (1, 128), 1) * 0 + (gx, gz, gy)[side // 2]
                edge = (0, (nx, nz, ny)[side // 2] - 1)[side & 1]
                line = jnp.where(index == edge, 0.0, line)
            lines.append(line)
        return lines

    def take(line, labels):
        return jnp.take_along_axis(
            jnp.broadcast_to(line, labels.shape), labels, axis=1, mode="promise_in_bounds"
        )

    def rim_of(lines):
        x_far = [take(lines[low], lxh[low]) for low in range(2)]
        y_own = [take(lines[6], lys[low]) for low in range(2)]
        y_far = [take(lines[2 + low], lyh[low]) for low in range(2)]
        z_own = [take(lines[6], lzs[half]) for half in range(2)]
        z_far = [
            jnp.where(even, take(lines[4], lzf[half]), take(lines[5], lzf[half]))
            for half in range(2)
        ]
        return x_far, y_own, y_far, z_own, z_far

    def outer_faces(y_own, y_far, z_own, z_far):
        for low in range(2):
            ey[low] = fyb[low] * (y_own[low] - y_far[low])
        for half in range(2):
            spread(fzp[half] * (z_own[half] - z_far[half]), half)

    loads[0].wait()
    loads[1].wait()
    sums = lax.fori_loop(0, cx, restrict_rhs, no_sums, unroll=4)
    line = message([label_sums(sums)], ())
    pl.semaphore_wait(barrier, len(partners))
    G1_first[pl.ds(gy * nx + gx, 1), :] = line
    phase_start(0, 0)
    loads[2].wait()

    def order_columns():
        for top in (0, 8):
            for j in range(ny):
                tiles = [inv_in[top : top + 8, pl.ds((i * ny + j) * 128, 128)] for i in range(nx)]
                for s in (4, 2, 1):
                    clear_bit = (lane8 >> 4) & s == 0
                    for i in range(nx):
                        if not i & s:
                            a, b = tiles[i], tiles[i | s]
                            tiles[i] = jnp.where(clear_bit, a, pltpu.roll(b, 16 * s, 1))
                            tiles[i | s] = jnp.where(clear_bit, pltpu.roll(a, 128 - 16 * s, 1), b)
                for i in range(nz):
                    inv[top : top + 8, pl.ds((i * ny + j) * 128, 128)] = tiles[i]

    def stage_static(x, carry):
        stage_plane(MOB, x, mob[x + 1])
        labels = lab[x]
        stage_rows(lys, x, labels)
        lt[x] = pack_plane(labels)
        return carry

    lax.fori_loop(0, cx, stage_static, 0, unroll=4)
    stage_end(MOB)
    for half in range(2):
        lzs[half] = pack_end(lt, half)
    exchange_start(MOB)
    exchange_start(LAB)
    loads[3].wait()
    order_columns()
    exchange_start(INV)

    def faces():
        for ref in (direction, ws, yrim_x, yrim_y, yrim_z, prim_y, prim_z):
            clear(ref)
        exchange_wait(MOB)
        exchange_wait(LAB)
        for half in range(2):
            lzf[half] = far(lzh, half)
            fzp[half] = 0.5 * (zs[MOB, half] + far(zh.at[MOB], half))
            spread(fzp[half], half)
        for low in range(2):
            fyb[low] = 0.5 * (ys[MOB, low] + yh[MOB, low])
            ey[low] = fyb[low]
        fx[0] = 0.5 * (mob[1] + mob[0])
        row = lax.broadcasted_iota(jnp.int32, (64, 128), 0)
        lane = lax.broadcasted_iota(jnp.int32, (64, 128), 1)

        def step(x, below):
            m = mob[x + 1]
            above = 0.5 * (mob[x + 2] + m)
            face_y = jnp.where(row == 63, 0.0, 0.5 * (pltpu.roll(m, 63, 0) + m))
            face_z = jnp.where(lane == 127, 0.0, 0.5 * (pltpu.roll(m, 127, 1) + m))
            edges = edge_tiles(x)
            diag = (
                (below + above)
                + (pltpu.roll(face_y, 1, 0) + face_y)
                + (pltpu.roll(face_z, 1, 1) + face_z)
                + edges
            )
            rim[x] = edges
            fx[x + 1] = above
            fy[x] = face_y
            fz[x] = face_z
            dinv[x] = 1.0 / diag
            return above

        lax.fori_loop(0, cx, step, fx[0], unroll=4)

    phase_wait(0, 0)
    G2_first[gz] = group_lines(G1_first)(0)
    phase_start(0, 1)
    faces()
    phase_wait(0, 1)

    exchange_wait(INV)
    lines = coarse(0)

    def first_iterate(x):
        plane = take(lines[6], lab[x])
        x0[x + 1] = plane
        return plane

    x_far, *rest = rim_of(lines)
    x0[0] = x_far[0]
    x0[cx + 1] = x_far[1]
    outer_faces(*rest)

    def first_residual(x, v, out, dot):
        residual = rhs[x] - out
        precond = residual * dinv[x]
        rs[x] = residual
        field[x + 1] = precond
        stage_plane(0, x, precond)
        return dot + fold(residual * precond)

    ry_part = apply_all(x0, first_residual, zero, edge_part, first_iterate)
    stage_end(0)

    def tall(row):
        return jnp.broadcast_to(row, (8, 128))

    def one_step(k, carry):
        ry, lines, dots, _, last_alpha = carry
        ry, lines = ry[0:1], [line[0:1] for line in lines]
        sums, parts = coarse_right_side(k)
        gather(
            k + 1,
            message([sums] + [parts[side] for side in (0, 1, 4, 5, 2, 3)], dots),
            lambda: exchange_start(k),
            lambda: exchange_wait(k),
        )
        more = coarse(k + 1)
        d0, d1, d2 = dots_of(k + 1)
        first = lax.broadcasted_iota(jnp.int32, (1, 128), 0) + k == 0
        alpha = jnp.where(first, 0.0, ry / d0)
        ry_next = jnp.where(first, d0, ry + alpha * (alpha * d2 - 2.0 * d1))
        beta = jnp.where(first, 0.0, ry_next / ry)
        gain = jnp.where(first, 1.0, -alpha)
        lines = [line + gain * extra for line, extra in zip(lines, more)]

        x_far, y_own, y_far, z_own, z_far = rim_of(lines)
        for low in range(2):
            outer = cx + 1 if low else 0
            layer = yrim_x[low] + gain * xh[k, low]
            yrim_x[low] = layer
            direction[outer] = (layer + beta * direction[outer]) - x_far[low]
        rows = [ys[k, 0], ys[k, 1], yh[k, 0], yh[k, 1]]
        packs = [zs[k, 0], zs[k, 1], far(zh.at[k], 0), far(zh.at[k], 1)]
        for i, (y_part, z_part) in enumerate(zip(y_own + y_far, z_own + z_far)):
            row = yrim_y[i] + gain * rows[i]
            pack = yrim_z[i] + gain * packs[i]
            yrim_y[i] = row
            yrim_z[i] = pack
            prim_y[i] = (row + beta * prim_y[i]) - y_part
            prim_z[i] = (pack + beta * prim_z[i]) - z_part
        outer_faces(
            [prim_y[0], prim_y[1]],
            [prim_y[2], prim_y[3]],
            [prim_z[0], prim_z[1]],
            [prim_z[2], prim_z[3]],
        )

        def next_direction(x):
            residual = rs[x] - alpha * ws[x]
            rs[x] = residual
            plane = (residual * dinv[x] + beta * direction[x + 1]) - take(lines[6], lab[x])
            direction[x + 1] = plane
            history[k, x] = plane
            return plane

        def image(x, v, out, dots):
            z = out * dinv[x]
            ws[x] = out
            field[x + 1] = z
            stage_plane(k + 1, x, z)
            return (
                dots[0] + fold(v * out),
                dots[1] + fold(rs[x] * z),
                dots[2] + fold(out * z),
            )

        dots = apply_all(direction, image, (zero, zero, zero), edge_part, next_direction)
        stage_end(k + 1)
        return tall(ry_next), [tall(line) for line in lines], dots, last_alpha, tall(alpha)

    ry, _, dots, *alphas = lax.fori_loop(
        0, STEPS, one_step, (zero + 1.0, [zero] * 7, (ry_part, zero, zero), zero, zero)
    )
    ry, alphas = ry[0:1], [alpha[0:1] for alpha in alphas]

    stores = [
        pltpu.make_async_copy(xs, x_hbm, out_sem.at[0]),
        pltpu.make_async_copy(history.at[STEPS - 1], p_hbm, out_sem.at[1]),
        pltpu.make_async_copy(rs, r_hbm, out_sem.at[2]),
        pltpu.make_async_copy(ws, w_hbm, out_sem.at[3]),
    ]
    G1_last[pl.ds(gy * nx + gx, 1), :] = jnp.sum(dots[0], axis=0, keepdims=True)
    phase_start(STEPS + 1, 0)
    for store in stores[1:]:
        store.start()

    def join_iterate(x, carry):
        xs[x] = (x0[x + 1] + alphas[0] * history[0, x]) + alphas[1] * history[1, x]
        return carry

    lax.fori_loop(0, cx, join_iterate, 0, unroll=4)
    stores[0].start()
    phase_wait(STEPS + 1, 0)
    G2_last[pl.ds(gz, 1), :] = jnp.sum(G1_last[...], axis=0, keepdims=True)
    phase_start(STEPS + 1, 1)
    phase_wait(STEPS + 1, 1)
    total = jnp.sum(jnp.sum(G2_last[...], axis=0, keepdims=True), axis=1, keepdims=True)
    step_out[...] = jnp.broadcast_to(ry / total, step_out.shape)
    for store in stores:
        store.wait()


def solution(mesh):
    nx, ny, nz = mesh.shape["gx"], mesh.shape["gy"], mesh.shape["gz"]

    def per_device(rhs, mobility, labels, coarse_inverse):
        cx, cy, cz = rhs.shape
        hbm = pl.BlockSpec(memory_space=pl.ANY)

        def vmem(*shape, dtype=F32):
            return pltpu.VMEM(shape, dtype)

        i32 = jnp.int32
        xs, p, rs, w, alpha = pl.pallas_call(
            functools.partial(kernel, nx, ny, nz),
            out_shape=[jax.ShapeDtypeStruct(rhs.shape, F32)] * 4
            + [jax.ShapeDtypeStruct((cy, cz), F32)],
            in_specs=[hbm] * 4,
            out_specs=[hbm] * 4 + [pl.BlockSpec(memory_space=pltpu.VMEM)],
            scratch_shapes=[
                *[vmem(cx + 2, cy, cz) for _ in range(4)],
                vmem(STEPS, cx, cy, cz),
                vmem(cx, cy, cz),
                vmem(cx, cy, cz, dtype=i32),
                vmem(*coarse_inverse.shape),
                vmem(*coarse_inverse.shape),
                vmem(6, *coarse_inverse.shape),
                vmem(cx + 1, cy, cz),
                *[vmem(cx, cy, cz) for _ in range(4)],
                vmem(4, cx, cy, cz),
                vmem(2, cx, cz),
                vmem(2, 8, 128),
                *[vmem(cx, cy, cz) for _ in range(3)],
                vmem(STEPS, 2, cy, cz),
                vmem(4, 2, cx, cz),
                vmem(4, 2, cx, cz),
                vmem(4, 2, 8, 128),
                vmem(4, 2, 2, 8, 128),
                vmem(2, cy, cz, dtype=i32),
                vmem(2, cx, cz, dtype=i32),
                vmem(2, cx, cz, dtype=i32),
                vmem(2, 8, 128, dtype=i32),
                vmem(2, 2, 8, 128, dtype=i32),
                vmem(2, 8, 128, dtype=i32),
                vmem(2, cy, cz),
                vmem(4, cx, cz),
                vmem(4, 8, 128),
                vmem(4, cx, cz),
                vmem(4, 8, 128),
                vmem(cx, 8, 128),
                vmem(cx, 8, 128, dtype=i32),
                vmem(cx, 8, 128),
                vmem(2, cx, cz),
                vmem(ny * nx, 128),
                vmem(nz, ny, 128),
                vmem(STEPS, ny * nx, 128),
                vmem(STEPS, nz, 3 * ny + 1, 128),
                vmem(ny * nx, 128),
                vmem(nz, 128),
                pltpu.SemaphoreType.DMA((4,)),
                pltpu.SemaphoreType.DMA((4,)),
                pltpu.SemaphoreType.DMA((6, 6)),
                pltpu.SemaphoreType.DMA((6, 6)),
                pltpu.SemaphoreType.DMA((5, 2)),
                pltpu.SemaphoreType.DMA((5, 2)),
            ],
            compiler_params=pltpu.CompilerParams(
                collective_id=0, has_side_effects=True, vmem_limit_bytes=VMEM_BYTES
            ),
            name="deflated_cg",
        )(rhs, mobility, labels, coarse_inverse)
        return xs + alpha * p, rs - alpha * w

    spec = P("gx", "gz", "gy")
    return jax.shard_map(
        per_device,
        mesh=mesh,
        in_specs=(spec, spec, spec, P(("gx", "gy", "gz"), None)),
        out_specs=(spec, spec),
        check_vma=False,
    )
```

```python
import functools

import jax
import jax.numpy as jnp
from jax import lax
from jax.experimental import pallas as pl
from jax.experimental.pallas import tpu as pltpu
from jax.sharding import PartitionSpec as P

LOGICAL = pl.DeviceIdType.LOGICAL
F32 = jnp.float32
LOOP = 5
VMEM_BYTES = 64 * 1024 * 1024 - 256 * 1024

STEPS = 3
MOB, LAB, INV = range(STEPS, STEPS + 3)


def farthest_first(n):
    return sorted(range(n), key=lambda k: -min(k, n - k))


def kernel(
    nx,
    ny,
    nz,
    rhs_hbm,
    mob_hbm,
    lab_hbm,
    inv_hbm,
    x_hbm,
    p_hbm,
    r_hbm,
    w_hbm,
    step_out,
    mob,
    x0,
    field,
    direction,
    history,
    rhs,
    lab,
    inv_in,
    inv,
    inv_far,
    fx,
    fy,
    fz,
    dinv,
    rim,
    bits,
    fyb,
    fzp,
    xs,
    rs,
    ws,
    xh,
    ys,
    yh,
    zs,
    zh,
    lxh,
    lys,
    lyh,
    lzs,
    lzh,
    lzf,
    yrim_x,
    yrim_y,
    yrim_z,
    prim_y,
    prim_z,
    zt,
    lt,
    et,
    ey,
    G1_first,
    G2_first,
    G1,
    G2,
    G1_last,
    G2_last,
    in_sem,
    out_sem,
    hs_sem,
    hr_sem,
    gs_sem,
    gr_sem,
):
    cx = rhs.shape[0]
    gx, gy, gz = lax.axis_index("gx"), lax.axis_index("gy"), lax.axis_index("gz")
    def logical(x, y, z):
        return (lax.rem(x, nx) * ny + lax.rem(y, ny)) * nz + lax.rem(z, nz)

    sides = (
        ("gx", gx > 0, logical(gx + nx - 1, gy, gz)),
        ("gx", gx < nx - 1, logical(gx + 1, gy, gz)),
        ("gz", gz > 0, logical(gx, gy, gz + nz - 1)),
        ("gz", gz < nz - 1, logical(gx, gy, gz + 1)),
        ("gy", gy > 0, logical(gx, gy + ny - 1, gz)),
        ("gy", gy < ny - 1, logical(gx, gy + 1, gz)),
    )

    loads = [
        pltpu.make_async_copy(rhs_hbm, rhs, in_sem.at[0]),
        pltpu.make_async_copy(lab_hbm, lab, in_sem.at[1]),
        pltpu.make_async_copy(mob_hbm, mob.at[pl.ds(1, cx)], in_sem.at[2]),
        pltpu.make_async_copy(inv_hbm, inv_in, in_sem.at[3]),
    ]
    for load in loads:
        load.start()

    def clear(ref, *index):
        ref[index or Ellipsis] = jnp.zeros(ref.shape[len(index) :], ref.dtype)

    for low in range(2):

        @pl.when(gx == (nx - 1 if low else 0))
        def _():
            clear(mob, cx + 1 if low else 0)
            clear(lxh, low)
            for e in range(STEPS):
                clear(xh, e, low)

        @pl.when(gz == (nz - 1 if low else 0))
        def _():
            clear(lyh, low)
            for e in range(STEPS + 1):
                clear(yh, e, low)

        @pl.when(gy == (ny - 1 if low else 0))
        def _():
            clear(lzh, low)
            for e in range(STEPS + 1):
                clear(zh, e, low)

    barrier = pltpu.get_barrier_semaphore()
    chips = nz // 2
    chip, core = lax.div(gz, 2), lax.rem(gz, 2)
    line_peers = [
        logical(gx + k, gy, 2 * chip + lax.rem(core + c, 2))
        for k in farthest_first(nx)
        for c in (1, 0)
        if k or c
    ]
    plane_peers = [
        logical(gx, gy + j, gz + 2 * k)
        for j in farthest_first(ny)
        for k in farthest_first(chips)
        if j or k
    ]
    phases = ((core * nx + gx, line_peers), (gy * chips + chip, plane_peers))
    partners = line_peers + plane_peers + [logical(gx, gy, gz + nz - 1 + 2 * core)]
    for partner in partners:
        pl.semaphore_signal(barrier, inc=1, device_id=partner, device_id_type=LOGICAL)

    clear(field, 0)
    clear(field, cx + 1)

    lane8 = lax.broadcasted_iota(jnp.int32, (8, 128), 1)
    row8 = lax.broadcasted_iota(jnp.int32, (8, 128), 0)
    lane16 = lax.broadcasted_iota(jnp.int32, (16, 128), 1)
    row16 = lax.broadcasted_iota(jnp.int32, (16, 128), 0)
    pair = ((lane8 + 1) >> 1) & 63
    ends = (lane8 == 0) | (lane8 == 127)
    even = (lane8 & 1) == 0
    zero = jnp.zeros((8, 128), F32)

    def fold(plane):
        tiles = [plane[k : k + 8] for k in range(0, plane.shape[0], 8)]
        while len(tiles) > 1:
            tiles = [a + b for a, b in zip(tiles[::2], tiles[1::2])]
        return tiles[0]

    def halo_copy(e, side):
        axis, _, index = sides[side]
        low, other = side & 1, 1 - (side & 1)
        kind = e if isinstance(e, int) else 0
        if kind == INV:
            src, dst = inv, inv_far.at[side ^ 1]
        elif kind == LAB:
            if axis == "gx":
                src, dst = lab.at[cx - 1 if low else 0], lxh.at[other]
            elif axis == "gz":
                src, dst = lys.at[low], lyh.at[other]
            else:
                src, dst = lzs, lzh.at[other]
        elif axis == "gx":
            src = (mob if kind == MOB else field).at[cx if low else 1]
            dst = mob.at[0 if low else cx + 1] if kind == MOB else xh.at[e, other]
        elif axis == "gz":
            src, dst = ys.at[e, low], yh.at[e, other]
        else:
            src, dst = zs.at[e], zh.at[e, other]
        return pltpu.make_async_remote_copy(
            src_ref=src,
            dst_ref=dst,
            send_sem=hs_sem.at[e, side],
            recv_sem=hr_sem.at[e, side ^ 1],
            device_id=index,
            device_id_type=LOGICAL,
        )

    def halo_landed(e, side):
        low = side & 1
        kind = e if isinstance(e, int) else 0
        if kind == INV:
            ref = inv_far.at[side]
        elif kind == LAB:
            ref = (lxh, lyh, lzh)[side // 2].at[low]
        elif side < 2:
            ref = mob.at[cx + 1 if low else 0] if kind == MOB else xh.at[e, low]
        else:
            ref = (yh, zh)[side // 2 - 1].at[e, low]
        return pltpu.make_async_copy(ref, ref, hr_sem.at[e, side])

    def exchange_start(e):
        for side in (0, 1, 4, 5, 2, 3):

            @pl.when(sides[side][1])
            def _():
                halo_copy(e, side).start()

    def exchange_wait(e):
        for side in range(6):

            @pl.when(sides[side][1])
            def _():
                halo_landed(e, side).wait()
                halo_copy(e, side).wait_send()

    def stage_rows(rows, x, plane):
        rows[0, pl.ds(x, 1), :] = plane[0:1]
        rows[1, pl.ds(x, 1), :] = plane[63:64]

    def pack_plane(plane):
        packed = plane[0:8]
        for k in range(1, 8):
            packed = jnp.where(pair == k, pltpu.roll(plane[8 * k : 8 * k + 8], 2 * k, 1), packed)
        return jnp.where(pair < 8, packed, jnp.zeros_like(packed))

    def pack_end(tiles, half):
        total = tiles[8 * half]
        for k in range(1, 8):
            total = total + pltpu.roll(tiles[8 * half + k], 16 * k, 1)
        return total

    def stage_plane(e, x, plane):
        stage_rows(ys.at[e], x, plane)
        zt[x] = pack_plane(plane)

    def stage_end(e):
        for half in range(2):
            zs[e, half] = pack_end(zt, half)

    def far(received, half):
        return jnp.where(
            even, pltpu.roll(received[0, half], 1, 1), pltpu.roll(received[1, half], 127, 1)
        )

    def spread(packed, half):
        et[8 * half] = packed
        for k in range(1, 8):
            et[8 * half + k] = pltpu.roll(packed, 128 - 16 * k, 1)

    def edge_part(x, v):
        return edge_tiles(x)

    def edge_tiles(x):
        tile = et[x]
        tiles = [
            jnp.where(ends, tile if k == 0 else pltpu.roll(tile, 128 - 2 * k, 1), 0.0)
            for k in range(8)
        ]
        first, last = ey[0, pl.ds(x, 1), :], ey[1, pl.ds(x, 1), :]
        tiles[0] = tiles[0] + jnp.where(row8 == 0, first, 0.0)
        tiles[7] = tiles[7] + jnp.where(row8 == 7, last, 0.0)
        return jnp.concatenate(tiles, axis=0)

    def apply_all(values, body, init, outer, make=None):
        def step(x, carry, above_v):
            below, v, rest = carry
            above = fx[x + 1] * (above_v - v)
            flux_y = fy[x] * (pltpu.roll(v, 63, 0) - v)
            flux_z = fz[x] * (pltpu.roll(v, 127, 1) - v)
            out = (
                (below - above)
                + (pltpu.roll(flux_y, 1, 0) - flux_y)
                + (pltpu.roll(flux_z, 1, 1) - flux_z)
                + outer(x, v)
            )
            return above, above_v, body(x, v, out, rest)

        if make is None:

            def make(x):
                return values[x + 1]

        v = make(0)
        carry = (fx[0] * (v - values[0]), v, init)
        carry = lax.fori_loop(
            0, cx - 1, lambda x, c: step(x, c, make(x + 1)), carry, unroll=LOOP
        )
        return step(cx - 1, carry, values[cx + 1])[2]

    def subset_sums(values, bits):
        terms = [values]
        for bit in bits:
            terms = terms + [term * bit for term in terms]
        return [fold(term) for term in terms]

    def label_sums(sums):
        sums = list(sums)
        for i in range(4):
            for value in range(16):
                if not value >> i & 1:
                    sums[value] = sums[value] - sums[value | 1 << i]
        return sums

    def bits_of(labels):
        return [((labels >> i) & 1).astype(F32) for i in range(4)]

    def by_label(labels, values):
        return label_sums(subset_sums(values, bits_of(labels)))

    def restrict_plane(x, plane, sums):
        more = subset_sums(plane, [bits[i, x] for i in range(4)])
        return tuple(total + extra for total, extra in zip(sums, more))

    def restrict_rhs(x, sums):
        planes = bits_of(lab[x])
        for i in range(4):
            bits[i, x] = planes[i]
        return tuple(total + extra for total, extra in zip(sums, subset_sums(rhs[x], planes)))

    no_sums = (zero,) * 16

    def rows_of(tiles):
        for shift in (4, 2, 1):
            low = (row8 & shift) == 0
            half = len(tiles) // 2
            merged = []
            for a, b in zip(tiles[:half], tiles[half:]):
                kept, moved = jnp.where(low, a, b), jnp.where(low, b, a)
                if shift == 4:
                    moved = pltpu.roll(moved, 4, 0)
                else:
                    moved = jnp.where(
                        low, pltpu.roll(moved, 8 - shift, 0), pltpu.roll(moved, shift, 0)
                    )
                merged.append(kept + moved)
            tiles = merged
        return tiles[0]

    def message(groups, dots):
        tiles = []
        for sums in groups:
            tiles += [rows_of(list(sums[:8])), rows_of(list(sums[8:]))]
        if dots:
            tiles.append(rows_of(list(dots) + [zero] * (8 - len(dots))))
        line = zero
        for k, tile in enumerate(tiles):
            column = jnp.sum(tile, axis=1, keepdims=True)
            line = line + jnp.where(lane8 == 8 * k + row8, column, 0.0)
        return jnp.sum(line, axis=0, keepdims=True)

    def transpose_groups(tile):
        for s in (4, 2, 1):
            group = (lane8 >> 4) & s
            up = pltpu.roll(pltpu.roll(tile, 8 - s, 0), 16 * s, 1)
            down = pltpu.roll(pltpu.roll(tile, s, 0), 128 - 16 * s, 1)
            tile = jnp.where((row8 & s) == group, tile, jnp.where(group != 0, up, down))
        return tile

    def neighbour_parts(e):
        parts = [
            by_label(lxh[0], -(fx[0] * field[1])),
            by_label(lxh[1], -(fx[cx] * field[cx])),
        ]
        for low in range(2):
            parts.append(by_label(lyh[low], -(fyb[low] * ys[e, low])))
        for keep in (even, ~even):
            halves = [
                by_label(lzf[half], jnp.where(keep, -(fzp[half] * zs[e, half]), 0.0))
                for half in range(2)
            ]
            parts.append([a + b for a, b in zip(*halves)])
        return parts

    def coarse_right_side(e):
        sums = apply_all(
            field, lambda x, v, out, s: restrict_plane(x, out, s), no_sums, lambda x, v: rim[x] * v
        )
        return label_sums(sums), neighbour_parts(e)

    def slots_of(g, ph):
        if isinstance(g, int):
            return ((G1_first, G2_first), (G1_last, G2_last))[g != 0][ph]
        return (G1, G2)[ph].at[g - 1]

    def phase_slots(g, ph, first, count):
        slots = slots_of(g, ph)
        return slots.at[pl.ds(first, count)]

    def phase_start(g, ph):
        me, peers = phases[ph]
        slot = phase_slots(g, ph, me, 1)
        for peer in peers:
            pltpu.make_async_remote_copy(
                src_ref=slot,
                dst_ref=slot,
                send_sem=gs_sem.at[g, ph],
                recv_sem=gr_sem.at[g, ph],
                device_id=peer,
                device_id_type=LOGICAL,
            ).start()

    def phase_wait(g, ph):
        part = phase_slots(g, ph, 0, len(phases[ph][1]))
        pltpu.make_async_copy(part, part, gr_sem.at[g, ph]).wait()
        pltpu.make_async_copy(part, part, gs_sem.at[g, ph]).wait()

    def group_lines(slots):
        return [transpose_groups(slots[nx * c : nx * (c + 1)]) for c in range(2)]

    def gather(g, line, started, between):
        G1[g - 1, pl.ds(phases[0][0], 1), :] = line
        phase_start(g, 0)
        started()
        phase_wait(g, 0)
        tiles = group_lines(G1.at[g - 1])

        def pick(group):
            return jnp.concatenate([tile[group : group + 1] for tile in tiles], axis=0)

        lane2 = lax.broadcasted_iota(jnp.int32, (2, 128), 1)
        own = pick(0)
        own = own + jnp.where(lane2 < 112, pltpu.roll(pick(1), 112, 1), 0.0)
        own = own + jnp.where(lane2 >= 16, pltpu.roll(pick(2), 16, 1), 0.0)
        own = own + jnp.concatenate([tiles[1][5:6], tiles[0][6:7]], axis=0)
        slot = phases[1][0]
        G2[g - 1, slot, 0:2] = own
        G2[g - 1, slot, 2:4] = pick(3)
        G2[g - 1, slot, 4:6] = pick(4)
        G2[g - 1, slot, 6:7] = tiles[0][5:6]
        G2[g - 1, slot, 7:8] = tiles[1][6:7]
        G2[g - 1, slot, 8:9] = tiles[0][7:8] + tiles[1][7:8]
        phase_start(g, 1)
        between()
        phase_wait(g, 1)

    def dots_of(g):
        row = jnp.sum(G2[g - 1, :, 8:9], axis=0)
        lane = lax.broadcasted_iota(jnp.int32, (1, 128), 1)
        return [
            jnp.broadcast_to(
                jnp.sum(jnp.where(lane & 15 == k, row, 0.0), axis=1, keepdims=True), (1, 128)
            )
            for k in range(3)
        ]

    def right_side(g):
        rows = [[None] * ny for _ in range(nz)]
        for j in range(ny):
            for k in range(chips):
                slot = j * chips + k
                if isinstance(g, int):
                    pairs = G2_first[slot]
                    low, high = pairs[0:1], pairs[1:2]
                else:
                    pairs = G2[g - 1, slot, 0:2]
                    if j + 1 < ny:
                        pairs = pairs + G2[g - 1, slot + chips, 2:4]
                    if j > 0:
                        pairs = pairs + G2[g - 1, slot - chips, 4:6]
                    low, high = pairs[0:1], pairs[1:2]
                    if k > 0:
                        low = low + G2[g - 1, slot - 1, 7:8]
                    if k + 1 < chips:
                        high = high + G2[g - 1, slot + 1, 6:7]
                rows[2 * k][j], rows[2 * k + 1][j] = low, high
        return rows

    def coarse(g):
        accs = [jnp.zeros((16, 128), F32) for _ in range(7)]
        for i, rows in enumerate(right_side(g)):
            for j in range(ny):
                columns = slice((i * ny + j) * 128, (i * ny + j + 1) * 128)
                row = rows[j]
                accs[6] = accs[6] + inv[:, columns] * row
                for side in range(6):
                    accs[side] = accs[side] + inv_far[side, :, columns] * row
        lines = []
        for side in range(7):
            total = jnp.sum(accs[side], axis=1, keepdims=True)
            line = jnp.sum(jnp.where(lane16 == row16, total, 0.0), axis=0, keepdims=True)
            if side < 6:
                index = lax.broadcasted_iota(jnp.int32, (1, 128), 1) * 0 + (gx, gz, gy)[side // 2]
                edge = (0, (nx, nz, ny)[side // 2] - 1)[side & 1]
                line = jnp.where(index == edge, 0.0, line)
            lines.append(line)
        return lines

    def take(line, labels):
        return jnp.take_along_axis(
            jnp.broadcast_to(line, labels.shape), labels, axis=1, mode="promise_in_bounds"
        )

    def rim_of(lines):
        x_far = [take(lines[low], lxh[low]) for low in range(2)]
        y_own = [take(lines[6], lys[low]) for low in range(2)]
        y_far = [take(lines[2 + low], lyh[low]) for low in range(2)]
        z_own = [take(lines[6], lzs[half]) for half in range(2)]
        z_far = [
            jnp.where(even, take(lines[4], lzf[half]), take(lines[5], lzf[half]))
            for half in range(2)
        ]
        return x_far, y_own, y_far, z_own, z_far

    def outer_faces(y_own, y_far, z_own, z_far):
        for low in range(2):
            ey[low] = fyb[low] * (y_own[low] - y_far[low])
        for half in range(2):
            spread(fzp[half] * (z_own[half] - z_far[half]), half)

    loads[0].wait()
    loads[1].wait()
    sums = lax.fori_loop(0, cx, restrict_rhs, no_sums, unroll=4)
    line = message([label_sums(sums)], ())
    pl.semaphore_wait(barrier, len(partners))
    G1_first[pl.ds(phases[0][0], 1), :] = line
    phase_start(0, 0)
    loads[2].wait()

    def order_columns():
        for top in (0, 8):
            for j in range(ny):
                tiles = [inv_in[top : top + 8, pl.ds((i * ny + j) * 128, 128)] for i in range(nx)]
                for s in (4, 2, 1):
                    clear_bit = (lane8 >> 4) & s == 0
                    for i in range(nx):
                        if not i & s:
                            a, b = tiles[i], tiles[i | s]
                            tiles[i] = jnp.where(clear_bit, a, pltpu.roll(b, 16 * s, 1))
                            tiles[i | s] = jnp.where(clear_bit, pltpu.roll(a, 128 - 16 * s, 1), b)
                for i in range(nz):
                    inv[top : top + 8, pl.ds((i * ny + j) * 128, 128)] = tiles[i]

    def stage_static(x, carry):
        stage_plane(MOB, x, mob[x + 1])
        labels = lab[x]
        stage_rows(lys, x, labels)
        lt[x] = pack_plane(labels)
        return carry

    lax.fori_loop(0, cx, stage_static, 0, unroll=4)
    stage_end(MOB)
    for half in range(2):
        lzs[half] = pack_end(lt, half)
    exchange_start(MOB)
    exchange_start(LAB)
    loads[3].wait()
    order_columns()
    exchange_start(INV)

    def faces():
        for ref in (direction, ws, yrim_x, yrim_y, yrim_z, prim_y, prim_z):
            clear(ref)
        exchange_wait(MOB)
        exchange_wait(LAB)
        for half in range(2):
            lzf[half] = far(lzh, half)
            fzp[half] = 0.5 * (zs[MOB, half] + far(zh.at[MOB], half))
            spread(fzp[half], half)
        for low in range(2):
            fyb[low] = 0.5 * (ys[MOB, low] + yh[MOB, low])
            ey[low] = fyb[low]
        fx[0] = 0.5 * (mob[1] + mob[0])
        row = lax.broadcasted_iota(jnp.int32, (64, 128), 0)
        lane = lax.broadcasted_iota(jnp.int32, (64, 128), 1)

        def step(x, below):
            m = mob[x + 1]
            above = 0.5 * (mob[x + 2] + m)
            face_y = jnp.where(row == 63, 0.0, 0.5 * (pltpu.roll(m, 63, 0) + m))
            face_z = jnp.where(lane == 127, 0.0, 0.5 * (pltpu.roll(m, 127, 1) + m))
            edges = edge_tiles(x)
            diag = (
                (below + above)
                + (pltpu.roll(face_y, 1, 0) + face_y)
                + (pltpu.roll(face_z, 1, 1) + face_z)
                + edges
            )
            rim[x] = edges
            fx[x + 1] = above
            fy[x] = face_y
            fz[x] = face_z
            dinv[x] = 1.0 / diag
            return above

        lax.fori_loop(0, cx, step, fx[0], unroll=4)

    phase_wait(0, 0)
    G2_first[phases[1][0]] = jnp.concatenate(
        [tile[0:1] for tile in group_lines(G1_first)], axis=0
    )
    phase_start(0, 1)
    faces()
    phase_wait(0, 1)

    exchange_wait(INV)
    lines = coarse(0)

    def first_iterate(x):
        plane = take(lines[6], lab[x])
        x0[x + 1] = plane
        return plane

    x_far, *rest = rim_of(lines)
    x0[0] = x_far[0]
    x0[cx + 1] = x_far[1]
    outer_faces(*rest)

    def first_residual(x, v, out, dot):
        residual = rhs[x] - out
        precond = residual * dinv[x]
        rs[x] = residual
        field[x + 1] = precond
        stage_plane(0, x, precond)
        return dot + fold(residual * precond)

    ry_part = apply_all(x0, first_residual, zero, edge_part, first_iterate)
    stage_end(0)

    def tall(row):
        return jnp.broadcast_to(row, (8, 128))

    def one_step(k, carry):
        ry, lines, dots, _, last_alpha = carry
        ry, lines = ry[0:1], [line[0:1] for line in lines]
        sums, parts = coarse_right_side(k)
        gather(
            k + 1,
            message([sums] + [parts[side] for side in (0, 1, 4, 5, 2, 3)], dots),
            lambda: exchange_start(k),
            lambda: exchange_wait(k),
        )
        more = coarse(k + 1)
        d0, d1, d2 = dots_of(k + 1)
        first = lax.broadcasted_iota(jnp.int32, (1, 128), 0) + k == 0
        alpha = jnp.where(first, 0.0, ry / d0)
        ry_next = jnp.where(first, d0, ry + alpha * (alpha * d2 - 2.0 * d1))
        beta = jnp.where(first, 0.0, ry_next / ry)
        gain = jnp.where(first, 1.0, -alpha)
        lines = [line + gain * extra for line, extra in zip(lines, more)]

        x_far, y_own, y_far, z_own, z_far = rim_of(lines)
        for low in range(2):
            outer = cx + 1 if low else 0
            layer = yrim_x[low] + gain * xh[k, low]
            yrim_x[low] = layer
            direction[outer] = (layer + beta * direction[outer]) - x_far[low]
        rows = [ys[k, 0], ys[k, 1], yh[k, 0], yh[k, 1]]
        packs = [zs[k, 0], zs[k, 1], far(zh.at[k], 0), far(zh.at[k], 1)]
        for i, (y_part, z_part) in enumerate(zip(y_own + y_far, z_own + z_far)):
            row = yrim_y[i] + gain * rows[i]
            pack = yrim_z[i] + gain * packs[i]
            yrim_y[i] = row
            yrim_z[i] = pack
            prim_y[i] = (row + beta * prim_y[i]) - y_part
            prim_z[i] = (pack + beta * prim_z[i]) - z_part
        outer_faces(
            [prim_y[0], prim_y[1]],
            [prim_y[2], prim_y[3]],
            [prim_z[0], prim_z[1]],
            [prim_z[2], prim_z[3]],
        )

        def next_direction(x):
            residual = rs[x] - alpha * ws[x]
            rs[x] = residual
            plane = (residual * dinv[x] + beta * direction[x + 1]) - take(lines[6], lab[x])
            direction[x + 1] = plane
            history[k, x] = plane
            return plane

        def image(x, v, out, dots):
            z = out * dinv[x]
            ws[x] = out
            field[x + 1] = z
            stage_plane(k + 1, x, z)
            return (
                dots[0] + fold(v * out),
                dots[1] + fold(rs[x] * z),
                dots[2] + fold(out * z),
            )

        dots = apply_all(direction, image, (zero, zero, zero), edge_part, next_direction)
        stage_end(k + 1)
        return tall(ry_next), [tall(line) for line in lines], dots, last_alpha, tall(alpha)

    ry, _, dots, *alphas = lax.fori_loop(
        0, STEPS, one_step, (zero + 1.0, [zero] * 7, (ry_part, zero, zero), zero, zero)
    )
    ry, alphas = ry[0:1], [alpha[0:1] for alpha in alphas]

    stores = [
        pltpu.make_async_copy(xs, x_hbm, out_sem.at[0]),
        pltpu.make_async_copy(history.at[STEPS - 1], p_hbm, out_sem.at[1]),
        pltpu.make_async_copy(rs, r_hbm, out_sem.at[2]),
        pltpu.make_async_copy(ws, w_hbm, out_sem.at[3]),
    ]
    G1_last[pl.ds(phases[0][0], 1), :] = jnp.sum(dots[0], axis=0, keepdims=True)
    phase_start(STEPS + 1, 0)
    for store in stores[1:]:
        store.start()

    def join_iterate(x, carry):
        xs[x] = (x0[x + 1] + alphas[0] * history[0, x]) + alphas[1] * history[1, x]
        return carry

    lax.fori_loop(0, cx, join_iterate, 0, unroll=4)
    stores[0].start()
    phase_wait(STEPS + 1, 0)
    G2_last[pl.ds(phases[1][0], 1), :] = jnp.sum(G1_last[...], axis=0, keepdims=True)
    phase_start(STEPS + 1, 1)
    phase_wait(STEPS + 1, 1)
    total = jnp.sum(jnp.sum(G2_last[...], axis=0, keepdims=True), axis=1, keepdims=True)
    step_out[...] = jnp.broadcast_to(ry / total, step_out.shape)
    for store in stores:
        store.wait()


def solution(mesh):
    nx, ny, nz = mesh.shape["gx"], mesh.shape["gy"], mesh.shape["gz"]

    def per_device(rhs, mobility, labels, coarse_inverse):
        cx, cy, cz = rhs.shape
        hbm = pl.BlockSpec(memory_space=pl.ANY)

        def vmem(*shape, dtype=F32):
            return pltpu.VMEM(shape, dtype)

        i32 = jnp.int32
        xs, p, rs, w, alpha = pl.pallas_call(
            functools.partial(kernel, nx, ny, nz),
            out_shape=[jax.ShapeDtypeStruct(rhs.shape, F32)] * 4
            + [jax.ShapeDtypeStruct((cy, cz), F32)],
            in_specs=[hbm] * 4,
            out_specs=[hbm] * 4 + [pl.BlockSpec(memory_space=pltpu.VMEM)],
            scratch_shapes=[
                *[vmem(cx + 2, cy, cz) for _ in range(4)],
                vmem(STEPS, cx, cy, cz),
                vmem(cx, cy, cz),
                vmem(cx, cy, cz, dtype=i32),
                vmem(*coarse_inverse.shape),
                vmem(*coarse_inverse.shape),
                vmem(6, *coarse_inverse.shape),
                vmem(cx + 1, cy, cz),
                *[vmem(cx, cy, cz) for _ in range(4)],
                vmem(4, cx, cy, cz),
                vmem(2, cx, cz),
                vmem(2, 8, 128),
                *[vmem(cx, cy, cz) for _ in range(3)],
                vmem(STEPS, 2, cy, cz),
                vmem(4, 2, cx, cz),
                vmem(4, 2, cx, cz),
                vmem(4, 2, 8, 128),
                vmem(4, 2, 2, 8, 128),
                vmem(2, cy, cz, dtype=i32),
                vmem(2, cx, cz, dtype=i32),
                vmem(2, cx, cz, dtype=i32),
                vmem(2, 8, 128, dtype=i32),
                vmem(2, 2, 8, 128, dtype=i32),
                vmem(2, 8, 128, dtype=i32),
                vmem(2, cy, cz),
                vmem(4, cx, cz),
                vmem(4, 8, 128),
                vmem(4, cx, cz),
                vmem(4, 8, 128),
                vmem(cx, 8, 128),
                vmem(cx, 8, 128, dtype=i32),
                vmem(cx, 8, 128),
                vmem(2, cx, cz),
                vmem(2 * nx, 128),
                vmem(ny * nz // 2, 2, 128),
                vmem(STEPS, 2 * nx, 128),
                vmem(STEPS, ny * nz // 2, 9, 128),
                vmem(2 * nx, 128),
                vmem(ny * nz // 2, 128),
                pltpu.SemaphoreType.DMA((4,)),
                pltpu.SemaphoreType.DMA((4,)),
                pltpu.SemaphoreType.DMA((6, 6)),
                pltpu.SemaphoreType.DMA((6, 6)),
                pltpu.SemaphoreType.DMA((5, 2)),
                pltpu.SemaphoreType.DMA((5, 2)),
            ],
            compiler_params=pltpu.CompilerParams(
                collective_id=0, has_side_effects=True, vmem_limit_bytes=VMEM_BYTES
            ),
            name="deflated_cg",
        )(rhs, mobility, labels, coarse_inverse)
        return xs + alpha * p, rs - alpha * w

    spec = P("gx", "gz", "gy")
    return jax.shard_map(
        per_device,
        mesh=mesh,
        in_specs=(spec, spec, spec, P(("gx", "gy", "gz"), None)),
        out_specs=(spec, spec),
        check_vma=False,
    )
```

```python
import functools

import jax
import jax.numpy as jnp
from jax import lax
from jax.experimental import pallas as pl
from jax.experimental.pallas import tpu as pltpu
from jax.sharding import PartitionSpec as P

LOGICAL = pl.DeviceIdType.LOGICAL
F32 = jnp.float32
LOOP = 5
VMEM_BYTES = 64 * 1024 * 1024 - 256 * 1024

STEPS = 3
MOB, LAB, INV = range(STEPS, STEPS + 3)


def farthest_first(n):
    return sorted(range(n), key=lambda k: -min(k, n - k))


def kernel(
    nx,
    ny,
    nz,
    rhs_hbm,
    mob_hbm,
    lab_hbm,
    inv_hbm,
    x_hbm,
    p_hbm,
    r_hbm,
    w_hbm,
    step_out,
    mob,
    x0,
    field,
    direction,
    history,
    rhs_in,
    lab_in,
    mob_in,
    rhs,
    lab,
    inv_in,
    inv,
    inv_far,
    fx,
    fy,
    fz,
    dinv,
    rim,
    bits,
    fyb,
    fzp,
    ordered,
    rs,
    ws,
    xh,
    ys,
    yh,
    zs,
    zh,
    lxh,
    lys,
    lyh,
    lzs,
    lzh,
    lzf,
    yrim_x,
    yrim_y,
    yrim_z,
    prim_y,
    prim_z,
    zt,
    lt,
    et,
    ey,
    G1_first,
    G2_first,
    G1,
    G2,
    G1_last,
    G2_last,
    in_sem,
    out_sem,
    hs_sem,
    hr_sem,
    gs_sem,
    gr_sem,
):
    cx = rhs.shape[0]
    gx, gy, gz = lax.axis_index("gx"), lax.axis_index("gy"), lax.axis_index("gz")
    def logical(x, y, z):
        return (lax.rem(x, nx) * ny + lax.rem(y, ny)) * nz + lax.rem(z, nz)

    sides = (
        ("gx", gx > 0, logical(gx + nx - 1, gy, gz)),
        ("gx", gx < nx - 1, logical(gx + 1, gy, gz)),
        ("gz", gz > 0, logical(gx, gy, gz + nz - 1)),
        ("gz", gz < nz - 1, logical(gx, gy, gz + 1)),
        ("gy", gy > 0, logical(gx, gy + ny - 1, gz)),
        ("gy", gy < ny - 1, logical(gx, gy + 1, gz)),
    )

    loads = [
        pltpu.make_async_copy(rhs_hbm, rhs_in, in_sem.at[0]),
        pltpu.make_async_copy(lab_hbm, lab_in, in_sem.at[1]),
        pltpu.make_async_copy(mob_hbm, mob_in, in_sem.at[2]),
        pltpu.make_async_copy(inv_hbm, inv_in, in_sem.at[3]),
    ]
    for load in loads:
        load.start()

    def clear(ref, *index):
        ref[index or Ellipsis] = jnp.zeros(ref.shape[len(index) :], ref.dtype)

    for low in range(2):

        @pl.when(gx == (nx - 1 if low else 0))
        def _():
            clear(mob, cx + 1 if low else 0)
            clear(lxh, low)
            for e in range(STEPS):
                clear(xh, e, low)

        @pl.when(gz == (nz - 1 if low else 0))
        def _():
            clear(lyh, low)
            for e in range(STEPS + 1):
                clear(yh, e, low)

        @pl.when(gy == (ny - 1 if low else 0))
        def _():
            clear(lzh, low)
            for e in range(STEPS + 1):
                clear(zh, e, low)

    barrier = pltpu.get_barrier_semaphore()
    chips = nz // 2
    chip, core = lax.div(gz, 2), lax.rem(gz, 2)
    line_peers = [
        logical(gx + k, gy, 2 * chip + lax.rem(core + c, 2))
        for k in farthest_first(nx)
        for c in (1, 0)
        if k or c
    ]
    plane_peers = [
        logical(gx, gy + j, gz + 2 * k)
        for j in farthest_first(ny)
        for k in farthest_first(chips)
        if j or k
    ]
    phases = ((core * nx + gx, line_peers), (gy * chips + chip, plane_peers))
    partners = line_peers + plane_peers + [logical(gx, gy, gz + nz - 1 + 2 * core)]
    for partner in partners:
        pl.semaphore_signal(barrier, inc=1, device_id=partner, device_id_type=LOGICAL)

    clear(field, 0)
    clear(field, cx + 1)

    lane8 = lax.broadcasted_iota(jnp.int32, (8, 128), 1)
    row8 = lax.broadcasted_iota(jnp.int32, (8, 128), 0)
    lane16 = lax.broadcasted_iota(jnp.int32, (16, 128), 1)
    row16 = lax.broadcasted_iota(jnp.int32, (16, 128), 0)
    pair = ((lane8 + 1) >> 1) & 63
    ends = (lane8 == 0) | (lane8 == 127)
    even = (lane8 & 1) == 0
    zero = jnp.zeros((8, 128), F32)

    def interleaved(ref, x):
        return jnp.concatenate([ref[x, pl.ds(k, 8, stride=8), :] for k in range(8)], axis=0)

    def store_in_order(ref, x, plane):
        for k in range(8):
            ref[x, pl.ds(k, 8, stride=8), :] = plane[8 * k : 8 * k + 8]

    def next_row(plane):
        return jnp.concatenate([plane[8:], pltpu.roll(plane[:8], 7, 0)], axis=0)

    def last_row(plane):
        return jnp.concatenate([pltpu.roll(plane[56:], 1, 0), plane[:56]], axis=0)

    def fold(plane):
        tiles = [plane[k : k + 8] for k in range(0, plane.shape[0], 8)]
        while len(tiles) > 1:
            tiles = [a + b for a, b in zip(tiles[::2], tiles[1::2])]
        return tiles[0]

    def halo_copy(e, side):
        axis, _, index = sides[side]
        low, other = side & 1, 1 - (side & 1)
        kind = e if isinstance(e, int) else 0
        if kind == INV:
            src, dst = inv, inv_far.at[side ^ 1]
        elif kind == LAB:
            if axis == "gx":
                src, dst = lab.at[cx - 1 if low else 0], lxh.at[other]
            elif axis == "gz":
                src, dst = lys.at[low], lyh.at[other]
            else:
                src, dst = lzs, lzh.at[other]
        elif axis == "gx":
            src = (mob if kind == MOB else field).at[cx if low else 1]
            dst = mob.at[0 if low else cx + 1] if kind == MOB else xh.at[e, other]
        elif axis == "gz":
            src, dst = ys.at[e, low], yh.at[e, other]
        else:
            src, dst = zs.at[e], zh.at[e, other]
        return pltpu.make_async_remote_copy(
            src_ref=src,
            dst_ref=dst,
            send_sem=hs_sem.at[e, side],
            recv_sem=hr_sem.at[e, side ^ 1],
            device_id=index,
            device_id_type=LOGICAL,
        )

    def halo_landed(e, side):
        low = side & 1
        kind = e if isinstance(e, int) else 0
        if kind == INV:
            ref = inv_far.at[side]
        elif kind == LAB:
            ref = (lxh, lyh, lzh)[side // 2].at[low]
        elif side < 2:
            ref = mob.at[cx + 1 if low else 0] if kind == MOB else xh.at[e, low]
        else:
            ref = (yh, zh)[side // 2 - 1].at[e, low]
        return pltpu.make_async_copy(ref, ref, hr_sem.at[e, side])

    def exchange_start(e):
        for side in (0, 1, 4, 5, 2, 3):

            @pl.when(sides[side][1])
            def _():
                halo_copy(e, side).start()

    def exchange_wait(e):
        for side in range(6):

            @pl.when(sides[side][1])
            def _():
                halo_landed(e, side).wait()
                halo_copy(e, side).wait_send()

    def stage_rows(rows, x, plane):
        rows[0, pl.ds(x, 1), :] = plane[0:1]
        rows[1, pl.ds(x, 1), :] = plane[63:64]

    def pack_plane(plane):
        packed = plane[0:8]
        for k in range(1, 8):
            packed = jnp.where(pair == k, pltpu.roll(plane[8 * k : 8 * k + 8], 2 * k, 1), packed)
        return jnp.where(pair < 8, packed, jnp.zeros_like(packed))

    def pack_end(tiles, half):
        total = tiles[8 * half]
        for k in range(1, 8):
            total = total + pltpu.roll(tiles[8 * half + k], 16 * k, 1)
        return total

    def stage_plane(e, x, plane):
        stage_rows(ys.at[e], x, plane)
        zt[x] = pack_plane(plane)

    def stage_end(e):
        for half in range(2):
            zs[e, half] = pack_end(zt, half)

    def far(received, half):
        return jnp.where(
            even, pltpu.roll(received[0, half], 1, 1), pltpu.roll(received[1, half], 127, 1)
        )

    def spread(packed, half):
        et[8 * half] = packed
        for k in range(1, 8):
            et[8 * half + k] = pltpu.roll(packed, 128 - 16 * k, 1)

    def edge_part(x, v):
        return edge_tiles(x)

    def edge_tiles(x):
        tile = et[x]
        tiles = [
            jnp.where(ends, tile if k == 0 else pltpu.roll(tile, 128 - 2 * k, 1), 0.0)
            for k in range(8)
        ]
        first, last = ey[0, pl.ds(x, 1), :], ey[1, pl.ds(x, 1), :]
        tiles[0] = tiles[0] + jnp.where(row8 == 0, first, 0.0)
        tiles[7] = tiles[7] + jnp.where(row8 == 7, last, 0.0)
        return jnp.concatenate(tiles, axis=0)

    def apply_all(values, body, init, outer, make=None):
        def step(x, carry, above_v):
            below, v, rest = carry
            above = fx[x + 1] * (above_v - v)
            flux_y = fy[x] * (next_row(v) - v)
            flux_z = fz[x] * (pltpu.roll(v, 127, 1) - v)
            out = (
                (below - above)
                + (last_row(flux_y) - flux_y)
                + (pltpu.roll(flux_z, 1, 1) - flux_z)
                + outer(x, v)
            )
            return above, above_v, body(x, v, out, rest)

        if make is None:

            def make(x):
                return values[x + 1]

        v = make(0)
        carry = (fx[0] * (v - values[0]), v, init)
        carry = lax.fori_loop(
            0, cx - 1, lambda x, c: step(x, c, make(x + 1)), carry, unroll=LOOP
        )
        return step(cx - 1, carry, values[cx + 1])[2]

    def subset_sums(values, bits):
        terms = [values]
        for bit in bits:
            terms = terms + [term * bit for term in terms]
        return [fold(term) for term in terms]

    def label_sums(sums):
        sums = list(sums)
        for i in range(4):
            for value in range(16):
                if not value >> i & 1:
                    sums[value] = sums[value] - sums[value | 1 << i]
        return sums

    def bits_of(labels):
        return [((labels >> i) & 1).astype(F32) for i in range(4)]

    def by_label(labels, values):
        return label_sums(subset_sums(values, bits_of(labels)))

    def restrict_plane(x, plane, sums):
        more = subset_sums(plane, [bits[i, x] for i in range(4)])
        return tuple(total + extra for total, extra in zip(sums, more))

    def restrict_rhs(x, sums):
        labels = interleaved(lab_in, x)
        values = interleaved(rhs_in, x)
        lab[x] = labels
        rhs[x] = values
        planes = bits_of(labels)
        for i in range(4):
            bits[i, x] = planes[i]
        return tuple(total + extra for total, extra in zip(sums, subset_sums(values, planes)))

    no_sums = (zero,) * 16

    def rows_of(tiles):
        for shift in (4, 2, 1):
            low = (row8 & shift) == 0
            half = len(tiles) // 2
            merged = []
            for a, b in zip(tiles[:half], tiles[half:]):
                kept, moved = jnp.where(low, a, b), jnp.where(low, b, a)
                if shift == 4:
                    moved = pltpu.roll(moved, 4, 0)
                else:
                    moved = jnp.where(
                        low, pltpu.roll(moved, 8 - shift, 0), pltpu.roll(moved, shift, 0)
                    )
                merged.append(kept + moved)
            tiles = merged
        return tiles[0]

    def message(groups, dots):
        tiles = []
        for sums in groups:
            tiles += [rows_of(list(sums[:8])), rows_of(list(sums[8:]))]
        if dots:
            tiles.append(rows_of(list(dots) + [zero] * (8 - len(dots))))
        line = zero
        for k, tile in enumerate(tiles):
            column = jnp.sum(tile, axis=1, keepdims=True)
            line = line + jnp.where(lane8 == 8 * k + row8, column, 0.0)
        return jnp.sum(line, axis=0, keepdims=True)

    def transpose_groups(tile):
        for s in (4, 2, 1):
            group = (lane8 >> 4) & s
            up = pltpu.roll(pltpu.roll(tile, 8 - s, 0), 16 * s, 1)
            down = pltpu.roll(pltpu.roll(tile, s, 0), 128 - 16 * s, 1)
            tile = jnp.where((row8 & s) == group, tile, jnp.where(group != 0, up, down))
        return tile

    def neighbour_parts(e):
        parts = [
            by_label(lxh[0], -(fx[0] * field[1])),
            by_label(lxh[1], -(fx[cx] * field[cx])),
        ]
        for low in range(2):
            parts.append(by_label(lyh[low], -(fyb[low] * ys[e, low])))
        for keep in (even, ~even):
            halves = [
                by_label(lzf[half], jnp.where(keep, -(fzp[half] * zs[e, half]), 0.0))
                for half in range(2)
            ]
            parts.append([a + b for a, b in zip(*halves)])
        return parts

    def coarse_right_side(e):
        sums = apply_all(
            field, lambda x, v, out, s: restrict_plane(x, out, s), no_sums, lambda x, v: rim[x] * v
        )
        return label_sums(sums), neighbour_parts(e)

    def slots_of(g, ph):
        if isinstance(g, int):
            return ((G1_first, G2_first), (G1_last, G2_last))[g != 0][ph]
        return (G1, G2)[ph].at[g - 1]

    def phase_slots(g, ph, first, count):
        slots = slots_of(g, ph)
        return slots.at[pl.ds(first, count)]

    def phase_start(g, ph):
        me, peers = phases[ph]
        slot = phase_slots(g, ph, me, 1)
        for peer in peers:
            pltpu.make_async_remote_copy(
                src_ref=slot,
                dst_ref=slot,
                send_sem=gs_sem.at[g, ph],
                recv_sem=gr_sem.at[g, ph],
                device_id=peer,
                device_id_type=LOGICAL,
            ).start()

    def phase_wait(g, ph):
        part = phase_slots(g, ph, 0, len(phases[ph][1]))
        pltpu.make_async_copy(part, part, gr_sem.at[g, ph]).wait()
        pltpu.make_async_copy(part, part, gs_sem.at[g, ph]).wait()

    def group_lines(slots):
        return [transpose_groups(slots[nx * c : nx * (c + 1)]) for c in range(2)]

    def gather(g, line, started, between):
        G1[g - 1, pl.ds(phases[0][0], 1), :] = line
        phase_start(g, 0)
        started()
        phase_wait(g, 0)
        tiles = group_lines(G1.at[g - 1])

        def pick(group):
            return jnp.concatenate([tile[group : group + 1] for tile in tiles], axis=0)

        lane2 = lax.broadcasted_iota(jnp.int32, (2, 128), 1)
        own = pick(0)
        own = own + jnp.where(lane2 < 112, pltpu.roll(pick(1), 112, 1), 0.0)
        own = own + jnp.where(lane2 >= 16, pltpu.roll(pick(2), 16, 1), 0.0)
        own = own + jnp.concatenate([tiles[1][5:6], tiles[0][6:7]], axis=0)
        slot = phases[1][0]
        G2[g - 1, slot, 0:2] = own
        G2[g - 1, slot, 2:4] = pick(3)
        G2[g - 1, slot, 4:6] = pick(4)
        G2[g - 1, slot, 6:7] = tiles[0][5:6]
        G2[g - 1, slot, 7:8] = tiles[1][6:7]
        G2[g - 1, slot, 8:9] = tiles[0][7:8] + tiles[1][7:8]
        phase_start(g, 1)
        between()
        phase_wait(g, 1)

    def dots_of(g):
        row = jnp.sum(G2[g - 1, :, 8:9], axis=0)
        lane = lax.broadcasted_iota(jnp.int32, (1, 128), 1)
        return [
            jnp.broadcast_to(
                jnp.sum(jnp.where(lane & 15 == k, row, 0.0), axis=1, keepdims=True), (1, 128)
            )
            for k in range(3)
        ]

    def right_side(g):
        rows = [[None] * ny for _ in range(nz)]
        for j in range(ny):
            for k in range(chips):
                slot = j * chips + k
                if isinstance(g, int):
                    pairs = G2_first[slot]
                    low, high = pairs[0:1], pairs[1:2]
                else:
                    pairs = G2[g - 1, slot, 0:2]
                    if j + 1 < ny:
                        pairs = pairs + G2[g - 1, slot + chips, 2:4]
                    if j > 0:
                        pairs = pairs + G2[g - 1, slot - chips, 4:6]
                    low, high = pairs[0:1], pairs[1:2]
                    if k > 0:
                        low = low + G2[g - 1, slot - 1, 7:8]
                    if k + 1 < chips:
                        high = high + G2[g - 1, slot + 1, 6:7]
                rows[2 * k][j], rows[2 * k + 1][j] = low, high
        return rows

    def coarse(g):
        accs = [jnp.zeros((16, 128), F32) for _ in range(7)]
        for i, rows in enumerate(right_side(g)):
            for j in range(ny):
                columns = slice((i * ny + j) * 128, (i * ny + j + 1) * 128)
                row = rows[j]
                accs[6] = accs[6] + inv[:, columns] * row
                for side in range(6):
                    accs[side] = accs[side] + inv_far[side, :, columns] * row
        lines = []
        for side in range(7):
            total = jnp.sum(accs[side], axis=1, keepdims=True)
            line = jnp.sum(jnp.where(lane16 == row16, total, 0.0), axis=0, keepdims=True)
            if side < 6:
                index = lax.broadcasted_iota(jnp.int32, (1, 128), 1) * 0 + (gx, gz, gy)[side // 2]
                edge = (0, (nx, nz, ny)[side // 2] - 1)[side & 1]
                line = jnp.where(index == edge, 0.0, line)
            lines.append(line)
        return lines

    def take(line, labels):
        return jnp.take_along_axis(
            jnp.broadcast_to(line, labels.shape), labels, axis=1, mode="promise_in_bounds"
        )

    def rim_of(lines):
        x_far = [take(lines[low], lxh[low]) for low in range(2)]
        y_own = [take(lines[6], lys[low]) for low in range(2)]
        y_far = [take(lines[2 + low], lyh[low]) for low in range(2)]
        z_own = [take(lines[6], lzs[half]) for half in range(2)]
        z_far = [
            jnp.where(even, take(lines[4], lzf[half]), take(lines[5], lzf[half]))
            for half in range(2)
        ]
        return x_far, y_own, y_far, z_own, z_far

    def outer_faces(y_own, y_far, z_own, z_far):
        for low in range(2):
            ey[low] = fyb[low] * (y_own[low] - y_far[low])
        for half in range(2):
            spread(fzp[half] * (z_own[half] - z_far[half]), half)

    loads[0].wait()
    loads[1].wait()
    sums = lax.fori_loop(0, cx, restrict_rhs, no_sums, unroll=4)
    line = message([label_sums(sums)], ())
    pl.semaphore_wait(barrier, len(partners))
    G1_first[pl.ds(phases[0][0], 1), :] = line
    phase_start(0, 0)
    loads[2].wait()

    def order_columns():
        for top in (0, 8):
            for j in range(ny):
                tiles = [inv_in[top : top + 8, pl.ds((i * ny + j) * 128, 128)] for i in range(nx)]
                for s in (4, 2, 1):
                    clear_bit = (lane8 >> 4) & s == 0
                    for i in range(nx):
                        if not i & s:
                            a, b = tiles[i], tiles[i | s]
                            tiles[i] = jnp.where(clear_bit, a, pltpu.roll(b, 16 * s, 1))
                            tiles[i | s] = jnp.where(clear_bit, pltpu.roll(a, 128 - 16 * s, 1), b)
                for i in range(nz):
                    inv[top : top + 8, pl.ds((i * ny + j) * 128, 128)] = tiles[i]

    def stage_static(x, carry):
        mobility = interleaved(mob_in, x)
        mob[x + 1] = mobility
        stage_plane(MOB, x, mobility)
        labels = lab[x]
        stage_rows(lys, x, labels)
        lt[x] = pack_plane(labels)
        return carry

    lax.fori_loop(0, cx, stage_static, 0, unroll=4)
    stage_end(MOB)
    for half in range(2):
        lzs[half] = pack_end(lt, half)
    exchange_start(MOB)
    exchange_start(LAB)
    loads[3].wait()
    order_columns()
    exchange_start(INV)

    def faces():
        for ref in (direction, ws, yrim_x, yrim_y, yrim_z, prim_y, prim_z):
            clear(ref)
        exchange_wait(MOB)
        exchange_wait(LAB)
        for half in range(2):
            lzf[half] = far(lzh, half)
            fzp[half] = 0.5 * (zs[MOB, half] + far(zh.at[MOB], half))
            spread(fzp[half], half)
        for low in range(2):
            fyb[low] = 0.5 * (ys[MOB, low] + yh[MOB, low])
            ey[low] = fyb[low]
        fx[0] = 0.5 * (mob[1] + mob[0])
        row = lax.broadcasted_iota(jnp.int32, (64, 128), 0)
        lane = lax.broadcasted_iota(jnp.int32, (64, 128), 1)

        def step(x, below):
            m = mob[x + 1]
            above = 0.5 * (mob[x + 2] + m)
            face_y = jnp.where(row == 63, 0.0, 0.5 * (next_row(m) + m))
            face_z = jnp.where(lane == 127, 0.0, 0.5 * (pltpu.roll(m, 127, 1) + m))
            edges = edge_tiles(x)
            diag = (
                (below + above)
                + (last_row(face_y) + face_y)
                + (pltpu.roll(face_z, 1, 1) + face_z)
                + edges
            )
            rim[x] = edges
            fx[x + 1] = above
            fy[x] = face_y
            fz[x] = face_z
            dinv[x] = 1.0 / diag
            return above

        lax.fori_loop(0, cx, step, fx[0], unroll=4)

    phase_wait(0, 0)
    G2_first[phases[1][0]] = jnp.concatenate(
        [tile[0:1] for tile in group_lines(G1_first)], axis=0
    )
    phase_start(0, 1)
    faces()
    phase_wait(0, 1)

    exchange_wait(INV)
    lines = coarse(0)

    def first_iterate(x):
        plane = take(lines[6], lab[x])
        x0[x + 1] = plane
        return plane

    x_far, *rest = rim_of(lines)
    x0[0] = x_far[0]
    x0[cx + 1] = x_far[1]
    outer_faces(*rest)

    def first_residual(x, v, out, dot):
        residual = rhs[x] - out
        precond = residual * dinv[x]
        rs[x] = residual
        field[x + 1] = precond
        stage_plane(0, x, precond)
        return dot + fold(residual * precond)

    ry_part = apply_all(x0, first_residual, zero, edge_part, first_iterate)
    stage_end(0)

    def tall(row):
        return jnp.broadcast_to(row, (8, 128))

    def one_step(k, carry):
        ry, lines, dots, _, last_alpha = carry
        ry, lines = ry[0:1], [line[0:1] for line in lines]
        sums, parts = coarse_right_side(k)
        gather(
            k + 1,
            message([sums] + [parts[side] for side in (0, 1, 4, 5, 2, 3)], dots),
            lambda: exchange_start(k),
            lambda: exchange_wait(k),
        )
        more = coarse(k + 1)
        d0, d1, d2 = dots_of(k + 1)
        first = lax.broadcasted_iota(jnp.int32, (1, 128), 0) + k == 0
        alpha = jnp.where(first, 0.0, ry / d0)
        ry_next = jnp.where(first, d0, ry + alpha * (alpha * d2 - 2.0 * d1))
        beta = jnp.where(first, 0.0, ry_next / ry)
        gain = jnp.where(first, 1.0, -alpha)
        lines = [line + gain * extra for line, extra in zip(lines, more)]

        x_far, y_own, y_far, z_own, z_far = rim_of(lines)
        for low in range(2):
            outer = cx + 1 if low else 0
            layer = yrim_x[low] + gain * xh[k, low]
            yrim_x[low] = layer
            direction[outer] = (layer + beta * direction[outer]) - x_far[low]
        rows = [ys[k, 0], ys[k, 1], yh[k, 0], yh[k, 1]]
        packs = [zs[k, 0], zs[k, 1], far(zh.at[k], 0), far(zh.at[k], 1)]
        for i, (y_part, z_part) in enumerate(zip(y_own + y_far, z_own + z_far)):
            row = yrim_y[i] + gain * rows[i]
            pack = yrim_z[i] + gain * packs[i]
            yrim_y[i] = row
            yrim_z[i] = pack
            prim_y[i] = (row + beta * prim_y[i]) - y_part
            prim_z[i] = (pack + beta * prim_z[i]) - z_part
        outer_faces(
            [prim_y[0], prim_y[1]],
            [prim_y[2], prim_y[3]],
            [prim_z[0], prim_z[1]],
            [prim_z[2], prim_z[3]],
        )

        def next_direction(x):
            residual = rs[x] - alpha * ws[x]
            rs[x] = residual
            plane = (residual * dinv[x] + beta * direction[x + 1]) - take(lines[6], lab[x])
            direction[x + 1] = plane
            history[k, x] = plane
            return plane

        def image(x, v, out, dots):
            z = out * dinv[x]
            ws[x] = out
            field[x + 1] = z
            stage_plane(k + 1, x, z)
            return (
                dots[0] + fold(v * out),
                dots[1] + fold(rs[x] * z),
                dots[2] + fold(out * z),
            )

        dots = apply_all(direction, image, (zero, zero, zero), edge_part, next_direction)
        stage_end(k + 1)
        return tall(ry_next), [tall(line) for line in lines], dots, last_alpha, tall(alpha)

    ry, _, dots, *alphas = lax.fori_loop(
        0, STEPS, one_step, (zero + 1.0, [zero] * 7, (ry_part, zero, zero), zero, zero)
    )
    ry, alphas = ry[0:1], [alpha[0:1] for alpha in alphas]

    stores = [
        pltpu.make_async_copy(ordered.at[i], out, out_sem.at[i])
        for i, out in enumerate((x_hbm, p_hbm, r_hbm, w_hbm))
    ]
    G1_last[pl.ds(phases[0][0], 1), :] = jnp.sum(dots[0], axis=0, keepdims=True)
    phase_start(STEPS + 1, 0)

    def join_iterate(x, carry):
        joined = (x0[x + 1] + alphas[0] * history[0, x]) + alphas[1] * history[1, x]
        for i, plane in enumerate((joined, history[STEPS - 1, x], rs[x], ws[x])):
            store_in_order(ordered.at[i], x, plane)
        return carry

    lax.fori_loop(0, cx, join_iterate, 0, unroll=4)
    for store in stores:
        store.start()
    phase_wait(STEPS + 1, 0)
    G2_last[pl.ds(phases[1][0], 1), :] = jnp.sum(G1_last[...], axis=0, keepdims=True)
    phase_start(STEPS + 1, 1)
    phase_wait(STEPS + 1, 1)
    total = jnp.sum(jnp.sum(G2_last[...], axis=0, keepdims=True), axis=1, keepdims=True)
    step_out[...] = jnp.broadcast_to(ry / total, step_out.shape)
    for store in stores:
        store.wait()


def solution(mesh):
    nx, ny, nz = mesh.shape["gx"], mesh.shape["gy"], mesh.shape["gz"]

    def per_device(rhs, mobility, labels, coarse_inverse):
        cx, cy, cz = rhs.shape
        hbm = pl.BlockSpec(memory_space=pl.ANY)

        def vmem(*shape, dtype=F32):
            return pltpu.VMEM(shape, dtype)

        i32 = jnp.int32
        xs, p, rs, w, alpha = pl.pallas_call(
            functools.partial(kernel, nx, ny, nz),
            out_shape=[jax.ShapeDtypeStruct(rhs.shape, F32)] * 4
            + [jax.ShapeDtypeStruct((cy, cz), F32)],
            in_specs=[hbm] * 4,
            out_specs=[hbm] * 4 + [pl.BlockSpec(memory_space=pltpu.VMEM)],
            scratch_shapes=[
                *[vmem(cx + 2, cy, cz) for _ in range(4)],
                vmem(STEPS, cx, cy, cz),
                vmem(cx, cy, cz),
                vmem(cx, cy, cz, dtype=i32),
                vmem(cx, cy, cz),
                vmem(cx, cy, cz),
                vmem(cx, cy, cz, dtype=i32),
                vmem(*coarse_inverse.shape),
                vmem(*coarse_inverse.shape),
                vmem(6, *coarse_inverse.shape),
                vmem(cx + 1, cy, cz),
                *[vmem(cx, cy, cz) for _ in range(4)],
                vmem(4, cx, cy, cz),
                vmem(2, cx, cz),
                vmem(2, 8, 128),
                vmem(4, cx, cy, cz),
                *[vmem(cx, cy, cz) for _ in range(2)],
                vmem(STEPS, 2, cy, cz),
                vmem(4, 2, cx, cz),
                vmem(4, 2, cx, cz),
                vmem(4, 2, 8, 128),
                vmem(4, 2, 2, 8, 128),
                vmem(2, cy, cz, dtype=i32),
                vmem(2, cx, cz, dtype=i32),
                vmem(2, cx, cz, dtype=i32),
                vmem(2, 8, 128, dtype=i32),
                vmem(2, 2, 8, 128, dtype=i32),
                vmem(2, 8, 128, dtype=i32),
                vmem(2, cy, cz),
                vmem(4, cx, cz),
                vmem(4, 8, 128),
                vmem(4, cx, cz),
                vmem(4, 8, 128),
                vmem(cx, 8, 128),
                vmem(cx, 8, 128, dtype=i32),
                vmem(cx, 8, 128),
                vmem(2, cx, cz),
                vmem(2 * nx, 128),
                vmem(ny * nz // 2, 2, 128),
                vmem(STEPS, 2 * nx, 128),
                vmem(STEPS, ny * nz // 2, 9, 128),
                vmem(2 * nx, 128),
                vmem(ny * nz // 2, 128),
                pltpu.SemaphoreType.DMA((4,)),
                pltpu.SemaphoreType.DMA((4,)),
                pltpu.SemaphoreType.DMA((6, 6)),
                pltpu.SemaphoreType.DMA((6, 6)),
                pltpu.SemaphoreType.DMA((5, 2)),
                pltpu.SemaphoreType.DMA((5, 2)),
            ],
            compiler_params=pltpu.CompilerParams(
                collective_id=0, has_side_effects=True, vmem_limit_bytes=VMEM_BYTES
            ),
            name="deflated_cg",
        )(rhs, mobility, labels, coarse_inverse)
        return xs + alpha * p, rs - alpha * w

    spec = P("gx", "gz", "gy")
    return jax.shard_map(
        per_device,
        mesh=mesh,
        in_specs=(spec, spec, spec, P(("gx", "gy", "gz"), None)),
        out_specs=(spec, spec),
        check_vma=False,
    )
```

```python
import functools

import jax
import jax.numpy as jnp
from jax import lax
from jax.experimental import pallas as pl
from jax.experimental.pallas import tpu as pltpu
from jax.sharding import PartitionSpec as P

LOGICAL = pl.DeviceIdType.LOGICAL
F32 = jnp.float32
LOOP = 5
VMEM_BYTES = 64 * 1024 * 1024 - 256 * 1024

STEPS = 3
MOB, LAB, INV = range(STEPS, STEPS + 3)


def farthest_first(n):
    return sorted(range(n), key=lambda k: -min(k, n - k))


def kernel(
    nx,
    ny,
    nz,
    rhs_hbm,
    mob_hbm,
    lab_hbm,
    inv_hbm,
    x_hbm,
    p_hbm,
    r_hbm,
    w_hbm,
    step_out,
    mob,
    x0,
    field,
    direction,
    history,
    rhs_in,
    lab_in,
    mob_in,
    rhs,
    lab,
    inv_in,
    inv,
    inv_far,
    fx,
    fy,
    fz,
    dinv,
    rim,
    bits,
    fyb,
    fzp,
    ordered,
    rs,
    ws,
    xh,
    ys,
    yh,
    zs,
    zh,
    lxh,
    lys,
    lyh,
    lzs,
    lzh,
    lzf,
    yrim_x,
    yrim_y,
    yrim_z,
    prim_y,
    prim_z,
    zt,
    lt,
    et,
    ey,
    G1_first,
    G2_first,
    G1,
    G2,
    G1_last,
    G2_last,
    in_sem,
    out_sem,
    hs_sem,
    hr_sem,
    gs_sem,
    gr_sem,
):
    cx = rhs.shape[0]
    gx, gy, gz = lax.axis_index("gx"), lax.axis_index("gy"), lax.axis_index("gz")
    def logical(x, y, z):
        return (lax.rem(x, nx) * ny + lax.rem(y, ny)) * nz + lax.rem(z, nz)

    sides = (
        ("gx", gx > 0, logical(gx + nx - 1, gy, gz)),
        ("gx", gx < nx - 1, logical(gx + 1, gy, gz)),
        ("gz", gz > 0, logical(gx, gy, gz + nz - 1)),
        ("gz", gz < nz - 1, logical(gx, gy, gz + 1)),
        ("gy", gy > 0, logical(gx, gy + ny - 1, gz)),
        ("gy", gy < ny - 1, logical(gx, gy + 1, gz)),
    )

    loads = [
        pltpu.make_async_copy(rhs_hbm, rhs_in, in_sem.at[0]),
        pltpu.make_async_copy(lab_hbm, lab_in, in_sem.at[1]),
        pltpu.make_async_copy(mob_hbm, mob_in, in_sem.at[2]),
        pltpu.make_async_copy(inv_hbm, inv_in, in_sem.at[3]),
    ]
    for load in loads:
        load.start()

    def clear(ref, *index):
        ref[index or Ellipsis] = jnp.zeros(ref.shape[len(index) :], ref.dtype)

    for low in range(2):

        @pl.when(gx == (nx - 1 if low else 0))
        def _():
            clear(mob, cx + 1 if low else 0)
            clear(lxh, low)
            for e in range(STEPS):
                clear(xh, e, low)

        @pl.when(gz == (nz - 1 if low else 0))
        def _():
            clear(lyh, low)
            for e in range(STEPS + 1):
                clear(yh, e, low)

        @pl.when(gy == (ny - 1 if low else 0))
        def _():
            clear(lzh, low)
            for e in range(STEPS + 1):
                clear(zh, e, low)

    barrier = pltpu.get_barrier_semaphore()
    chips = nz // 2
    chip, core = lax.div(gz, 2), lax.rem(gz, 2)
    line_peers = [
        logical(gx + k, gy, 2 * chip + lax.rem(core + c, 2))
        for k in farthest_first(nx)
        for c in (1, 0)
        if k or c
    ]
    plane_peers = [
        logical(gx, gy + j, gz + 2 * k)
        for j in farthest_first(ny)
        for k in farthest_first(chips)
        if j or k
    ]
    phases = ((core * nx + gx, line_peers), (gy * chips + chip, plane_peers))
    partners = line_peers + plane_peers + [logical(gx, gy, gz + nz - 1 + 2 * core)]
    for partner in partners:
        pl.semaphore_signal(barrier, inc=1, device_id=partner, device_id_type=LOGICAL)

    clear(field, 0)
    clear(field, cx + 1)

    lane8 = lax.broadcasted_iota(jnp.int32, (8, 128), 1)
    row8 = lax.broadcasted_iota(jnp.int32, (8, 128), 0)
    lane16 = lax.broadcasted_iota(jnp.int32, (16, 128), 1)
    row16 = lax.broadcasted_iota(jnp.int32, (16, 128), 0)
    pair = ((lane8 + 1) >> 1) & 63
    ends = (lane8 == 0) | (lane8 == 127)
    even = (lane8 & 1) == 0
    zero = jnp.zeros((8, 128), F32)

    def interleaved(ref, x):
        return jnp.concatenate([ref[x, pl.ds(k, 8, stride=8), :] for k in range(8)], axis=0)

    def store_in_order(ref, x, plane):
        for k in range(8):
            ref[x, pl.ds(k, 8, stride=8), :] = plane[8 * k : 8 * k + 8]

    def next_row(plane):
        return jnp.concatenate([plane[8:], pltpu.roll(plane[:8], 7, 0)], axis=0)

    def last_row(plane):
        return jnp.concatenate([pltpu.roll(plane[56:], 1, 0), plane[:56]], axis=0)

    def fold(plane):
        tiles = [plane[k : k + 8] for k in range(0, plane.shape[0], 8)]
        while len(tiles) > 1:
            tiles = [a + b for a, b in zip(tiles[::2], tiles[1::2])]
        return tiles[0]

    def halo_copy(e, side):
        axis, _, index = sides[side]
        low, other = side & 1, 1 - (side & 1)
        kind = e if isinstance(e, int) else 0
        if kind == INV:
            src, dst = inv, inv_far.at[side ^ 1]
        elif kind == LAB:
            if axis == "gx":
                src, dst = lab.at[cx - 1 if low else 0], lxh.at[other]
            elif axis == "gz":
                src, dst = lys.at[low], lyh.at[other]
            else:
                src, dst = lzs, lzh.at[other]
        elif axis == "gx":
            src = (mob if kind == MOB else field).at[cx if low else 1]
            dst = mob.at[0 if low else cx + 1] if kind == MOB else xh.at[e, other]
        elif axis == "gz":
            src, dst = ys.at[e, low], yh.at[e, other]
        else:
            src, dst = zs.at[e], zh.at[e, other]
        return pltpu.make_async_remote_copy(
            src_ref=src,
            dst_ref=dst,
            send_sem=hs_sem.at[e, side],
            recv_sem=hr_sem.at[e, side ^ 1],
            device_id=index,
            device_id_type=LOGICAL,
        )

    def halo_landed(e, side):
        low = side & 1
        kind = e if isinstance(e, int) else 0
        if kind == INV:
            ref = inv_far.at[side]
        elif kind == LAB:
            ref = (lxh, lyh, lzh)[side // 2].at[low]
        elif side < 2:
            ref = mob.at[cx + 1 if low else 0] if kind == MOB else xh.at[e, low]
        else:
            ref = (yh, zh)[side // 2 - 1].at[e, low]
        return pltpu.make_async_copy(ref, ref, hr_sem.at[e, side])

    def exchange_start(e):
        for side in (0, 1, 4, 5, 2, 3):

            @pl.when(sides[side][1])
            def _():
                halo_copy(e, side).start()

    def exchange_wait(e):
        for side in range(6):

            @pl.when(sides[side][1])
            def _():
                halo_landed(e, side).wait()
                halo_copy(e, side).wait_send()

    def stage_rows(rows, x, plane):
        rows[0, pl.ds(x, 1), :] = plane[0:1]
        rows[1, pl.ds(x, 1), :] = plane[63:64]

    def pack_plane(plane):
        packed = plane[0:8]
        for k in range(1, 8):
            packed = jnp.where(pair == k, pltpu.roll(plane[8 * k : 8 * k + 8], 2 * k, 1), packed)
        return jnp.where(pair < 8, packed, jnp.zeros_like(packed))

    def pack_end(tiles, half):
        total = tiles[8 * half]
        for k in range(1, 8):
            total = total + pltpu.roll(tiles[8 * half + k], 16 * k, 1)
        return total

    def stage_plane(e, x, plane):
        stage_rows(ys.at[e], x, plane)
        zt[x] = pack_plane(plane)

    def stage_end(e):
        for half in range(2):
            zs[e, half] = pack_end(zt, half)

    def far(received, half):
        return jnp.where(
            even, pltpu.roll(received[0, half], 1, 1), pltpu.roll(received[1, half], 127, 1)
        )

    def spread(packed, half):
        et[8 * half] = packed
        for k in range(1, 8):
            et[8 * half + k] = pltpu.roll(packed, 128 - 16 * k, 1)

    def edge_part(x, v):
        return edge_tiles(x)

    def edge_tiles(x):
        tile = et[x]
        tiles = [
            jnp.where(ends, tile if k == 0 else pltpu.roll(tile, 128 - 2 * k, 1), 0.0)
            for k in range(8)
        ]
        first, last = ey[0, pl.ds(x, 1), :], ey[1, pl.ds(x, 1), :]
        tiles[0] = tiles[0] + jnp.where(row8 == 0, first, 0.0)
        tiles[7] = tiles[7] + jnp.where(row8 == 7, last, 0.0)
        return jnp.concatenate(tiles, axis=0)

    def apply_all(values, body, init, outer, make=None):
        def step(x, carry, above_v):
            below, v, rest = carry
            above = fx[x + 1] * (above_v - v)
            flux_y = fy[x] * (next_row(v) - v)
            flux_z = fz[x] * (pltpu.roll(v, 127, 1) - v)
            out = (
                (below - above)
                + (last_row(flux_y) - flux_y)
                + (pltpu.roll(flux_z, 1, 1) - flux_z)
                + outer(x, v)
            )
            return above, above_v, body(x, v, out, rest)

        if make is None:

            def make(x):
                return values[x + 1]

        v = make(0)
        carry = (fx[0] * (v - values[0]), v, init)
        carry = lax.fori_loop(
            0, cx - 1, lambda x, c: step(x, c, make(x + 1)), carry, unroll=LOOP
        )
        return step(cx - 1, carry, values[cx + 1])[2]

    def subset_sums(values, bits):
        terms = [values]
        for bit in bits:
            terms = terms + [term * bit for term in terms]
        return [fold(term) for term in terms]

    def label_sums(sums):
        sums = list(sums)
        for i in range(4):
            for value in range(16):
                if not value >> i & 1:
                    sums[value] = sums[value] - sums[value | 1 << i]
        return sums

    def bits_of(labels):
        return [((labels >> i) & 1).astype(F32) for i in range(4)]

    def by_label(labels, values):
        return label_sums(subset_sums(values, bits_of(labels)))

    def restrict_plane(x, plane, sums):
        more = subset_sums(plane, [bits[i, x] for i in range(4)])
        return tuple(total + extra for total, extra in zip(sums, more))

    def restrict_rhs(x, sums):
        labels = interleaved(lab_in, x)
        values = interleaved(rhs_in, x)
        lab[x] = labels
        rhs[x] = values
        planes = bits_of(labels)
        for i in range(4):
            bits[i, x] = planes[i]
        return tuple(total + extra for total, extra in zip(sums, subset_sums(values, planes)))

    no_sums = (zero,) * 16

    def rows_of(tiles):
        for shift in (4, 2, 1):
            low = (row8 & shift) == 0
            half = len(tiles) // 2
            merged = []
            for a, b in zip(tiles[:half], tiles[half:]):
                kept, moved = jnp.where(low, a, b), jnp.where(low, b, a)
                if shift == 4:
                    moved = pltpu.roll(moved, 4, 0)
                else:
                    moved = jnp.where(
                        low, pltpu.roll(moved, 8 - shift, 0), pltpu.roll(moved, shift, 0)
                    )
                merged.append(kept + moved)
            tiles = merged
        return tiles[0]

    def message(groups, dots):
        tiles = []
        for sums in groups:
            tiles += [rows_of(list(sums[:8])), rows_of(list(sums[8:]))]
        if dots:
            tiles.append(rows_of(list(dots) + [zero] * (8 - len(dots))))
        line = zero
        for k, tile in enumerate(tiles):
            column = jnp.sum(tile, axis=1, keepdims=True)
            line = line + jnp.where(lane8 == 8 * k + row8, column, 0.0)
        return jnp.sum(line, axis=0, keepdims=True)

    def transpose_groups(tile):
        for s in (4, 2, 1):
            group = (lane8 >> 4) & s
            up = pltpu.roll(pltpu.roll(tile, 8 - s, 0), 16 * s, 1)
            down = pltpu.roll(pltpu.roll(tile, s, 0), 128 - 16 * s, 1)
            tile = jnp.where((row8 & s) == group, tile, jnp.where(group != 0, up, down))
        return tile

    def neighbour_parts(e):
        parts = [
            by_label(lxh[0], -(fx[0] * field[1])),
            by_label(lxh[1], -(fx[cx] * field[cx])),
        ]
        for low in range(2):
            parts.append(by_label(lyh[low], -(fyb[low] * ys[e, low])))
        for keep in (even, ~even):
            halves = [
                by_label(lzf[half], jnp.where(keep, -(fzp[half] * zs[e, half]), 0.0))
                for half in range(2)
            ]
            parts.append([a + b for a, b in zip(*halves)])
        return parts

    def coarse_right_side(e):
        sums = apply_all(
            field, lambda x, v, out, s: restrict_plane(x, out, s), no_sums, lambda x, v: rim[x] * v
        )
        return label_sums(sums), neighbour_parts(e)

    def slots_of(g, ph):
        if isinstance(g, int):
            return ((G1_first, G2_first), (G1_last, G2_last))[g != 0][ph]
        return (G1, G2)[ph].at[g - 1]

    def phase_slots(g, ph, first, count):
        slots = slots_of(g, ph)
        return slots.at[pl.ds(first, count)]

    def phase_start(g, ph):
        me, peers = phases[ph]
        slot = phase_slots(g, ph, me, 1)
        for peer in peers:
            pltpu.make_async_remote_copy(
                src_ref=slot,
                dst_ref=slot,
                send_sem=gs_sem.at[g, ph],
                recv_sem=gr_sem.at[g, ph],
                device_id=peer,
                device_id_type=LOGICAL,
            ).start()

    def phase_wait(g, ph):
        part = phase_slots(g, ph, 0, len(phases[ph][1]))
        pltpu.make_async_copy(part, part, gr_sem.at[g, ph]).wait()
        pltpu.make_async_copy(part, part, gs_sem.at[g, ph]).wait()

    def group_lines(slots):
        return [transpose_groups(slots[nx * c : nx * (c + 1)]) for c in range(2)]

    def gather(g, line, started, between):
        G1[g - 1, pl.ds(phases[0][0], 1), :] = line
        phase_start(g, 0)
        started()
        phase_wait(g, 0)
        tiles = group_lines(G1.at[g - 1])

        def pick(group):
            return jnp.concatenate([tile[group : group + 1] for tile in tiles], axis=0)

        lane2 = lax.broadcasted_iota(jnp.int32, (2, 128), 1)
        own = pick(0)
        own = own + jnp.where(lane2 < 112, pltpu.roll(pick(1), 112, 1), 0.0)
        own = own + jnp.where(lane2 >= 16, pltpu.roll(pick(2), 16, 1), 0.0)
        own = own + jnp.concatenate([tiles[1][5:6], tiles[0][6:7]], axis=0)
        slot = phases[1][0]
        G2[g - 1, slot, 0:2] = own
        G2[g - 1, slot, 2:4] = pick(3)
        G2[g - 1, slot, 4:6] = pick(4)
        G2[g - 1, slot, 6:7] = tiles[0][5:6]
        G2[g - 1, slot, 7:8] = tiles[1][6:7]
        G2[g - 1, slot, 8:9] = tiles[0][7:8] + tiles[1][7:8]
        phase_start(g, 1)
        between()
        phase_wait(g, 1)

    def dots_of(g):
        row = jnp.sum(G2[g - 1, :, 8:9], axis=0)
        lane = lax.broadcasted_iota(jnp.int32, (1, 128), 1)
        return [
            jnp.broadcast_to(
                jnp.sum(jnp.where(lane & 15 == k, row, 0.0), axis=1, keepdims=True), (1, 128)
            )
            for k in range(3)
        ]

    def right_side(g):
        rows = [[None] * ny for _ in range(nz)]
        for j in range(ny):
            for k in range(chips):
                slot = j * chips + k
                if isinstance(g, int):
                    pairs = G2_first[slot]
                    low, high = pairs[0:1], pairs[1:2]
                else:
                    pairs = G2[g - 1, slot, 0:2]
                    if j + 1 < ny:
                        pairs = pairs + G2[g - 1, slot + chips, 2:4]
                    if j > 0:
                        pairs = pairs + G2[g - 1, slot - chips, 4:6]
                    low, high = pairs[0:1], pairs[1:2]
                    if k > 0:
                        low = low + G2[g - 1, slot - 1, 7:8]
                    if k + 1 < chips:
                        high = high + G2[g - 1, slot + 1, 6:7]
                rows[2 * k][j], rows[2 * k + 1][j] = low, high
        return rows

    def coarse(g):
        accs = [jnp.zeros((16, 128), F32) for _ in range(7)]
        for i, rows in enumerate(right_side(g)):
            for j in range(ny):
                columns = slice((i * ny + j) * 128, (i * ny + j + 1) * 128)
                row = rows[j]
                accs[6] = accs[6] + inv[:, columns] * row
                for side in range(6):
                    accs[side] = accs[side] + inv_far[side, :, columns] * row
        values = []
        for side in range(7):
            total = jnp.broadcast_to(jnp.sum(accs[side], axis=1, keepdims=True), (16, 128))
            if side < 6:
                index = row16 * 0 + (gx, gz, gy)[side // 2]
                edge = (0, (nx, nz, ny)[side // 2] - 1)[side & 1]
                total = jnp.where(index == edge, 0.0, total)
            values.append(total)
        return values

    def take(values, masks):
        picked = [jnp.broadcast_to(values[m : m + 1], masks[0].shape) for m in range(16)]
        for mask in masks:
            picked = [jnp.where(mask, b, a) for a, b in zip(picked[::2], picked[1::2])]
        return picked[0]

    def masks_of(labels):
        return [labels & (1 << i) != 0 for i in range(4)]

    def take_plane(values, x):
        return take(values, [bits[i, x] > 0.5 for i in range(4)])

    def rim_of(values):
        x_far = [take(values[low], masks_of(lxh[low])) for low in range(2)]
        y_own = [take(values[6], masks_of(lys[low])) for low in range(2)]
        y_far = [take(values[2 + low], masks_of(lyh[low])) for low in range(2)]
        z_own = [take(values[6], masks_of(lzs[half])) for half in range(2)]
        z_far = []
        for half in range(2):
            masks = masks_of(lzf[half])
            z_far.append(jnp.where(even, take(values[4], masks), take(values[5], masks)))
        return x_far, y_own, y_far, z_own, z_far

    def outer_faces(y_own, y_far, z_own, z_far):
        for low in range(2):
            ey[low] = fyb[low] * (y_own[low] - y_far[low])
        for half in range(2):
            spread(fzp[half] * (z_own[half] - z_far[half]), half)

    loads[0].wait()
    loads[1].wait()
    sums = lax.fori_loop(0, cx, restrict_rhs, no_sums, unroll=4)
    line = message([label_sums(sums)], ())
    pl.semaphore_wait(barrier, len(partners))
    G1_first[pl.ds(phases[0][0], 1), :] = line
    phase_start(0, 0)
    loads[2].wait()

    def order_columns():
        for top in (0, 8):
            for j in range(ny):
                tiles = [inv_in[top : top + 8, pl.ds((i * ny + j) * 128, 128)] for i in range(nx)]
                for s in (4, 2, 1):
                    clear_bit = (lane8 >> 4) & s == 0
                    for i in range(nx):
                        if not i & s:
                            a, b = tiles[i], tiles[i | s]
                            tiles[i] = jnp.where(clear_bit, a, pltpu.roll(b, 16 * s, 1))
                            tiles[i | s] = jnp.where(clear_bit, pltpu.roll(a, 128 - 16 * s, 1), b)
                for i in range(nz):
                    inv[top : top + 8, pl.ds((i * ny + j) * 128, 128)] = tiles[i]

    def stage_static(x, carry):
        mobility = interleaved(mob_in, x)
        mob[x + 1] = mobility
        stage_plane(MOB, x, mobility)
        labels = lab[x]
        stage_rows(lys, x, labels)
        lt[x] = pack_plane(labels)
        return carry

    lax.fori_loop(0, cx, stage_static, 0, unroll=4)
    stage_end(MOB)
    for half in range(2):
        lzs[half] = pack_end(lt, half)
    exchange_start(MOB)
    exchange_start(LAB)
    loads[3].wait()
    order_columns()
    exchange_start(INV)

    def faces():
        for ref in (direction, ws, yrim_x, yrim_y, yrim_z, prim_y, prim_z):
            clear(ref)
        exchange_wait(MOB)
        exchange_wait(LAB)
        for half in range(2):
            lzf[half] = far(lzh, half)
            fzp[half] = 0.5 * (zs[MOB, half] + far(zh.at[MOB], half))
            spread(fzp[half], half)
        for low in range(2):
            fyb[low] = 0.5 * (ys[MOB, low] + yh[MOB, low])
            ey[low] = fyb[low]
        fx[0] = 0.5 * (mob[1] + mob[0])
        row = lax.broadcasted_iota(jnp.int32, (64, 128), 0)
        lane = lax.broadcasted_iota(jnp.int32, (64, 128), 1)

        def step(x, below):
            m = mob[x + 1]
            above = 0.5 * (mob[x + 2] + m)
            face_y = jnp.where(row == 63, 0.0, 0.5 * (next_row(m) + m))
            face_z = jnp.where(lane == 127, 0.0, 0.5 * (pltpu.roll(m, 127, 1) + m))
            edges = edge_tiles(x)
            diag = (
                (below + above)
                + (last_row(face_y) + face_y)
                + (pltpu.roll(face_z, 1, 1) + face_z)
                + edges
            )
            rim[x] = edges
            fx[x + 1] = above
            fy[x] = face_y
            fz[x] = face_z
            dinv[x] = 1.0 / diag
            return above

        lax.fori_loop(0, cx, step, fx[0], unroll=4)

    phase_wait(0, 0)
    G2_first[phases[1][0]] = jnp.concatenate(
        [tile[0:1] for tile in group_lines(G1_first)], axis=0
    )
    phase_start(0, 1)
    faces()
    phase_wait(0, 1)

    exchange_wait(INV)
    lines = coarse(0)

    def first_iterate(x):
        plane = take_plane(lines[6], x)
        x0[x + 1] = plane
        return plane

    x_far, *rest = rim_of(lines)
    x0[0] = x_far[0]
    x0[cx + 1] = x_far[1]
    outer_faces(*rest)

    def first_residual(x, v, out, dot):
        residual = rhs[x] - out
        precond = residual * dinv[x]
        rs[x] = residual
        field[x + 1] = precond
        stage_plane(0, x, precond)
        return dot + fold(residual * precond)

    ry_part = apply_all(x0, first_residual, zero, edge_part, first_iterate)
    stage_end(0)

    def tall(row):
        return jnp.broadcast_to(row, (8, 128))

    def one_step(k, carry):
        ry, lines, dots, _, last_alpha = carry
        ry = ry[0:1]
        sums, parts = coarse_right_side(k)
        gather(
            k + 1,
            message([sums] + [parts[side] for side in (0, 1, 4, 5, 2, 3)], dots),
            lambda: exchange_start(k),
            lambda: exchange_wait(k),
        )
        more = coarse(k + 1)
        d0, d1, d2 = dots_of(k + 1)
        first = lax.broadcasted_iota(jnp.int32, (1, 128), 0) + k == 0
        alpha = jnp.where(first, 0.0, ry / d0)
        ry_next = jnp.where(first, d0, ry + alpha * (alpha * d2 - 2.0 * d1))
        beta = jnp.where(first, 0.0, ry_next / ry)
        gain = jnp.where(first, 1.0, -alpha)
        lines = [line + gain * extra for line, extra in zip(lines, more)]

        x_far, y_own, y_far, z_own, z_far = rim_of(lines)
        for low in range(2):
            outer = cx + 1 if low else 0
            layer = yrim_x[low] + gain * xh[k, low]
            yrim_x[low] = layer
            direction[outer] = (layer + beta * direction[outer]) - x_far[low]
        rows = [ys[k, 0], ys[k, 1], yh[k, 0], yh[k, 1]]
        packs = [zs[k, 0], zs[k, 1], far(zh.at[k], 0), far(zh.at[k], 1)]
        for i, (y_part, z_part) in enumerate(zip(y_own + y_far, z_own + z_far)):
            row = yrim_y[i] + gain * rows[i]
            pack = yrim_z[i] + gain * packs[i]
            yrim_y[i] = row
            yrim_z[i] = pack
            prim_y[i] = (row + beta * prim_y[i]) - y_part
            prim_z[i] = (pack + beta * prim_z[i]) - z_part
        outer_faces(
            [prim_y[0], prim_y[1]],
            [prim_y[2], prim_y[3]],
            [prim_z[0], prim_z[1]],
            [prim_z[2], prim_z[3]],
        )

        def next_direction(x):
            residual = rs[x] - alpha * ws[x]
            rs[x] = residual
            plane = (residual * dinv[x] + beta * direction[x + 1]) - take_plane(lines[6], x)
            direction[x + 1] = plane
            history[k, x] = plane
            return plane

        def image(x, v, out, dots):
            z = out * dinv[x]
            ws[x] = out
            field[x + 1] = z
            stage_plane(k + 1, x, z)
            return (
                dots[0] + fold(v * out),
                dots[1] + fold(rs[x] * z),
                dots[2] + fold(out * z),
            )

        dots = apply_all(direction, image, (zero, zero, zero), edge_part, next_direction)
        stage_end(k + 1)
        return tall(ry_next), lines, dots, last_alpha, tall(alpha)

    ry, _, dots, *alphas = lax.fori_loop(
        0, STEPS, one_step, (zero + 1.0, [jnp.zeros((16, 128), F32)] * 7, (ry_part, zero, zero), zero, zero)
    )
    ry, alphas = ry[0:1], [alpha[0:1] for alpha in alphas]

    stores = [
        pltpu.make_async_copy(ordered.at[i], out, out_sem.at[i])
        for i, out in enumerate((x_hbm, p_hbm, r_hbm, w_hbm))
    ]
    G1_last[pl.ds(phases[0][0], 1), :] = jnp.sum(dots[0], axis=0, keepdims=True)
    phase_start(STEPS + 1, 0)

    def join_iterate(x, carry):
        joined = (x0[x + 1] + alphas[0] * history[0, x]) + alphas[1] * history[1, x]
        for i, plane in enumerate((joined, history[STEPS - 1, x], rs[x], ws[x])):
            store_in_order(ordered.at[i], x, plane)
        return carry

    lax.fori_loop(0, cx, join_iterate, 0, unroll=4)
    for store in stores:
        store.start()
    phase_wait(STEPS + 1, 0)
    G2_last[pl.ds(phases[1][0], 1), :] = jnp.sum(G1_last[...], axis=0, keepdims=True)
    phase_start(STEPS + 1, 1)
    phase_wait(STEPS + 1, 1)
    total = jnp.sum(jnp.sum(G2_last[...], axis=0, keepdims=True), axis=1, keepdims=True)
    step_out[...] = jnp.broadcast_to(ry / total, step_out.shape)
    for store in stores:
        store.wait()


def solution(mesh):
    nx, ny, nz = mesh.shape["gx"], mesh.shape["gy"], mesh.shape["gz"]

    def per_device(rhs, mobility, labels, coarse_inverse):
        cx, cy, cz = rhs.shape
        hbm = pl.BlockSpec(memory_space=pl.ANY)

        def vmem(*shape, dtype=F32):
            return pltpu.VMEM(shape, dtype)

        i32 = jnp.int32
        xs, p, rs, w, alpha = pl.pallas_call(
            functools.partial(kernel, nx, ny, nz),
            out_shape=[jax.ShapeDtypeStruct(rhs.shape, F32)] * 4
            + [jax.ShapeDtypeStruct((cy, cz), F32)],
            in_specs=[hbm] * 4,
            out_specs=[hbm] * 4 + [pl.BlockSpec(memory_space=pltpu.VMEM)],
            scratch_shapes=[
                *[vmem(cx + 2, cy, cz) for _ in range(4)],
                vmem(STEPS, cx, cy, cz),
                vmem(cx, cy, cz),
                vmem(cx, cy, cz, dtype=i32),
                vmem(cx, cy, cz),
                vmem(cx, cy, cz),
                vmem(cx, cy, cz, dtype=i32),
                vmem(*coarse_inverse.shape),
                vmem(*coarse_inverse.shape),
                vmem(6, *coarse_inverse.shape),
                vmem(cx + 1, cy, cz),
                *[vmem(cx, cy, cz) for _ in range(4)],
                vmem(4, cx, cy, cz),
                vmem(2, cx, cz),
                vmem(2, 8, 128),
                vmem(4, cx, cy, cz),
                *[vmem(cx, cy, cz) for _ in range(2)],
                vmem(STEPS, 2, cy, cz),
                vmem(4, 2, cx, cz),
                vmem(4, 2, cx, cz),
                vmem(4, 2, 8, 128),
                vmem(4, 2, 2, 8, 128),
                vmem(2, cy, cz, dtype=i32),
                vmem(2, cx, cz, dtype=i32),
                vmem(2, cx, cz, dtype=i32),
                vmem(2, 8, 128, dtype=i32),
                vmem(2, 2, 8, 128, dtype=i32),
                vmem(2, 8, 128, dtype=i32),
                vmem(2, cy, cz),
                vmem(4, cx, cz),
                vmem(4, 8, 128),
                vmem(4, cx, cz),
                vmem(4, 8, 128),
                vmem(cx, 8, 128),
                vmem(cx, 8, 128, dtype=i32),
                vmem(cx, 8, 128),
                vmem(2, cx, cz),
                vmem(2 * nx, 128),
                vmem(ny * nz // 2, 2, 128),
                vmem(STEPS, 2 * nx, 128),
                vmem(STEPS, ny * nz // 2, 9, 128),
                vmem(2 * nx, 128),
                vmem(ny * nz // 2, 128),
                pltpu.SemaphoreType.DMA((4,)),
                pltpu.SemaphoreType.DMA((4,)),
                pltpu.SemaphoreType.DMA((6, 6)),
                pltpu.SemaphoreType.DMA((6, 6)),
                pltpu.SemaphoreType.DMA((5, 2)),
                pltpu.SemaphoreType.DMA((5, 2)),
            ],
            compiler_params=pltpu.CompilerParams(
                collective_id=0, has_side_effects=True, vmem_limit_bytes=VMEM_BYTES
            ),
            name="deflated_cg",
        )(rhs, mobility, labels, coarse_inverse)
        return xs + alpha * p, rs - alpha * w

    spec = P("gx", "gz", "gy")
    return jax.shard_map(
        per_device,
        mesh=mesh,
        in_specs=(spec, spec, spec, P(("gx", "gy", "gz"), None)),
        out_specs=(spec, spec),
        check_vma=False,
    )
```

```python
import functools

import jax
import jax.numpy as jnp
from jax import lax
from jax.experimental import pallas as pl
from jax.experimental.pallas import tpu as pltpu
from jax.sharding import PartitionSpec as P

LOGICAL = pl.DeviceIdType.LOGICAL
F32 = jnp.float32
LOOP = 5
VMEM_BYTES = 64 * 1024 * 1024 - 256 * 1024

STEPS = 3
MOB, LAB, INV = range(STEPS, STEPS + 3)


def farthest_first(n):
    return sorted(range(n), key=lambda k: -min(k, n - k))


def kernel(
    nx,
    ny,
    nz,
    rhs_hbm,
    mob_hbm,
    lab_hbm,
    inv_hbm,
    x_hbm,
    p_hbm,
    r_hbm,
    w_hbm,
    step_out,
    mob,
    x0,
    field,
    direction,
    history,
    rhs_in,
    lab_in,
    mob_in,
    rhs,
    lab,
    inv_in,
    inv,
    inv_far,
    fx,
    fy,
    fz,
    dinv,
    rim,
    bits,
    fyb,
    fzp,
    ordered,
    rs,
    ws,
    xh,
    ys,
    yh,
    zs,
    zh,
    lxh,
    lys,
    lyh,
    lzs,
    lzh,
    lzf,
    yrim_x,
    yrim_y,
    yrim_z,
    prim_y,
    prim_z,
    zt,
    lt,
    et,
    ey,
    G1_first,
    G2_first,
    G1,
    G2,
    G1_last,
    G2_last,
    in_sem,
    out_sem,
    hs_sem,
    hr_sem,
    gs_sem,
    gr_sem,
):
    cx = rhs.shape[0]
    gx, gy, gz = lax.axis_index("gx"), lax.axis_index("gy"), lax.axis_index("gz")
    def logical(x, y, z):
        return (lax.rem(x, nx) * ny + lax.rem(y, ny)) * nz + lax.rem(z, nz)

    sides = (
        ("gx", gx > 0, logical(gx + nx - 1, gy, gz)),
        ("gx", gx < nx - 1, logical(gx + 1, gy, gz)),
        ("gz", gz > 0, logical(gx, gy, gz + nz - 1)),
        ("gz", gz < nz - 1, logical(gx, gy, gz + 1)),
        ("gy", gy > 0, logical(gx, gy + ny - 1, gz)),
        ("gy", gy < ny - 1, logical(gx, gy + 1, gz)),
    )

    loads = [
        pltpu.make_async_copy(rhs_hbm, rhs_in, in_sem.at[0]),
        pltpu.make_async_copy(lab_hbm, lab_in, in_sem.at[1]),
        pltpu.make_async_copy(mob_hbm, mob_in, in_sem.at[2]),
        pltpu.make_async_copy(inv_hbm, inv_in, in_sem.at[3]),
    ]
    for load in loads:
        load.start()

    def clear(ref, *index):
        ref[index or Ellipsis] = jnp.zeros(ref.shape[len(index) :], ref.dtype)

    for low in range(2):

        @pl.when(gx == (nx - 1 if low else 0))
        def _():
            clear(mob, cx + 1 if low else 0)
            clear(lxh, low)
            for e in range(STEPS):
                clear(xh, e, low)

        @pl.when(gz == (nz - 1 if low else 0))
        def _():
            clear(lyh, low)
            for e in range(STEPS + 1):
                clear(yh, e, low)

        @pl.when(gy == (ny - 1 if low else 0))
        def _():
            clear(lzh, low)
            for e in range(STEPS + 1):
                clear(zh, e, low)

    barrier = pltpu.get_barrier_semaphore()
    chips = nz // 2
    chip, core = lax.div(gz, 2), lax.rem(gz, 2)
    line_peers = [
        logical(gx + k, gy, 2 * chip + lax.rem(core + c, 2))
        for k in farthest_first(nx)
        for c in (1, 0)
        if k or c
    ]
    plane_peers = [
        logical(gx, gy + j, gz + 2 * k)
        for j in farthest_first(ny)
        for k in farthest_first(chips)
        if j or k
    ]
    phases = ((core * nx + gx, line_peers), (gy * chips + chip, plane_peers))
    partners = line_peers + plane_peers + [logical(gx, gy, gz + nz - 1 + 2 * core)]
    for partner in partners:
        pl.semaphore_signal(barrier, inc=1, device_id=partner, device_id_type=LOGICAL)

    clear(field, 0)
    clear(field, cx + 1)

    lane8 = lax.broadcasted_iota(jnp.int32, (8, 128), 1)
    row8 = lax.broadcasted_iota(jnp.int32, (8, 128), 0)
    lane16 = lax.broadcasted_iota(jnp.int32, (16, 128), 1)
    row16 = lax.broadcasted_iota(jnp.int32, (16, 128), 0)
    pair = ((lane8 + 1) >> 1) & 63
    ends = (lane8 == 0) | (lane8 == 127)
    even = (lane8 & 1) == 0
    zero = jnp.zeros((8, 128), F32)

    def interleaved(ref, x):
        return jnp.concatenate([ref[x, pl.ds(k, 8, stride=8), :] for k in range(8)], axis=0)

    def store_in_order(ref, x, plane):
        for k in range(8):
            ref[x, pl.ds(k, 8, stride=8), :] = plane[8 * k : 8 * k + 8]

    def next_row(plane):
        return jnp.concatenate([plane[8:], pltpu.roll(plane[:8], 7, 0)], axis=0)

    def last_row(plane):
        return jnp.concatenate([pltpu.roll(plane[56:], 1, 0), plane[:56]], axis=0)

    def fold(plane):
        tiles = [plane[k : k + 8] for k in range(0, plane.shape[0], 8)]
        while len(tiles) > 1:
            tiles = [a + b for a, b in zip(tiles[::2], tiles[1::2])]
        return tiles[0]

    def halo_copy(e, side):
        axis, _, index = sides[side]
        low, other = side & 1, 1 - (side & 1)
        kind = e if isinstance(e, int) else 0
        if kind == INV:
            src, dst = inv, inv_far.at[side ^ 1]
        elif kind == LAB:
            if axis == "gx":
                src, dst = lab.at[cx - 1 if low else 0], lxh.at[other]
            elif axis == "gz":
                src, dst = lys.at[low], lyh.at[other]
            else:
                src, dst = lzs, lzh.at[other]
        elif axis == "gx":
            src = (mob if kind == MOB else field).at[cx if low else 1]
            dst = mob.at[0 if low else cx + 1] if kind == MOB else xh.at[e, other]
        elif axis == "gz":
            src, dst = ys.at[e, low], yh.at[e, other]
        else:
            src, dst = zs.at[e], zh.at[e, other]
        return pltpu.make_async_remote_copy(
            src_ref=src,
            dst_ref=dst,
            send_sem=hs_sem.at[e, side],
            recv_sem=hr_sem.at[e, side ^ 1],
            device_id=index,
            device_id_type=LOGICAL,
        )

    def halo_landed(e, side):
        low = side & 1
        kind = e if isinstance(e, int) else 0
        if kind == INV:
            ref = inv_far.at[side]
        elif kind == LAB:
            ref = (lxh, lyh, lzh)[side // 2].at[low]
        elif side < 2:
            ref = mob.at[cx + 1 if low else 0] if kind == MOB else xh.at[e, low]
        else:
            ref = (yh, zh)[side // 2 - 1].at[e, low]
        return pltpu.make_async_copy(ref, ref, hr_sem.at[e, side])

    def exchange_start(e):
        for side in (0, 1, 4, 5, 2, 3):

            @pl.when(sides[side][1])
            def _():
                halo_copy(e, side).start()

    def exchange_wait(e):
        for side in range(6):

            @pl.when(sides[side][1])
            def _():
                halo_landed(e, side).wait()
                halo_copy(e, side).wait_send()

    def stage_rows(rows, x, plane):
        rows[0, pl.ds(x, 1), :] = plane[0:1]
        rows[1, pl.ds(x, 1), :] = plane[63:64]

    def pack_plane(plane):
        packed = plane[0:8]
        for k in range(1, 8):
            packed = jnp.where(pair == k, pltpu.roll(plane[8 * k : 8 * k + 8], 2 * k, 1), packed)
        return jnp.where(pair < 8, packed, jnp.zeros_like(packed))

    def pack_end(tiles, half):
        total = tiles[8 * half]
        for k in range(1, 8):
            total = total + pltpu.roll(tiles[8 * half + k], 16 * k, 1)
        return total

    def stage_plane(e, x, plane):
        stage_rows(ys.at[e], x, plane)
        zt[x] = pack_plane(plane)

    def stage_end(e):
        for half in range(2):
            zs[e, half] = pack_end(zt, half)

    def far(received, half):
        return jnp.where(
            even, pltpu.roll(received[0, half], 1, 1), pltpu.roll(received[1, half], 127, 1)
        )

    def spread(packed, half):
        et[8 * half] = packed
        for k in range(1, 8):
            et[8 * half + k] = pltpu.roll(packed, 128 - 16 * k, 1)

    def edge_part(x, v):
        return edge_tiles(x)

    def edge_tiles(x):
        tile = et[x]
        tiles = [
            jnp.where(ends, tile if k == 0 else pltpu.roll(tile, 128 - 2 * k, 1), 0.0)
            for k in range(8)
        ]
        first, last = ey[0, pl.ds(x, 1), :], ey[1, pl.ds(x, 1), :]
        tiles[0] = tiles[0] + jnp.where(row8 == 0, first, 0.0)
        tiles[7] = tiles[7] + jnp.where(row8 == 7, last, 0.0)
        return jnp.concatenate(tiles, axis=0)

    def apply_all(values, body, init, outer, make=None):
        def step(x, carry, above_v):
            below, v, rest = carry
            above = fx[x + 1] * (above_v - v)
            flux_y = fy[x] * (next_row(v) - v)
            flux_z = fz[x] * (pltpu.roll(v, 127, 1) - v)
            out = (
                (below - above)
                + (last_row(flux_y) - flux_y)
                + (pltpu.roll(flux_z, 1, 1) - flux_z)
                + outer(x, v)
            )
            return above, above_v, body(x, v, out, rest)

        if make is None:

            def make(x):
                return values[x + 1]

        v = make(0)
        carry = (fx[0] * (v - values[0]), v, init)
        carry = lax.fori_loop(
            0, cx - 1, lambda x, c: step(x, c, make(x + 1)), carry, unroll=LOOP
        )
        return step(cx - 1, carry, values[cx + 1])[2]

    def subset_sums(values, bits):
        terms = [values]
        for bit in bits:
            terms = terms + [term * bit for term in terms]
        return [fold(term) for term in terms]

    def label_sums(sums):
        sums = list(sums)
        for i in range(4):
            for value in range(16):
                if not value >> i & 1:
                    sums[value] = sums[value] - sums[value | 1 << i]
        return sums

    def bits_of(labels):
        return [((labels >> i) & 1).astype(F32) for i in range(4)]

    def by_label(labels, values):
        return label_sums(subset_sums(values, bits_of(labels)))

    def restrict_plane(x, plane, sums):
        more = subset_sums(plane, [bits[i, x] for i in range(4)])
        return tuple(total + extra for total, extra in zip(sums, more))

    def restrict_rhs(x, sums):
        labels = interleaved(lab_in, x)
        values = interleaved(rhs_in, x)
        lab[x] = labels
        rhs[x] = values
        planes = bits_of(labels)
        for i in range(4):
            bits[i, x] = planes[i]
        return tuple(total + extra for total, extra in zip(sums, subset_sums(values, planes)))

    no_sums = (zero,) * 16

    def rows_of(tiles):
        for shift in (4, 2, 1):
            low = (row8 & shift) == 0
            half = len(tiles) // 2
            merged = []
            for a, b in zip(tiles[:half], tiles[half:]):
                kept, moved = jnp.where(low, a, b), jnp.where(low, b, a)
                if shift == 4:
                    moved = pltpu.roll(moved, 4, 0)
                else:
                    moved = jnp.where(
                        low, pltpu.roll(moved, 8 - shift, 0), pltpu.roll(moved, shift, 0)
                    )
                merged.append(kept + moved)
            tiles = merged
        return tiles[0]

    def placed(sums, block):
        rows = jnp.concatenate([rows_of(list(sums[:8])), rows_of(list(sums[8:]))], axis=0)
        column = jnp.sum(rows, axis=1, keepdims=True)
        return fold(jnp.where(lane16 == 16 * block + row16, column, 0.0))

    def message(sums, parts, dots):
        tiles = [placed(sums, gx) + placed(parts[0], gx - 1) + placed(parts[1], gx + 1)]
        for side in (4, 5, 2, 3):
            tiles.append(placed(parts[side], gx))
        joined = zero
        for k, dot in enumerate(dots):
            dot = dot + pltpu.roll(dot, 64, 1)
            joined = jnp.where(lane8 >> 5 == k, dot + pltpu.roll(dot, 32, 1), joined)
        return rows_of(tiles + [joined, zero, zero])[:6]

    def neighbour_parts(e):
        parts = [
            by_label(lxh[0], -(fx[0] * field[1])),
            by_label(lxh[1], -(fx[cx] * field[cx])),
        ]
        for low in range(2):
            parts.append(by_label(lyh[low], -(fyb[low] * ys[e, low])))
        for keep in (even, ~even):
            halves = [
                by_label(lzf[half], jnp.where(keep, -(fzp[half] * zs[e, half]), 0.0))
                for half in range(2)
            ]
            parts.append([a + b for a, b in zip(*halves)])
        return parts

    def coarse_right_side(e):
        sums = apply_all(
            field, lambda x, v, out, s: restrict_plane(x, out, s), no_sums, lambda x, v: rim[x] * v
        )
        return label_sums(sums), neighbour_parts(e)

    def slots_of(g, ph):
        if isinstance(g, int):
            return ((G1_first, G2_first), (G1_last, G2_last))[g != 0][ph]
        return (G1, G2)[ph].at[g - 1]

    def phase_slots(g, ph, first, count):
        slots = slots_of(g, ph)
        return slots.at[pl.ds(first, count)]

    def phase_start(g, ph):
        me, peers = phases[ph]
        slot = phase_slots(g, ph, me, 1)
        for peer in peers:
            pltpu.make_async_remote_copy(
                src_ref=slot,
                dst_ref=slot,
                send_sem=gs_sem.at[g, ph],
                recv_sem=gr_sem.at[g, ph],
                device_id=peer,
                device_id_type=LOGICAL,
            ).start()

    def phase_wait(g, ph):
        part = phase_slots(g, ph, 0, len(phases[ph][1]))
        pltpu.make_async_copy(part, part, gr_sem.at[g, ph]).wait()
        pltpu.make_async_copy(part, part, gs_sem.at[g, ph]).wait()

    def gather(g, tile, started, between):
        G1[g - 1, phases[0][0]] = tile
        phase_start(g, 0)
        started()
        phase_wait(g, 0)
        low, high = [jnp.sum(G1[g - 1, nx * c : nx * (c + 1)], axis=0) for c in range(2)]
        slot = phases[1][0]
        rows = [
            low[0:1] + high[3:4],
            high[0:1] + low[4:5],
            low[1:2],
            high[1:2],
            low[2:3],
            high[2:3],
            low[3:4],
            high[4:5],
            low[5:6] + high[5:6],
        ]
        for k, row in enumerate(rows):
            G2[g - 1, slot, k : k + 1] = row
        phase_start(g, 1)
        between()
        phase_wait(g, 1)

    def dots_of(g):
        row = jnp.sum(G2[g - 1, :, 8:9], axis=0)
        lane = lax.broadcasted_iota(jnp.int32, (1, 128), 1)
        return [
            jnp.broadcast_to(
                jnp.sum(jnp.where(lane >> 5 == k, row, 0.0), axis=1, keepdims=True), (1, 128)
            )
            for k in range(3)
        ]

    def right_side(g):
        def row(slot, k):
            if isinstance(g, int):
                return jnp.broadcast_to(G2_first[slot, k : k + 1], (8, 128))
            return jnp.broadcast_to(G2[g - 1, slot, k : k + 1], (8, 128))

        rows = [[None] * ny for _ in range(nz)]
        for j in range(ny):
            for k in range(chips):
                slot = j * chips + k
                for c in range(2):
                    total = row(slot, c)
                    if not isinstance(g, int):
                        if j + 1 < ny:
                            total = total + row(slot + chips, 2 + c)
                        if j > 0:
                            total = total + row(slot - chips, 4 + c)
                        if c == 0 and k > 0:
                            total = total + row(slot - 1, 7)
                        if c == 1 and k + 1 < chips:
                            total = total + row(slot + 1, 6)
                    rows[2 * k + c][j] = total
        return rows

    def coarse(g):
        accs = [jnp.zeros((16, 128), F32) for _ in range(7)]
        for i, rows in enumerate(right_side(g)):
            for j in range(ny):
                columns = slice((i * ny + j) * 128, (i * ny + j + 1) * 128)
                row = jnp.concatenate([rows[j], rows[j]], axis=0)
                accs[6] = accs[6] + inv[:, columns] * row
                for side in range(6):
                    accs[side] = accs[side] + inv_far[side, :, columns] * row
        values = []
        for side in range(7):
            total = jnp.broadcast_to(jnp.sum(accs[side], axis=1, keepdims=True), (16, 128))
            if side < 6:
                index = row16 * 0 + (gx, gz, gy)[side // 2]
                edge = (0, (nx, nz, ny)[side // 2] - 1)[side & 1]
                total = jnp.where(index == edge, 0.0, total)
            values.append(total)
        return values

    def take(values, masks):
        picked = [jnp.broadcast_to(values[m : m + 1], masks[0].shape) for m in range(16)]
        for mask in masks:
            picked = [jnp.where(mask, b, a) for a, b in zip(picked[::2], picked[1::2])]
        return picked[0]

    def masks_of(labels):
        return [labels & (1 << i) != 0 for i in range(4)]

    def take_plane(values, x):
        return take(values, [bits[i, x] > 0.5 for i in range(4)])

    def rim_of(values):
        x_far = [take(values[low], masks_of(lxh[low])) for low in range(2)]
        y_own = [take(values[6], masks_of(lys[low])) for low in range(2)]
        y_far = [take(values[2 + low], masks_of(lyh[low])) for low in range(2)]
        z_own = [take(values[6], masks_of(lzs[half])) for half in range(2)]
        z_far = []
        for half in range(2):
            masks = masks_of(lzf[half])
            z_far.append(jnp.where(even, take(values[4], masks), take(values[5], masks)))
        return x_far, y_own, y_far, z_own, z_far

    def outer_faces(y_own, y_far, z_own, z_far):
        for low in range(2):
            ey[low] = fyb[low] * (y_own[low] - y_far[low])
        for half in range(2):
            spread(fzp[half] * (z_own[half] - z_far[half]), half)

    def order_columns():
        for top in (0, 8):
            for j in range(ny):
                tiles = [inv_in[top : top + 8, pl.ds((i * ny + j) * 128, 128)] for i in range(nx)]
                for s in (4, 2, 1):
                    clear_bit = (lane8 >> 4) & s == 0
                    for i in range(nx):
                        if not i & s:
                            a, b = tiles[i], tiles[i | s]
                            tiles[i] = jnp.where(clear_bit, a, pltpu.roll(b, 16 * s, 1))
                            tiles[i | s] = jnp.where(clear_bit, pltpu.roll(a, 128 - 16 * s, 1), b)
                for i in range(nz):
                    inv[top : top + 8, pl.ds((i * ny + j) * 128, 128)] = tiles[i]

    loads[0].wait()
    loads[1].wait()
    sums = lax.fori_loop(0, cx, restrict_rhs, no_sums, unroll=4)
    line = jnp.sum(placed(label_sums(sums), gx), axis=0, keepdims=True)
    loads[3].wait()
    order_columns()
    pl.semaphore_wait(barrier, len(partners))
    G1_first[pl.ds(phases[0][0], 1), :] = line
    phase_start(0, 0)
    loads[2].wait()

    def stage_static(x, carry):
        mobility = interleaved(mob_in, x)
        mob[x + 1] = mobility
        stage_plane(MOB, x, mobility)
        labels = lab[x]
        stage_rows(lys, x, labels)
        lt[x] = pack_plane(labels)
        return carry

    lax.fori_loop(0, cx, stage_static, 0, unroll=4)
    stage_end(MOB)
    for half in range(2):
        lzs[half] = pack_end(lt, half)
    exchange_start(MOB)
    exchange_start(LAB)
    exchange_start(INV)

    def faces():
        for ref in (direction, ws, yrim_x, yrim_y, yrim_z, prim_y, prim_z):
            clear(ref)
        exchange_wait(MOB)
        exchange_wait(LAB)
        for half in range(2):
            lzf[half] = far(lzh, half)
            fzp[half] = 0.5 * (zs[MOB, half] + far(zh.at[MOB], half))
            spread(fzp[half], half)
        for low in range(2):
            fyb[low] = 0.5 * (ys[MOB, low] + yh[MOB, low])
            ey[low] = fyb[low]
        fx[0] = 0.5 * (mob[1] + mob[0])
        row = lax.broadcasted_iota(jnp.int32, (64, 128), 0)
        lane = lax.broadcasted_iota(jnp.int32, (64, 128), 1)

        def step(x, below):
            m = mob[x + 1]
            above = 0.5 * (mob[x + 2] + m)
            face_y = jnp.where(row == 63, 0.0, 0.5 * (next_row(m) + m))
            face_z = jnp.where(lane == 127, 0.0, 0.5 * (pltpu.roll(m, 127, 1) + m))
            edges = edge_tiles(x)
            diag = (
                (below + above)
                + (last_row(face_y) + face_y)
                + (pltpu.roll(face_z, 1, 1) + face_z)
                + edges
            )
            rim[x] = edges
            fx[x + 1] = above
            fy[x] = face_y
            fz[x] = face_z
            dinv[x] = 1.0 / diag
            return above

        lax.fori_loop(0, cx, step, fx[0], unroll=4)

    phase_wait(0, 0)
    G2_first[phases[1][0]] = jnp.concatenate(
        [jnp.sum(G1_first[nx * c : nx * (c + 1)], axis=0, keepdims=True) for c in range(2)], axis=0
    )
    phase_start(0, 1)
    faces()
    phase_wait(0, 1)

    exchange_wait(INV)
    lines = coarse(0)

    def first_iterate(x):
        plane = take_plane(lines[6], x)
        x0[x + 1] = plane
        return plane

    x_far, *rest = rim_of(lines)
    x0[0] = x_far[0]
    x0[cx + 1] = x_far[1]
    outer_faces(*rest)

    def first_residual(x, v, out, dot):
        residual = rhs[x] - out
        precond = residual * dinv[x]
        rs[x] = residual
        field[x + 1] = precond
        stage_plane(0, x, precond)
        return dot + fold(residual * precond)

    ry_part = apply_all(x0, first_residual, zero, edge_part, first_iterate)
    stage_end(0)

    def tall(row):
        return jnp.broadcast_to(row, (8, 128))

    def one_step(k, carry):
        ry, lines, dots, _, last_alpha = carry
        ry = ry[0:1]
        sums, parts = coarse_right_side(k)
        gather(
            k + 1,
            message(sums, parts, dots),
            lambda: exchange_start(k),
            lambda: exchange_wait(k),
        )
        more = coarse(k + 1)
        d0, d1, d2 = dots_of(k + 1)
        first = lax.broadcasted_iota(jnp.int32, (1, 128), 0) + k == 0
        alpha = jnp.where(first, 0.0, ry / d0)
        ry_next = jnp.where(first, d0, ry + alpha * (alpha * d2 - 2.0 * d1))
        beta = jnp.where(first, 0.0, ry_next / ry)
        gain = jnp.where(first, 1.0, -alpha)
        lines = [line + gain * extra for line, extra in zip(lines, more)]

        x_far, y_own, y_far, z_own, z_far = rim_of(lines)
        for low in range(2):
            outer = cx + 1 if low else 0
            layer = yrim_x[low] + gain * xh[k, low]
            yrim_x[low] = layer
            direction[outer] = (layer + beta * direction[outer]) - x_far[low]
        rows = [ys[k, 0], ys[k, 1], yh[k, 0], yh[k, 1]]
        packs = [zs[k, 0], zs[k, 1], far(zh.at[k], 0), far(zh.at[k], 1)]
        for i, (y_part, z_part) in enumerate(zip(y_own + y_far, z_own + z_far)):
            row = yrim_y[i] + gain * rows[i]
            pack = yrim_z[i] + gain * packs[i]
            yrim_y[i] = row
            yrim_z[i] = pack
            prim_y[i] = (row + beta * prim_y[i]) - y_part
            prim_z[i] = (pack + beta * prim_z[i]) - z_part
        outer_faces(
            [prim_y[0], prim_y[1]],
            [prim_y[2], prim_y[3]],
            [prim_z[0], prim_z[1]],
            [prim_z[2], prim_z[3]],
        )

        def next_direction(x):
            residual = rs[x] - alpha * ws[x]
            rs[x] = residual
            plane = (residual * dinv[x] + beta * direction[x + 1]) - take_plane(lines[6], x)
            direction[x + 1] = plane
            history[k, x] = plane
            return plane

        def image(x, v, out, dots):
            z = out * dinv[x]
            ws[x] = out
            field[x + 1] = z
            stage_plane(k + 1, x, z)
            return (
                dots[0] + fold(v * out),
                dots[1] + fold(rs[x] * z),
                dots[2] + fold(out * z),
            )

        dots = apply_all(direction, image, (zero, zero, zero), edge_part, next_direction)
        stage_end(k + 1)
        return tall(ry_next), lines, dots, last_alpha, tall(alpha)

    ry, _, dots, *alphas = lax.fori_loop(
        0, STEPS, one_step, (zero + 1.0, [jnp.zeros((16, 128), F32)] * 7, (ry_part, zero, zero), zero, zero)
    )
    ry, alphas = ry[0:1], [alpha[0:1] for alpha in alphas]

    stores = [
        pltpu.make_async_copy(ordered.at[i], out, out_sem.at[i])
        for i, out in enumerate((x_hbm, p_hbm, r_hbm, w_hbm))
    ]
    G1_last[pl.ds(phases[0][0], 1), :] = jnp.sum(dots[0], axis=0, keepdims=True)
    phase_start(STEPS + 1, 0)

    def join_iterate(x, carry):
        joined = (x0[x + 1] + alphas[0] * history[0, x]) + alphas[1] * history[1, x]
        for i, plane in enumerate((joined, history[STEPS - 1, x], rs[x], ws[x])):
            store_in_order(ordered.at[i], x, plane)
        return carry

    lax.fori_loop(0, cx, join_iterate, 0, unroll=4)
    for store in stores:
        store.start()
    phase_wait(STEPS + 1, 0)
    G2_last[pl.ds(phases[1][0], 1), :] = jnp.sum(G1_last[...], axis=0, keepdims=True)
    phase_start(STEPS + 1, 1)
    phase_wait(STEPS + 1, 1)
    total = jnp.sum(jnp.sum(G2_last[...], axis=0, keepdims=True), axis=1, keepdims=True)
    step_out[...] = jnp.broadcast_to(ry / total, step_out.shape)
    for store in stores:
        store.wait()


def solution(mesh):
    nx, ny, nz = mesh.shape["gx"], mesh.shape["gy"], mesh.shape["gz"]

    def per_device(rhs, mobility, labels, coarse_inverse):
        cx, cy, cz = rhs.shape
        hbm = pl.BlockSpec(memory_space=pl.ANY)

        def vmem(*shape, dtype=F32):
            return pltpu.VMEM(shape, dtype)

        i32 = jnp.int32
        xs, p, rs, w, alpha = pl.pallas_call(
            functools.partial(kernel, nx, ny, nz),
            out_shape=[jax.ShapeDtypeStruct(rhs.shape, F32)] * 4
            + [jax.ShapeDtypeStruct((cy, cz), F32)],
            in_specs=[hbm] * 4,
            out_specs=[hbm] * 4 + [pl.BlockSpec(memory_space=pltpu.VMEM)],
            scratch_shapes=[
                *[vmem(cx + 2, cy, cz) for _ in range(4)],
                vmem(STEPS, cx, cy, cz),
                vmem(cx, cy, cz),
                vmem(cx, cy, cz, dtype=i32),
                vmem(cx, cy, cz),
                vmem(cx, cy, cz),
                vmem(cx, cy, cz, dtype=i32),
                vmem(*coarse_inverse.shape),
                vmem(*coarse_inverse.shape),
                vmem(6, *coarse_inverse.shape),
                vmem(cx + 1, cy, cz),
                *[vmem(cx, cy, cz) for _ in range(4)],
                vmem(4, cx, cy, cz),
                vmem(2, cx, cz),
                vmem(2, 8, 128),
                vmem(4, cx, cy, cz),
                *[vmem(cx, cy, cz) for _ in range(2)],
                vmem(STEPS, 2, cy, cz),
                vmem(4, 2, cx, cz),
                vmem(4, 2, cx, cz),
                vmem(4, 2, 8, 128),
                vmem(4, 2, 2, 8, 128),
                vmem(2, cy, cz, dtype=i32),
                vmem(2, cx, cz, dtype=i32),
                vmem(2, cx, cz, dtype=i32),
                vmem(2, 8, 128, dtype=i32),
                vmem(2, 2, 8, 128, dtype=i32),
                vmem(2, 8, 128, dtype=i32),
                vmem(2, cy, cz),
                vmem(4, cx, cz),
                vmem(4, 8, 128),
                vmem(4, cx, cz),
                vmem(4, 8, 128),
                vmem(cx, 8, 128),
                vmem(cx, 8, 128, dtype=i32),
                vmem(cx, 8, 128),
                vmem(2, cx, cz),
                vmem(2 * nx, 128),
                vmem(ny * nz // 2, 2, 128),
                vmem(STEPS, 2 * nx, 6, 128),
                vmem(STEPS, ny * nz // 2, 9, 128),
                vmem(2 * nx, 128),
                vmem(ny * nz // 2, 128),
                pltpu.SemaphoreType.DMA((4,)),
                pltpu.SemaphoreType.DMA((4,)),
                pltpu.SemaphoreType.DMA((6, 6)),
                pltpu.SemaphoreType.DMA((6, 6)),
                pltpu.SemaphoreType.DMA((5, 2)),
                pltpu.SemaphoreType.DMA((5, 2)),
            ],
            compiler_params=pltpu.CompilerParams(
                collective_id=0, has_side_effects=True, vmem_limit_bytes=VMEM_BYTES
            ),
            name="deflated_cg",
        )(rhs, mobility, labels, coarse_inverse)
        return xs + alpha * p, rs - alpha * w

    spec = P("gx", "gz", "gy")
    return jax.shard_map(
        per_device,
        mesh=mesh,
        in_specs=(spec, spec, spec, P(("gx", "gy", "gz"), None)),
        out_specs=(spec, spec),
        check_vma=False,
    )
```

```python
import functools

import jax
import jax.numpy as jnp
from jax import lax
from jax.experimental import pallas as pl
from jax.experimental.pallas import tpu as pltpu
from jax.sharding import PartitionSpec as P

LOGICAL = pl.DeviceIdType.LOGICAL
F32 = jnp.float32
LOOP = 5
VMEM_BYTES = 64 * 1024 * 1024 - 256 * 1024

STEPS = 3
MOB, LAB, INV = range(STEPS, STEPS + 3)


def farthest_first(n):
    return sorted(range(n), key=lambda k: -min(k, n - k))


def kernel(
    nx,
    ny,
    nz,
    rhs_hbm,
    mob_hbm,
    lab_hbm,
    inv_hbm,
    x_hbm,
    p_hbm,
    r_hbm,
    w_hbm,
    step_out,
    mob,
    x0,
    field,
    direction,
    history,
    rhs_in,
    lab_in,
    mob_in,
    rhs,
    lab,
    inv_in,
    inv,
    inv_far,
    fx,
    fy,
    fz,
    dinv,
    rim,
    bits,
    fyb,
    fzp,
    ordered,
    rs,
    ws,
    xh,
    ys,
    yh,
    zs,
    zh,
    lxh,
    lys,
    lyh,
    lzs,
    lzh,
    lzf,
    yrim_x,
    yrim_y,
    yrim_z,
    prim_y,
    prim_z,
    zt,
    lt,
    et,
    ey,
    G1_first,
    G2_first,
    G1,
    G2,
    G1_last,
    G2_last,
    in_sem,
    out_sem,
    hs_sem,
    hr_sem,
    gs_sem,
    gr_sem,
):
    cx = rhs.shape[0]
    gx, gy, gz = lax.axis_index("gx"), lax.axis_index("gy"), lax.axis_index("gz")
    def logical(x, y, z):
        return (lax.rem(x, nx) * ny + lax.rem(y, ny)) * nz + lax.rem(z, nz)

    sides = (
        ("gx", gx > 0, logical(gx + nx - 1, gy, gz)),
        ("gx", gx < nx - 1, logical(gx + 1, gy, gz)),
        ("gz", gz > 0, logical(gx, gy, gz + nz - 1)),
        ("gz", gz < nz - 1, logical(gx, gy, gz + 1)),
        ("gy", gy > 0, logical(gx, gy + ny - 1, gz)),
        ("gy", gy < ny - 1, logical(gx, gy + 1, gz)),
    )

    loads = [
        pltpu.make_async_copy(rhs_hbm, rhs_in, in_sem.at[0]),
        pltpu.make_async_copy(lab_hbm, lab_in, in_sem.at[1]),
        pltpu.make_async_copy(mob_hbm, mob_in, in_sem.at[2]),
        pltpu.make_async_copy(inv_hbm, inv_in, in_sem.at[3]),
    ]
    for load in loads:
        load.start()

    barrier = pltpu.get_barrier_semaphore()
    chips = nz // 2
    chip, core = lax.div(gz, 2), lax.rem(gz, 2)
    line_peers = [
        logical(gx + k, gy, 2 * chip + lax.rem(core + c, 2))
        for k in farthest_first(nx)
        for c in (1, 0)
        if k or c
    ]
    plane_peers = [
        logical(gx, gy + j, gz + 2 * k)
        for j in farthest_first(ny)
        for k in farthest_first(chips)
        if j or k
    ]
    phases = ((core * nx + gx, line_peers), (gy * chips + chip, plane_peers))
    partners = line_peers + plane_peers + [logical(gx, gy, gz + nz - 1 + 2 * core)]
    for partner in partners:
        pl.semaphore_signal(barrier, inc=1, device_id=partner, device_id_type=LOGICAL)

    def clear(ref, *index):
        ref[index or Ellipsis] = jnp.zeros(ref.shape[len(index) :], ref.dtype)

    for low in range(2):

        @pl.when(gx == (nx - 1 if low else 0))
        def _():
            clear(mob, cx + 1 if low else 0)
            clear(lxh, low)
            for e in range(STEPS):
                clear(xh, e, low)

        @pl.when(gz == (nz - 1 if low else 0))
        def _():
            clear(lyh, low)
            for e in range(STEPS + 1):
                clear(yh, e, low)

        @pl.when(gy == (ny - 1 if low else 0))
        def _():
            clear(lzh, low)
            for e in range(STEPS + 1):
                clear(zh, e, low)

    clear(field, 0)
    clear(field, cx + 1)

    lane8 = lax.broadcasted_iota(jnp.int32, (8, 128), 1)
    row8 = lax.broadcasted_iota(jnp.int32, (8, 128), 0)
    lane16 = lax.broadcasted_iota(jnp.int32, (16, 128), 1)
    row16 = lax.broadcasted_iota(jnp.int32, (16, 128), 0)
    pair = ((lane8 + 1) >> 1) & 63
    ends = (lane8 == 0) | (lane8 == 127)
    even = (lane8 & 1) == 0
    zero = jnp.zeros((8, 128), F32)

    def interleaved(ref, x):
        return jnp.concatenate([ref[x, pl.ds(k, 8, stride=8), :] for k in range(8)], axis=0)

    def store_in_order(ref, x, plane):
        for k in range(8):
            ref[x, pl.ds(k, 8, stride=8), :] = plane[8 * k : 8 * k + 8]

    def next_row(plane):
        return jnp.concatenate([plane[8:], pltpu.roll(plane[:8], 7, 0)], axis=0)

    def last_row(plane):
        return jnp.concatenate([pltpu.roll(plane[56:], 1, 0), plane[:56]], axis=0)

    def fold(plane):
        tiles = [plane[k : k + 8] for k in range(0, plane.shape[0], 8)]
        while len(tiles) > 1:
            tiles = [a + b for a, b in zip(tiles[::2], tiles[1::2])]
        return tiles[0]

    def halo_copy(e, side):
        axis, _, index = sides[side]
        low, other = side & 1, 1 - (side & 1)
        kind = e if isinstance(e, int) else 0
        if kind == INV:
            src, dst = inv, inv_far.at[side ^ 1]
        elif kind == LAB:
            if axis == "gx":
                src, dst = lab.at[cx - 1 if low else 0], lxh.at[other]
            elif axis == "gz":
                src, dst = lys.at[low], lyh.at[other]
            else:
                src, dst = lzs, lzh.at[other]
        elif axis == "gx":
            src = (mob if kind == MOB else field).at[cx if low else 1]
            dst = mob.at[0 if low else cx + 1] if kind == MOB else xh.at[e, other]
        elif axis == "gz":
            src, dst = ys.at[e, low], yh.at[e, other]
        else:
            src, dst = zs.at[e], zh.at[e, other]
        return pltpu.make_async_remote_copy(
            src_ref=src,
            dst_ref=dst,
            send_sem=hs_sem.at[e, side],
            recv_sem=hr_sem.at[e, side ^ 1],
            device_id=index,
            device_id_type=LOGICAL,
        )

    def halo_landed(e, side):
        low = side & 1
        kind = e if isinstance(e, int) else 0
        if kind == INV:
            ref = inv_far.at[side]
        elif kind == LAB:
            ref = (lxh, lyh, lzh)[side // 2].at[low]
        elif side < 2:
            ref = mob.at[cx + 1 if low else 0] if kind == MOB else xh.at[e, low]
        else:
            ref = (yh, zh)[side // 2 - 1].at[e, low]
        return pltpu.make_async_copy(ref, ref, hr_sem.at[e, side])

    def exchange_start(e):
        for side in (0, 1, 4, 5, 2, 3):

            @pl.when(sides[side][1])
            def _():
                halo_copy(e, side).start()

    def exchange_wait(e):
        for side in range(6):

            @pl.when(sides[side][1])
            def _():
                halo_landed(e, side).wait()
                halo_copy(e, side).wait_send()

    def stage_rows(rows, x, plane):
        rows[0, pl.ds(x, 1), :] = plane[0:1]
        rows[1, pl.ds(x, 1), :] = plane[63:64]

    def pack_plane(plane):
        packed = plane[0:8]
        for k in range(1, 8):
            packed = jnp.where(pair == k, pltpu.roll(plane[8 * k : 8 * k + 8], 2 * k, 1), packed)
        return jnp.where(pair < 8, packed, jnp.zeros_like(packed))

    def pack_end(tiles, half):
        total = tiles[8 * half]
        for k in range(1, 8):
            total = total + pltpu.roll(tiles[8 * half + k], 16 * k, 1)
        return total

    def stage_plane(e, x, plane):
        stage_rows(ys.at[e], x, plane)
        zt[x] = pack_plane(plane)

    def stage_end(e):
        for half in range(2):
            zs[e, half] = pack_end(zt, half)

    def far(received, half):
        return jnp.where(
            even, pltpu.roll(received[0, half], 1, 1), pltpu.roll(received[1, half], 127, 1)
        )

    def spread(packed, half):
        et[8 * half] = packed
        for k in range(1, 8):
            et[8 * half + k] = pltpu.roll(packed, 128 - 16 * k, 1)

    def edge_part(x, v):
        return edge_tiles(x)

    def edge_tiles(x):
        tile = et[x]
        tiles = [
            jnp.where(ends, tile if k == 0 else pltpu.roll(tile, 128 - 2 * k, 1), 0.0)
            for k in range(8)
        ]
        first, last = ey[0, pl.ds(x, 1), :], ey[1, pl.ds(x, 1), :]
        tiles[0] = tiles[0] + jnp.where(row8 == 0, first, 0.0)
        tiles[7] = tiles[7] + jnp.where(row8 == 7, last, 0.0)
        return jnp.concatenate(tiles, axis=0)

    def apply_all(values, body, init, outer, make=None):
        def step(x, carry, above_v):
            below, v, rest = carry
            above = fx[x + 1] * (above_v - v)
            flux_y = fy[x] * (next_row(v) - v)
            flux_z = fz[x] * (pltpu.roll(v, 127, 1) - v)
            out = (
                (below - above)
                + (last_row(flux_y) - flux_y)
                + (pltpu.roll(flux_z, 1, 1) - flux_z)
                + outer(x, v)
            )
            return above, above_v, body(x, v, out, rest)

        if make is None:

            def make(x):
                return values[x + 1]

        v = make(0)
        carry = (fx[0] * (v - values[0]), v, init)
        carry = lax.fori_loop(
            0, cx - 1, lambda x, c: step(x, c, make(x + 1)), carry, unroll=LOOP
        )
        return step(cx - 1, carry, values[cx + 1])[2]

    def subset_sums(values, bits):
        terms = [values]
        for bit in bits:
            terms = terms + [term * bit for term in terms]
        return [fold(term) for term in terms]

    def label_sums(sums):
        sums = list(sums)
        for i in range(4):
            for value in range(16):
                if not value >> i & 1:
                    sums[value] = sums[value] - sums[value | 1 << i]
        return sums

    def bits_of(labels):
        return [((labels >> i) & 1).astype(F32) for i in range(4)]

    def by_label(labels, values):
        return label_sums(subset_sums(values, bits_of(labels)))

    def restrict_plane(x, plane, sums):
        more = subset_sums(plane, [bits[i, x] for i in range(4)])
        return tuple(total + extra for total, extra in zip(sums, more))

    def restrict_rhs(x, sums):
        labels = interleaved(lab_in, x)
        values = interleaved(rhs_in, x)
        lab[x] = labels
        rhs[x] = values
        planes = bits_of(labels)
        for i in range(4):
            bits[i, x] = planes[i]
        return tuple(total + extra for total, extra in zip(sums, subset_sums(values, planes)))

    no_sums = (zero,) * 16

    def rows_of(tiles):
        for shift in (4, 2, 1):
            low = (row8 & shift) == 0
            half = len(tiles) // 2
            merged = []
            for a, b in zip(tiles[:half], tiles[half:]):
                kept, moved = jnp.where(low, a, b), jnp.where(low, b, a)
                if shift == 4:
                    moved = pltpu.roll(moved, 4, 0)
                else:
                    moved = jnp.where(
                        low, pltpu.roll(moved, 8 - shift, 0), pltpu.roll(moved, shift, 0)
                    )
                merged.append(kept + moved)
            tiles = merged
        return tiles[0]

    def placed(sums, block):
        rows = jnp.concatenate([rows_of(list(sums[:8])), rows_of(list(sums[8:]))], axis=0)
        column = jnp.sum(rows, axis=1, keepdims=True)
        return fold(jnp.where(lane16 == 16 * block + row16, column, 0.0))

    def message(sums, parts, dots):
        tiles = [placed(sums, gx) + placed(parts[0], gx - 1) + placed(parts[1], gx + 1)]
        for side in (4, 5, 2, 3):
            tiles.append(placed(parts[side], gx))
        joined = zero
        for k, dot in enumerate(dots):
            dot = dot + pltpu.roll(dot, 64, 1)
            joined = jnp.where(lane8 >> 5 == k, dot + pltpu.roll(dot, 32, 1), joined)
        return rows_of(tiles + [joined, zero, zero])[:6]

    def neighbour_parts(e):
        parts = [
            by_label(lxh[0], -(fx[0] * field[1])),
            by_label(lxh[1], -(fx[cx] * field[cx])),
        ]
        for low in range(2):
            parts.append(by_label(lyh[low], -(fyb[low] * ys[e, low])))
        for keep in (even, ~even):
            halves = [
                by_label(lzf[half], jnp.where(keep, -(fzp[half] * zs[e, half]), 0.0))
                for half in range(2)
            ]
            parts.append([a + b for a, b in zip(*halves)])
        return parts

    def coarse_right_side(e):
        sums = apply_all(
            field, lambda x, v, out, s: restrict_plane(x, out, s), no_sums, lambda x, v: rim[x] * v
        )
        return label_sums(sums), neighbour_parts(e)

    def slots_of(g, ph):
        if isinstance(g, int):
            return ((G1_first, G2_first), (G1_last, G2_last))[g != 0][ph]
        return (G1, G2)[ph].at[g - 1]

    def phase_slots(g, ph, first, count):
        slots = slots_of(g, ph)
        return slots.at[pl.ds(first, count)]

    def phase_start(g, ph):
        me, peers = phases[ph]
        slot = phase_slots(g, ph, me, 1)
        for peer in peers:
            pltpu.make_async_remote_copy(
                src_ref=slot,
                dst_ref=slot,
                send_sem=gs_sem.at[g, ph],
                recv_sem=gr_sem.at[g, ph],
                device_id=peer,
                device_id_type=LOGICAL,
            ).start()

    def phase_wait(g, ph):
        part = phase_slots(g, ph, 0, len(phases[ph][1]))
        pltpu.make_async_copy(part, part, gr_sem.at[g, ph]).wait()
        pltpu.make_async_copy(part, part, gs_sem.at[g, ph]).wait()

    def gather(g, tile, started, between):
        G1[g - 1, phases[0][0]] = tile
        phase_start(g, 0)
        started()
        phase_wait(g, 0)
        low, high = [jnp.sum(G1[g - 1, nx * c : nx * (c + 1)], axis=0) for c in range(2)]
        slot = phases[1][0]
        rows = [
            low[0:1] + high[3:4],
            high[0:1] + low[4:5],
            low[1:2],
            high[1:2],
            low[2:3],
            high[2:3],
            low[3:4],
            high[4:5],
            low[5:6] + high[5:6],
        ]
        for k, row in enumerate(rows):
            G2[g - 1, slot, k : k + 1] = row
        phase_start(g, 1)
        between()
        phase_wait(g, 1)

    def dots_of(g):
        row = jnp.sum(G2[g - 1, :, 8:9], axis=0)
        lane = lax.broadcasted_iota(jnp.int32, (1, 128), 1)
        return [
            jnp.broadcast_to(
                jnp.sum(jnp.where(lane >> 5 == k, row, 0.0), axis=1, keepdims=True), (1, 128)
            )
            for k in range(3)
        ]

    def right_side(g):
        def row(slot, k):
            if isinstance(g, int):
                return jnp.broadcast_to(G2_first[slot, k : k + 1], (8, 128))
            return jnp.broadcast_to(G2[g - 1, slot, k : k + 1], (8, 128))

        rows = [[None] * ny for _ in range(nz)]
        for j in range(ny):
            for k in range(chips):
                slot = j * chips + k
                for c in range(2):
                    total = row(slot, c)
                    if not isinstance(g, int):
                        if j + 1 < ny:
                            total = total + row(slot + chips, 2 + c)
                        if j > 0:
                            total = total + row(slot - chips, 4 + c)
                        if c == 0 and k > 0:
                            total = total + row(slot - 1, 7)
                        if c == 1 and k + 1 < chips:
                            total = total + row(slot + 1, 6)
                    rows[2 * k + c][j] = total
        return rows

    def coarse(g):
        accs = [jnp.zeros((16, 128), F32) for _ in range(7)]
        for i, rows in enumerate(right_side(g)):
            for j in range(ny):
                columns = slice((i * ny + j) * 128, (i * ny + j + 1) * 128)
                row = jnp.concatenate([rows[j], rows[j]], axis=0)
                accs[6] = accs[6] + inv[:, columns] * row
                for side in range(6):
                    accs[side] = accs[side] + inv_far[side, :, columns] * row
        values = []
        for side in range(7):
            total = jnp.broadcast_to(jnp.sum(accs[side], axis=1, keepdims=True), (16, 128))
            if side < 6:
                index = row16 * 0 + (gx, gz, gy)[side // 2]
                edge = (0, (nx, nz, ny)[side // 2] - 1)[side & 1]
                total = jnp.where(index == edge, 0.0, total)
            values.append(total)
        return values

    def take(values, masks):
        picked = [jnp.broadcast_to(values[m : m + 1], masks[0].shape) for m in range(16)]
        for mask in masks:
            picked = [jnp.where(mask, b, a) for a, b in zip(picked[::2], picked[1::2])]
        return picked[0]

    def masks_of(labels):
        return [labels & (1 << i) != 0 for i in range(4)]

    def take_plane(values, x):
        return take(values, [bits[i, x] > 0.5 for i in range(4)])

    def rim_of(values):
        x_far = [take(values[low], masks_of(lxh[low])) for low in range(2)]
        y_own = [take(values[6], masks_of(lys[low])) for low in range(2)]
        y_far = [take(values[2 + low], masks_of(lyh[low])) for low in range(2)]
        z_own = [take(values[6], masks_of(lzs[half])) for half in range(2)]
        z_far = []
        for half in range(2):
            masks = masks_of(lzf[half])
            z_far.append(jnp.where(even, take(values[4], masks), take(values[5], masks)))
        return x_far, y_own, y_far, z_own, z_far

    def outer_faces(y_own, y_far, z_own, z_far):
        for low in range(2):
            ey[low] = fyb[low] * (y_own[low] - y_far[low])
        for half in range(2):
            spread(fzp[half] * (z_own[half] - z_far[half]), half)

    def order_columns():
        for top in (0, 8):
            for j in range(ny):
                tiles = [inv_in[top : top + 8, pl.ds((i * ny + j) * 128, 128)] for i in range(nx)]
                for s in (4, 2, 1):
                    clear_bit = (lane8 >> 4) & s == 0
                    for i in range(nx):
                        if not i & s:
                            a, b = tiles[i], tiles[i | s]
                            tiles[i] = jnp.where(clear_bit, a, pltpu.roll(b, 16 * s, 1))
                            tiles[i | s] = jnp.where(clear_bit, pltpu.roll(a, 128 - 16 * s, 1), b)
                for i in range(nz):
                    inv[top : top + 8, pl.ds((i * ny + j) * 128, 128)] = tiles[i]

    def stage_static(x, carry):
        mobility = interleaved(mob_in, x)
        mob[x + 1] = mobility
        stage_plane(MOB, x, mobility)
        labels = lab[x]
        stage_rows(lys, x, labels)
        lt[x] = pack_plane(labels)
        return carry

    loads[0].wait()
    loads[1].wait()
    sums = lax.fori_loop(0, cx, restrict_rhs, no_sums, unroll=4)
    line = jnp.sum(placed(label_sums(sums), gx), axis=0, keepdims=True)
    loads[3].wait()
    order_columns()
    loads[2].wait()
    lax.fori_loop(0, cx, stage_static, 0, unroll=4)
    stage_end(MOB)
    for half in range(2):
        lzs[half] = pack_end(lt, half)
    pl.semaphore_wait(barrier, len(partners))
    G1_first[pl.ds(phases[0][0], 1), :] = line
    phase_start(0, 0)
    exchange_start(MOB)
    exchange_start(LAB)
    exchange_start(INV)

    def faces():
        for ref in (direction, ws, yrim_x, yrim_y, yrim_z, prim_y, prim_z):
            clear(ref)
        exchange_wait(MOB)
        exchange_wait(LAB)
        for half in range(2):
            lzf[half] = far(lzh, half)
            fzp[half] = 0.5 * (zs[MOB, half] + far(zh.at[MOB], half))
            spread(fzp[half], half)
        for low in range(2):
            fyb[low] = 0.5 * (ys[MOB, low] + yh[MOB, low])
            ey[low] = fyb[low]
        fx[0] = 0.5 * (mob[1] + mob[0])
        row = lax.broadcasted_iota(jnp.int32, (64, 128), 0)
        lane = lax.broadcasted_iota(jnp.int32, (64, 128), 1)

        def step(x, below):
            m = mob[x + 1]
            above = 0.5 * (mob[x + 2] + m)
            face_y = jnp.where(row == 63, 0.0, 0.5 * (next_row(m) + m))
            face_z = jnp.where(lane == 127, 0.0, 0.5 * (pltpu.roll(m, 127, 1) + m))
            edges = edge_tiles(x)
            diag = (
                (below + above)
                + (last_row(face_y) + face_y)
                + (pltpu.roll(face_z, 1, 1) + face_z)
                + edges
            )
            rim[x] = edges
            fx[x + 1] = above
            fy[x] = face_y
            fz[x] = face_z
            dinv[x] = 1.0 / diag
            return above

        lax.fori_loop(0, cx, step, fx[0], unroll=4)

    phase_wait(0, 0)
    G2_first[phases[1][0]] = jnp.concatenate(
        [jnp.sum(G1_first[nx * c : nx * (c + 1)], axis=0, keepdims=True) for c in range(2)], axis=0
    )
    phase_start(0, 1)
    faces()
    phase_wait(0, 1)

    exchange_wait(INV)
    lines = coarse(0)

    def first_iterate(x):
        plane = take_plane(lines[6], x)
        x0[x + 1] = plane
        return plane

    x_far, *rest = rim_of(lines)
    x0[0] = x_far[0]
    x0[cx + 1] = x_far[1]
    outer_faces(*rest)

    def first_residual(x, v, out, dot):
        residual = rhs[x] - out
        precond = residual * dinv[x]
        rs[x] = residual
        field[x + 1] = precond
        stage_plane(0, x, precond)
        return dot + fold(residual * precond)

    ry_part = apply_all(x0, first_residual, zero, edge_part, first_iterate)
    stage_end(0)

    def tall(row):
        return jnp.broadcast_to(row, (8, 128))

    def one_step(k, carry):
        ry, lines, dots, _, last_alpha = carry
        ry = ry[0:1]
        sums, parts = coarse_right_side(k)
        gather(
            k + 1,
            message(sums, parts, dots),
            lambda: exchange_start(k),
            lambda: exchange_wait(k),
        )
        more = coarse(k + 1)
        d0, d1, d2 = dots_of(k + 1)
        first = lax.broadcasted_iota(jnp.int32, (1, 128), 0) + k == 0
        alpha = jnp.where(first, 0.0, ry / d0)
        ry_next = jnp.where(first, d0, ry + alpha * (alpha * d2 - 2.0 * d1))
        beta = jnp.where(first, 0.0, ry_next / ry)
        gain = jnp.where(first, 1.0, -alpha)
        lines = [line + gain * extra for line, extra in zip(lines, more)]

        x_far, y_own, y_far, z_own, z_far = rim_of(lines)
        for low in range(2):
            outer = cx + 1 if low else 0
            layer = yrim_x[low] + gain * xh[k, low]
            yrim_x[low] = layer
            direction[outer] = (layer + beta * direction[outer]) - x_far[low]
        rows = [ys[k, 0], ys[k, 1], yh[k, 0], yh[k, 1]]
        packs = [zs[k, 0], zs[k, 1], far(zh.at[k], 0), far(zh.at[k], 1)]
        for i, (y_part, z_part) in enumerate(zip(y_own + y_far, z_own + z_far)):
            row = yrim_y[i] + gain * rows[i]
            pack = yrim_z[i] + gain * packs[i]
            yrim_y[i] = row
            yrim_z[i] = pack
            prim_y[i] = (row + beta * prim_y[i]) - y_part
            prim_z[i] = (pack + beta * prim_z[i]) - z_part
        outer_faces(
            [prim_y[0], prim_y[1]],
            [prim_y[2], prim_y[3]],
            [prim_z[0], prim_z[1]],
            [prim_z[2], prim_z[3]],
        )

        def next_direction(x):
            residual = rs[x] - alpha * ws[x]
            rs[x] = residual
            plane = (residual * dinv[x] + beta * direction[x + 1]) - take_plane(lines[6], x)
            direction[x + 1] = plane
            history[k, x] = plane
            return plane

        def image(x, v, out, dots):
            z = out * dinv[x]
            ws[x] = out
            field[x + 1] = z
            stage_plane(k + 1, x, z)
            return (
                dots[0] + fold(v * out),
                dots[1] + fold(rs[x] * z),
                dots[2] + fold(out * z),
            )

        dots = apply_all(direction, image, (zero, zero, zero), edge_part, next_direction)
        stage_end(k + 1)
        return tall(ry_next), lines, dots, last_alpha, tall(alpha)

    ry, _, dots, *alphas = lax.fori_loop(
        0, STEPS, one_step, (zero + 1.0, [jnp.zeros((16, 128), F32)] * 7, (ry_part, zero, zero), zero, zero)
    )
    ry, alphas = ry[0:1], [alpha[0:1] for alpha in alphas]

    stores = [
        pltpu.make_async_copy(ordered.at[i], out, out_sem.at[i])
        for i, out in enumerate((x_hbm, p_hbm, r_hbm, w_hbm))
    ]
    G1_last[pl.ds(phases[0][0], 1), :] = jnp.sum(dots[0], axis=0, keepdims=True)
    phase_start(STEPS + 1, 0)

    def join_iterate(x, carry):
        joined = (x0[x + 1] + alphas[0] * history[0, x]) + alphas[1] * history[1, x]
        for i, plane in enumerate((joined, history[STEPS - 1, x], rs[x], ws[x])):
            store_in_order(ordered.at[i], x, plane)
        return carry

    lax.fori_loop(0, cx, join_iterate, 0, unroll=4)
    for store in stores:
        store.start()
    phase_wait(STEPS + 1, 0)
    G2_last[pl.ds(phases[1][0], 1), :] = jnp.sum(G1_last[...], axis=0, keepdims=True)
    phase_start(STEPS + 1, 1)
    phase_wait(STEPS + 1, 1)
    total = jnp.sum(jnp.sum(G2_last[...], axis=0, keepdims=True), axis=1, keepdims=True)
    step_out[...] = jnp.broadcast_to(ry / total, step_out.shape)
    for store in stores:
        store.wait()


def solution(mesh):
    nx, ny, nz = mesh.shape["gx"], mesh.shape["gy"], mesh.shape["gz"]

    def per_device(rhs, mobility, labels, coarse_inverse):
        cx, cy, cz = rhs.shape
        hbm = pl.BlockSpec(memory_space=pl.ANY)

        def vmem(*shape, dtype=F32):
            return pltpu.VMEM(shape, dtype)

        i32 = jnp.int32
        xs, p, rs, w, alpha = pl.pallas_call(
            functools.partial(kernel, nx, ny, nz),
            out_shape=[jax.ShapeDtypeStruct(rhs.shape, F32)] * 4
            + [jax.ShapeDtypeStruct((cy, cz), F32)],
            in_specs=[hbm] * 4,
            out_specs=[hbm] * 4 + [pl.BlockSpec(memory_space=pltpu.VMEM)],
            scratch_shapes=[
                *[vmem(cx + 2, cy, cz) for _ in range(4)],
                vmem(STEPS, cx, cy, cz),
                vmem(cx, cy, cz),
                vmem(cx, cy, cz, dtype=i32),
                vmem(cx, cy, cz),
                vmem(cx, cy, cz),
                vmem(cx, cy, cz, dtype=i32),
                vmem(*coarse_inverse.shape),
                vmem(*coarse_inverse.shape),
                vmem(6, *coarse_inverse.shape),
                vmem(cx + 1, cy, cz),
                *[vmem(cx, cy, cz) for _ in range(4)],
                vmem(4, cx, cy, cz),
                vmem(2, cx, cz),
                vmem(2, 8, 128),
                vmem(4, cx, cy, cz),
                *[vmem(cx, cy, cz) for _ in range(2)],
                vmem(STEPS, 2, cy, cz),
                vmem(4, 2, cx, cz),
                vmem(4, 2, cx, cz),
                vmem(4, 2, 8, 128),
                vmem(4, 2, 2, 8, 128),
                vmem(2, cy, cz, dtype=i32),
                vmem(2, cx, cz, dtype=i32),
                vmem(2, cx, cz, dtype=i32),
                vmem(2, 8, 128, dtype=i32),
                vmem(2, 2, 8, 128, dtype=i32),
                vmem(2, 8, 128, dtype=i32),
                vmem(2, cy, cz),
                vmem(4, cx, cz),
                vmem(4, 8, 128),
                vmem(4, cx, cz),
                vmem(4, 8, 128),
                vmem(cx, 8, 128),
                vmem(cx, 8, 128, dtype=i32),
                vmem(cx, 8, 128),
                vmem(2, cx, cz),
                vmem(2 * nx, 128),
                vmem(ny * nz // 2, 2, 128),
                vmem(STEPS, 2 * nx, 6, 128),
                vmem(STEPS, ny * nz // 2, 9, 128),
                vmem(2 * nx, 128),
                vmem(ny * nz // 2, 128),
                pltpu.SemaphoreType.DMA((4,)),
                pltpu.SemaphoreType.DMA((4,)),
                pltpu.SemaphoreType.DMA((6, 6)),
                pltpu.SemaphoreType.DMA((6, 6)),
                pltpu.SemaphoreType.DMA((5, 2)),
                pltpu.SemaphoreType.DMA((5, 2)),
            ],
            compiler_params=pltpu.CompilerParams(
                collective_id=0, has_side_effects=True, vmem_limit_bytes=VMEM_BYTES
            ),
            name="deflated_cg",
        )(rhs, mobility, labels, coarse_inverse)
        return xs + alpha * p, rs - alpha * w

    spec = P("gx", "gz", "gy")
    return jax.shard_map(
        per_device,
        mesh=mesh,
        in_specs=(spec, spec, spec, P(("gx", "gy", "gz"), None)),
        out_specs=(spec, spec),
        check_vma=False,
    )
```

```python
import functools

import jax
import jax.numpy as jnp
from jax import lax
from jax.experimental import pallas as pl
from jax.experimental.pallas import tpu as pltpu
from jax.sharding import PartitionSpec as P

LOGICAL = pl.DeviceIdType.LOGICAL
F32 = jnp.float32
LOOP = 5
VMEM_BYTES = 64 * 1024 * 1024 - 256 * 1024

STEPS = 3
MOB, LAB, INV = range(STEPS, STEPS + 3)


def farthest_first(n):
    return sorted(range(n), key=lambda k: -min(k, n - k))


def kernel(
    nx,
    ny,
    nz,
    rhs_hbm,
    mob_hbm,
    lab_hbm,
    inv_hbm,
    x_hbm,
    p_hbm,
    r_hbm,
    w_hbm,
    step_out,
    mob,
    x0,
    field,
    direction,
    history,
    rhs_in,
    lab_in,
    mob_in,
    rhs,
    lab,
    inv_in,
    inv,
    inv_far,
    fx,
    fy,
    fz,
    dinv,
    rim,
    bits,
    fyb,
    fzp,
    ordered,
    rs,
    ws,
    xh,
    ys,
    yh,
    zs,
    zh,
    lxh,
    lys,
    lyh,
    lzs,
    lzh,
    lzf,
    yrim_x,
    yrim_y,
    yrim_z,
    prim_y,
    prim_z,
    zt,
    lt,
    et,
    ey,
    G1_first,
    G2_first,
    G1,
    G2,
    G1_last,
    G2_last,
    in_sem,
    out_sem,
    hs_sem,
    hr_sem,
    gs_sem,
    gr_sem,
):
    cx = rhs.shape[0]
    gx, gy, gz = lax.axis_index("gx"), lax.axis_index("gy"), lax.axis_index("gz")
    def logical(x, y, z):
        return (lax.rem(x, nx) * ny + lax.rem(y, ny)) * nz + lax.rem(z, nz)

    sides = (
        ("gx", gx > 0, logical(gx + nx - 1, gy, gz)),
        ("gx", gx < nx - 1, logical(gx + 1, gy, gz)),
        ("gz", gz > 0, logical(gx, gy, gz + nz - 1)),
        ("gz", gz < nz - 1, logical(gx, gy, gz + 1)),
        ("gy", gy > 0, logical(gx, gy + ny - 1, gz)),
        ("gy", gy < ny - 1, logical(gx, gy + 1, gz)),
    )

    loads = [
        pltpu.make_async_copy(rhs_hbm, rhs_in, in_sem.at[0]),
        pltpu.make_async_copy(lab_hbm, lab_in, in_sem.at[1]),
        pltpu.make_async_copy(mob_hbm, mob_in, in_sem.at[2]),
        pltpu.make_async_copy(inv_hbm, inv_in, in_sem.at[3]),
    ]
    for load in loads:
        load.start()

    barrier = pltpu.get_barrier_semaphore()
    chips = nz // 2
    chip, core = lax.div(gz, 2), lax.rem(gz, 2)
    line_peers = [
        logical(gx + k, gy, 2 * chip + lax.rem(core + c, 2))
        for k in farthest_first(nx)
        for c in (1, 0)
        if k or c
    ]
    plane_peers = [
        logical(gx, gy + j, gz + 2 * k)
        for j in farthest_first(ny)
        for k in farthest_first(chips)
        if j or k
    ]
    phases = ((core * nx + gx, line_peers), (gy * chips + chip, plane_peers))
    partners = line_peers + plane_peers + [logical(gx, gy, gz + nz - 1 + 2 * core)]
    for partner in partners:
        pl.semaphore_signal(barrier, inc=1, device_id=partner, device_id_type=LOGICAL)

    def clear(ref, *index):
        ref[index or Ellipsis] = jnp.zeros(ref.shape[len(index) :], ref.dtype)

    for low in range(2):

        @pl.when(gx == (nx - 1 if low else 0))
        def _():
            clear(mob, cx + 1 if low else 0)
            clear(lxh, low)
            for e in range(STEPS):
                clear(xh, e, low)

        @pl.when(gz == (nz - 1 if low else 0))
        def _():
            clear(lyh, low)
            for e in range(STEPS + 1):
                clear(yh, e, low)

        @pl.when(gy == (ny - 1 if low else 0))
        def _():
            clear(lzh, low)
            for e in range(STEPS + 1):
                clear(zh, e, low)

    clear(field, 0)
    clear(field, cx + 1)

    lane8 = lax.broadcasted_iota(jnp.int32, (8, 128), 1)
    row8 = lax.broadcasted_iota(jnp.int32, (8, 128), 0)
    lane16 = lax.broadcasted_iota(jnp.int32, (16, 128), 1)
    row16 = lax.broadcasted_iota(jnp.int32, (16, 128), 0)
    pair = ((lane8 + 1) >> 1) & 63
    ends = (lane8 == 0) | (lane8 == 127)
    even = (lane8 & 1) == 0
    zero = jnp.zeros((8, 128), F32)

    def interleaved(ref, x):
        return jnp.concatenate([ref[x, pl.ds(k, 8, stride=8), :] for k in range(8)], axis=0)

    def store_in_order(ref, x, plane):
        for k in range(8):
            ref[x, pl.ds(k, 8, stride=8), :] = plane[8 * k : 8 * k + 8]

    def next_row(plane):
        return jnp.concatenate([plane[8:], pltpu.roll(plane[:8], 7, 0)], axis=0)

    def last_row(plane):
        return jnp.concatenate([pltpu.roll(plane[56:], 1, 0), plane[:56]], axis=0)

    def fold(plane):
        tiles = [plane[k : k + 8] for k in range(0, plane.shape[0], 8)]
        while len(tiles) > 1:
            tiles = [a + b for a, b in zip(tiles[::2], tiles[1::2])]
        return tiles[0]

    def halo_copy(e, side):
        axis, _, index = sides[side]
        low, other = side & 1, 1 - (side & 1)
        kind = e if isinstance(e, int) else 0
        if kind == INV:
            src, dst = inv, inv_far.at[side ^ 1]
        elif kind == LAB:
            if axis == "gx":
                src, dst = lab.at[cx - 1 if low else 0], lxh.at[other]
            elif axis == "gz":
                src, dst = lys.at[low], lyh.at[other]
            else:
                src, dst = lzs, lzh.at[other]
        elif axis == "gx":
            src = (mob if kind == MOB else field).at[cx if low else 1]
            dst = mob.at[0 if low else cx + 1] if kind == MOB else xh.at[e, other]
        elif axis == "gz":
            src, dst = ys.at[e, low], yh.at[e, other]
        else:
            src, dst = zs.at[e], zh.at[e, other]
        return pltpu.make_async_remote_copy(
            src_ref=src,
            dst_ref=dst,
            send_sem=hs_sem.at[e, side],
            recv_sem=hr_sem.at[e, side ^ 1],
            device_id=index,
            device_id_type=LOGICAL,
        )

    def halo_landed(e, side):
        low = side & 1
        kind = e if isinstance(e, int) else 0
        if kind == INV:
            ref = inv_far.at[side]
        elif kind == LAB:
            ref = (lxh, lyh, lzh)[side // 2].at[low]
        elif side < 2:
            ref = mob.at[cx + 1 if low else 0] if kind == MOB else xh.at[e, low]
        else:
            ref = (yh, zh)[side // 2 - 1].at[e, low]
        return pltpu.make_async_copy(ref, ref, hr_sem.at[e, side])

    def exchange_start(e):
        for side in (0, 1, 4, 5, 2, 3):

            @pl.when(sides[side][1])
            def _():
                halo_copy(e, side).start()

    def exchange_wait(e):
        for side in range(6):

            @pl.when(sides[side][1])
            def _():
                halo_landed(e, side).wait()
                halo_copy(e, side).wait_send()

    def stage_rows(rows, x, plane):
        rows[0, pl.ds(x, 1), :] = plane[0:1]
        rows[1, pl.ds(x, 1), :] = plane[63:64]

    def pack_plane(plane):
        packed = plane[0:8]
        for k in range(1, 8):
            packed = jnp.where(pair == k, pltpu.roll(plane[8 * k : 8 * k + 8], 2 * k, 1), packed)
        return jnp.where(pair < 8, packed, jnp.zeros_like(packed))

    def pack_end(tiles, half):
        total = tiles[8 * half]
        for k in range(1, 8):
            total = total + pltpu.roll(tiles[8 * half + k], 16 * k, 1)
        return total

    def stage_plane(e, x, plane):
        stage_rows(ys.at[e], x, plane)
        zt[x] = pack_plane(plane)

    def stage_end(e):
        for half in range(2):
            zs[e, half] = pack_end(zt, half)

    def far(received, half):
        return jnp.where(
            even, pltpu.roll(received[0, half], 1, 1), pltpu.roll(received[1, half], 127, 1)
        )

    def spread(packed, half):
        et[8 * half] = packed
        for k in range(1, 8):
            et[8 * half + k] = pltpu.roll(packed, 128 - 16 * k, 1)

    def edge_part(x, v):
        return edge_tiles(x)

    def edge_tiles(x):
        tile = et[x]
        tiles = [
            jnp.where(ends, tile if k == 0 else pltpu.roll(tile, 128 - 2 * k, 1), 0.0)
            for k in range(8)
        ]
        first, last = ey[0, pl.ds(x, 1), :], ey[1, pl.ds(x, 1), :]
        tiles[0] = tiles[0] + jnp.where(row8 == 0, first, 0.0)
        tiles[7] = tiles[7] + jnp.where(row8 == 7, last, 0.0)
        return jnp.concatenate(tiles, axis=0)

    def apply_all(values, body, init, outer, make=None):
        def step(x, carry, above_v):
            below, v, rest = carry
            above = fx[x + 1] * (above_v - v)
            flux_y = fy[x] * (next_row(v) - v)
            flux_z = fz[x] * (pltpu.roll(v, 127, 1) - v)
            out = (
                (below - above)
                + (last_row(flux_y) - flux_y)
                + (pltpu.roll(flux_z, 1, 1) - flux_z)
                + outer(x, v)
            )
            return above, above_v, body(x, v, out, rest)

        if make is None:

            def make(x):
                return values[x + 1]

        v = make(0)
        carry = (fx[0] * (v - values[0]), v, init)
        carry = lax.fori_loop(
            0, cx - 1, lambda x, c: step(x, c, make(x + 1)), carry, unroll=LOOP
        )
        return step(cx - 1, carry, values[cx + 1])[2]

    def add_tile(sums, tile, tile_bits):
        terms = [tile]
        for bit in tile_bits:
            terms = terms + [term * bit for term in terms]
        return [total + term for total, term in zip(sums, terms)]

    def label_sums(sums):
        sums = list(sums)
        for i in range(4):
            for value in range(16):
                if not value >> i & 1:
                    sums[value] = sums[value] - sums[value | 1 << i]
        return sums

    def bits_of(labels):
        return [((labels >> i) & 1).astype(F32) for i in range(4)]

    def by_label(labels, values):
        sums = no_sums
        for k in range(0, values.shape[0], 8):
            sums = add_tile(sums, values[k : k + 8], bits_of(labels[k : k + 8]))
        return label_sums(sums)

    def restrict_plane(x, plane, sums):
        for k in range(0, 64, 8):
            tile_bits = [bits[i, x, k : k + 8] for i in range(4)]
            sums = add_tile(sums, plane[k : k + 8], tile_bits)
        return tuple(sums)

    def restrict_rhs(x, sums):
        for k in range(8):
            labels = lab_in[x, pl.ds(k, 8, stride=8), :]
            values = rhs_in[x, pl.ds(k, 8, stride=8), :]
            tile_bits = bits_of(labels)
            rows = slice(8 * k, 8 * k + 8)
            lab[x, rows] = labels
            rhs[x, rows] = values
            for i in range(4):
                bits[i, x, rows] = tile_bits[i]
            sums = add_tile(sums, values, tile_bits)
        return tuple(sums)

    no_sums = (zero,) * 16

    def rows_of(tiles):
        for shift in (4, 2, 1):
            low = (row8 & shift) == 0
            half = len(tiles) // 2
            merged = []
            for a, b in zip(tiles[:half], tiles[half:]):
                kept, moved = jnp.where(low, a, b), jnp.where(low, b, a)
                if shift == 4:
                    moved = pltpu.roll(moved, 4, 0)
                else:
                    moved = jnp.where(
                        low, pltpu.roll(moved, 8 - shift, 0), pltpu.roll(moved, shift, 0)
                    )
                merged.append(kept + moved)
            tiles = merged
        return tiles[0]

    def placed(sums, block):
        rows = jnp.concatenate([rows_of(list(sums[:8])), rows_of(list(sums[8:]))], axis=0)
        column = jnp.sum(rows, axis=1, keepdims=True)
        return fold(jnp.where(lane16 == 16 * block + row16, column, 0.0))

    def message(sums, parts, dots):
        tiles = [placed(sums, gx) + placed(parts[0], gx - 1) + placed(parts[1], gx + 1)]
        for side in (4, 5, 2, 3):
            tiles.append(placed(parts[side], gx))
        joined = zero
        for k, dot in enumerate(dots):
            dot = dot + pltpu.roll(dot, 64, 1)
            joined = jnp.where(lane8 >> 5 == k, dot + pltpu.roll(dot, 32, 1), joined)
        return rows_of(tiles + [joined, zero, zero])[:6]

    def neighbour_parts(e):
        parts = [
            by_label(lxh[0], -(fx[0] * field[1])),
            by_label(lxh[1], -(fx[cx] * field[cx])),
        ]
        for low in range(2):
            parts.append(by_label(lyh[low], -(fyb[low] * ys[e, low])))
        for keep in (even, ~even):
            halves = [
                by_label(lzf[half], jnp.where(keep, -(fzp[half] * zs[e, half]), 0.0))
                for half in range(2)
            ]
            parts.append([a + b for a, b in zip(*halves)])
        return parts

    def coarse_right_side(e):
        sums = apply_all(
            field, lambda x, v, out, s: restrict_plane(x, out, s), no_sums, lambda x, v: rim[x] * v
        )
        return label_sums(sums), neighbour_parts(e)

    def slots_of(g, ph):
        if isinstance(g, int):
            return ((G1_first, G2_first), (G1_last, G2_last))[g != 0][ph]
        return (G1, G2)[ph].at[g - 1]

    def phase_slots(g, ph, first, count):
        slots = slots_of(g, ph)
        return slots.at[pl.ds(first, count)]

    def phase_start(g, ph):
        me, peers = phases[ph]
        slot = phase_slots(g, ph, me, 1)
        for peer in peers:
            pltpu.make_async_remote_copy(
                src_ref=slot,
                dst_ref=slot,
                send_sem=gs_sem.at[g, ph],
                recv_sem=gr_sem.at[g, ph],
                device_id=peer,
                device_id_type=LOGICAL,
            ).start()

    def phase_wait(g, ph):
        part = phase_slots(g, ph, 0, len(phases[ph][1]))
        pltpu.make_async_copy(part, part, gr_sem.at[g, ph]).wait()
        pltpu.make_async_copy(part, part, gs_sem.at[g, ph]).wait()

    def gather(g, tile, started, between):
        G1[g - 1, phases[0][0]] = tile
        phase_start(g, 0)
        started()
        phase_wait(g, 0)
        low, high = [jnp.sum(G1[g - 1, nx * c : nx * (c + 1)], axis=0) for c in range(2)]
        slot = phases[1][0]
        rows = [
            low[0:1] + high[3:4],
            high[0:1] + low[4:5],
            low[1:2],
            high[1:2],
            low[2:3],
            high[2:3],
            low[3:4],
            high[4:5],
            low[5:6] + high[5:6],
        ]
        for k, row in enumerate(rows):
            G2[g - 1, slot, k : k + 1] = row
        phase_start(g, 1)
        between()
        phase_wait(g, 1)

    def dots_of(g):
        row = jnp.sum(G2[g - 1, :, 8:9], axis=0)
        lane = lax.broadcasted_iota(jnp.int32, (1, 128), 1)
        return [
            jnp.broadcast_to(
                jnp.sum(jnp.where(lane >> 5 == k, row, 0.0), axis=1, keepdims=True), (1, 128)
            )
            for k in range(3)
        ]

    def right_side(g):
        def row(slot, k):
            if isinstance(g, int):
                return jnp.broadcast_to(G2_first[slot, k : k + 1], (8, 128))
            return jnp.broadcast_to(G2[g - 1, slot, k : k + 1], (8, 128))

        rows = [[None] * ny for _ in range(nz)]
        for j in range(ny):
            for k in range(chips):
                slot = j * chips + k
                for c in range(2):
                    total = row(slot, c)
                    if not isinstance(g, int):
                        if j + 1 < ny:
                            total = total + row(slot + chips, 2 + c)
                        if j > 0:
                            total = total + row(slot - chips, 4 + c)
                        if c == 0 and k > 0:
                            total = total + row(slot - 1, 7)
                        if c == 1 and k + 1 < chips:
                            total = total + row(slot + 1, 6)
                    rows[2 * k + c][j] = total
        return rows

    def coarse(g):
        accs = [jnp.zeros((16, 128), F32) for _ in range(7)]
        for i, rows in enumerate(right_side(g)):
            for j in range(ny):
                columns = slice((i * ny + j) * 128, (i * ny + j + 1) * 128)
                row = jnp.concatenate([rows[j], rows[j]], axis=0)
                accs[6] = accs[6] + inv[:, columns] * row
                for side in range(6):
                    accs[side] = accs[side] + inv_far[side, :, columns] * row
        values = []
        for side in range(7):
            total = jnp.broadcast_to(jnp.sum(accs[side], axis=1, keepdims=True), (16, 128))
            if side < 6:
                index = row16 * 0 + (gx, gz, gy)[side // 2]
                edge = (0, (nx, nz, ny)[side // 2] - 1)[side & 1]
                total = jnp.where(index == edge, 0.0, total)
            values.append(total)
        return values

    def splats_of(values):
        return [jnp.broadcast_to(values[m : m + 1], (8, 128)) for m in range(16)]

    def pick(splats, masks):
        if len(splats) == 1:
            return splats[0]
        half = len(splats) // 2
        return jnp.where(
            masks[-1], pick(splats[half:], masks[:-1]), pick(splats[:half], masks[:-1])
        )

    def masks_of(labels):
        return [labels & (1 << i) != 0 for i in range(4)]

    def take(splats, labels):
        tiles = [
            pick(splats, masks_of(labels[k : k + 8])) for k in range(0, labels.shape[0], 8)
        ]
        return jnp.concatenate(tiles, axis=0)

    def take_plane(splats, x):
        tiles = [
            pick(splats, [bits[i, x, k : k + 8] > 0.5 for i in range(4)]) for k in range(0, 64, 8)
        ]
        return jnp.concatenate(tiles, axis=0)

    def rim_of(values):
        splats = [splats_of(value) for value in values]
        x_far = [take(splats[low], lxh[low]) for low in range(2)]
        y_own = [take(splats[6], lys[low]) for low in range(2)]
        y_far = [take(splats[2 + low], lyh[low]) for low in range(2)]
        z_own = [take(splats[6], lzs[half]) for half in range(2)]
        z_far = [
            jnp.where(even, take(splats[4], lzf[half]), take(splats[5], lzf[half]))
            for half in range(2)
        ]
        return x_far, y_own, y_far, z_own, z_far

    def outer_faces(y_own, y_far, z_own, z_far):
        for low in range(2):
            ey[low] = fyb[low] * (y_own[low] - y_far[low])
        for half in range(2):
            spread(fzp[half] * (z_own[half] - z_far[half]), half)

    def order_columns():
        for top in (0, 8):
            for j in range(ny):
                tiles = [inv_in[top : top + 8, pl.ds((i * ny + j) * 128, 128)] for i in range(nx)]
                for s in (4, 2, 1):
                    clear_bit = (lane8 >> 4) & s == 0
                    for i in range(nx):
                        if not i & s:
                            a, b = tiles[i], tiles[i | s]
                            tiles[i] = jnp.where(clear_bit, a, pltpu.roll(b, 16 * s, 1))
                            tiles[i | s] = jnp.where(clear_bit, pltpu.roll(a, 128 - 16 * s, 1), b)
                for i in range(nz):
                    inv[top : top + 8, pl.ds((i * ny + j) * 128, 128)] = tiles[i]

    def stage_static(x, carry):
        mobility = interleaved(mob_in, x)
        mob[x + 1] = mobility
        stage_plane(MOB, x, mobility)
        labels = lab[x]
        stage_rows(lys, x, labels)
        lt[x] = pack_plane(labels)
        return carry

    loads[0].wait()
    loads[1].wait()
    sums = lax.fori_loop(0, cx, restrict_rhs, no_sums, unroll=4)
    line = jnp.sum(placed(label_sums(sums), gx), axis=0, keepdims=True)
    loads[3].wait()
    order_columns()
    loads[2].wait()
    lax.fori_loop(0, cx, stage_static, 0, unroll=4)
    stage_end(MOB)
    for half in range(2):
        lzs[half] = pack_end(lt, half)
    pl.semaphore_wait(barrier, len(partners))
    G1_first[pl.ds(phases[0][0], 1), :] = line
    phase_start(0, 0)
    exchange_start(MOB)
    exchange_start(LAB)
    exchange_start(INV)

    def faces():
        for ref in (direction, ws, yrim_x, yrim_y, yrim_z, prim_y, prim_z):
            clear(ref)
        exchange_wait(MOB)
        exchange_wait(LAB)
        for half in range(2):
            lzf[half] = far(lzh, half)
            fzp[half] = 0.5 * (zs[MOB, half] + far(zh.at[MOB], half))
            spread(fzp[half], half)
        for low in range(2):
            fyb[low] = 0.5 * (ys[MOB, low] + yh[MOB, low])
            ey[low] = fyb[low]
        fx[0] = 0.5 * (mob[1] + mob[0])
        row = lax.broadcasted_iota(jnp.int32, (64, 128), 0)
        lane = lax.broadcasted_iota(jnp.int32, (64, 128), 1)

        def step(x, below):
            m = mob[x + 1]
            above = 0.5 * (mob[x + 2] + m)
            face_y = jnp.where(row == 63, 0.0, 0.5 * (next_row(m) + m))
            face_z = jnp.where(lane == 127, 0.0, 0.5 * (pltpu.roll(m, 127, 1) + m))
            edges = edge_tiles(x)
            diag = (
                (below + above)
                + (last_row(face_y) + face_y)
                + (pltpu.roll(face_z, 1, 1) + face_z)
                + edges
            )
            rim[x] = edges
            fx[x + 1] = above
            fy[x] = face_y
            fz[x] = face_z
            dinv[x] = 1.0 / diag
            return above

        lax.fori_loop(0, cx, step, fx[0], unroll=4)

    phase_wait(0, 0)
    G2_first[phases[1][0]] = jnp.concatenate(
        [jnp.sum(G1_first[nx * c : nx * (c + 1)], axis=0, keepdims=True) for c in range(2)], axis=0
    )
    phase_start(0, 1)
    faces()
    phase_wait(0, 1)

    exchange_wait(INV)
    lines = coarse(0)

    own_splats = splats_of(lines[6])

    def first_iterate(x):
        plane = take_plane(own_splats, x)
        x0[x + 1] = plane
        return plane

    x_far, *rest = rim_of(lines)
    x0[0] = x_far[0]
    x0[cx + 1] = x_far[1]
    outer_faces(*rest)

    def first_residual(x, v, out, dot):
        residual = rhs[x] - out
        precond = residual * dinv[x]
        rs[x] = residual
        field[x + 1] = precond
        stage_plane(0, x, precond)
        return dot + fold(residual * precond)

    ry_part = apply_all(x0, first_residual, zero, edge_part, first_iterate)
    stage_end(0)

    def tall(row):
        return jnp.broadcast_to(row, (8, 128))

    def one_step(k, carry):
        ry, lines, dots, _, last_alpha = carry
        ry = ry[0:1]
        sums, parts = coarse_right_side(k)
        gather(
            k + 1,
            message(sums, parts, dots),
            lambda: exchange_start(k),
            lambda: exchange_wait(k),
        )
        more = coarse(k + 1)
        d0, d1, d2 = dots_of(k + 1)
        first = lax.broadcasted_iota(jnp.int32, (1, 128), 0) + k == 0
        alpha = jnp.where(first, 0.0, ry / d0)
        ry_next = jnp.where(first, d0, ry + alpha * (alpha * d2 - 2.0 * d1))
        beta = jnp.where(first, 0.0, ry_next / ry)
        gain = jnp.where(first, 1.0, -alpha)
        lines = [line + gain * extra for line, extra in zip(lines, more)]

        x_far, y_own, y_far, z_own, z_far = rim_of(lines)
        for low in range(2):
            outer = cx + 1 if low else 0
            layer = yrim_x[low] + gain * xh[k, low]
            yrim_x[low] = layer
            direction[outer] = (layer + beta * direction[outer]) - x_far[low]
        rows = [ys[k, 0], ys[k, 1], yh[k, 0], yh[k, 1]]
        packs = [zs[k, 0], zs[k, 1], far(zh.at[k], 0), far(zh.at[k], 1)]
        for i, (y_part, z_part) in enumerate(zip(y_own + y_far, z_own + z_far)):
            row = yrim_y[i] + gain * rows[i]
            pack = yrim_z[i] + gain * packs[i]
            yrim_y[i] = row
            yrim_z[i] = pack
            prim_y[i] = (row + beta * prim_y[i]) - y_part
            prim_z[i] = (pack + beta * prim_z[i]) - z_part
        outer_faces(
            [prim_y[0], prim_y[1]],
            [prim_y[2], prim_y[3]],
            [prim_z[0], prim_z[1]],
            [prim_z[2], prim_z[3]],
        )

        splats = splats_of(lines[6])

        def next_direction(x):
            residual = rs[x] - alpha * ws[x]
            rs[x] = residual
            plane = (residual * dinv[x] + beta * direction[x + 1]) - take_plane(splats, x)
            direction[x + 1] = plane
            history[k, x] = plane
            return plane

        def image(x, v, out, dots):
            z = out * dinv[x]
            ws[x] = out
            field[x + 1] = z
            stage_plane(k + 1, x, z)
            return (
                dots[0] + fold(v * out),
                dots[1] + fold(rs[x] * z),
                dots[2] + fold(out * z),
            )

        dots = apply_all(direction, image, (zero, zero, zero), edge_part, next_direction)
        stage_end(k + 1)
        return tall(ry_next), lines, dots, last_alpha, tall(alpha)

    ry, _, dots, *alphas = lax.fori_loop(
        0, STEPS, one_step, (zero + 1.0, [jnp.zeros((16, 128), F32)] * 7, (ry_part, zero, zero), zero, zero)
    )
    ry, alphas = ry[0:1], [alpha[0:1] for alpha in alphas]

    stores = [
        pltpu.make_async_copy(ordered.at[i], out, out_sem.at[i])
        for i, out in enumerate((x_hbm, p_hbm, r_hbm, w_hbm))
    ]
    G1_last[pl.ds(phases[0][0], 1), :] = jnp.sum(dots[0], axis=0, keepdims=True)
    phase_start(STEPS + 1, 0)

    def join_iterate(x, carry):
        joined = (x0[x + 1] + alphas[0] * history[0, x]) + alphas[1] * history[1, x]
        for i, plane in enumerate((joined, history[STEPS - 1, x], rs[x], ws[x])):
            store_in_order(ordered.at[i], x, plane)
        return carry

    lax.fori_loop(0, cx, join_iterate, 0, unroll=4)
    for store in stores:
        store.start()
    phase_wait(STEPS + 1, 0)
    G2_last[pl.ds(phases[1][0], 1), :] = jnp.sum(G1_last[...], axis=0, keepdims=True)
    phase_start(STEPS + 1, 1)
    phase_wait(STEPS + 1, 1)
    total = jnp.sum(jnp.sum(G2_last[...], axis=0, keepdims=True), axis=1, keepdims=True)
    step_out[...] = jnp.broadcast_to(ry / total, step_out.shape)
    for store in stores:
        store.wait()


def solution(mesh):
    nx, ny, nz = mesh.shape["gx"], mesh.shape["gy"], mesh.shape["gz"]

    def per_device(rhs, mobility, labels, coarse_inverse):
        cx, cy, cz = rhs.shape
        hbm = pl.BlockSpec(memory_space=pl.ANY)

        def vmem(*shape, dtype=F32):
            return pltpu.VMEM(shape, dtype)

        i32 = jnp.int32
        xs, p, rs, w, alpha = pl.pallas_call(
            functools.partial(kernel, nx, ny, nz),
            out_shape=[jax.ShapeDtypeStruct(rhs.shape, F32)] * 4
            + [jax.ShapeDtypeStruct((cy, cz), F32)],
            in_specs=[hbm] * 4,
            out_specs=[hbm] * 4 + [pl.BlockSpec(memory_space=pltpu.VMEM)],
            scratch_shapes=[
                *[vmem(cx + 2, cy, cz) for _ in range(4)],
                vmem(STEPS, cx, cy, cz),
                vmem(cx, cy, cz),
                vmem(cx, cy, cz, dtype=i32),
                vmem(cx, cy, cz),
                vmem(cx, cy, cz),
                vmem(cx, cy, cz, dtype=i32),
                vmem(*coarse_inverse.shape),
                vmem(*coarse_inverse.shape),
                vmem(6, *coarse_inverse.shape),
                vmem(cx + 1, cy, cz),
                *[vmem(cx, cy, cz) for _ in range(4)],
                vmem(4, cx, cy, cz),
                vmem(2, cx, cz),
                vmem(2, 8, 128),
                vmem(4, cx, cy, cz),
                *[vmem(cx, cy, cz) for _ in range(2)],
                vmem(STEPS, 2, cy, cz),
                vmem(4, 2, cx, cz),
                vmem(4, 2, cx, cz),
                vmem(4, 2, 8, 128),
                vmem(4, 2, 2, 8, 128),
                vmem(2, cy, cz, dtype=i32),
                vmem(2, cx, cz, dtype=i32),
                vmem(2, cx, cz, dtype=i32),
                vmem(2, 8, 128, dtype=i32),
                vmem(2, 2, 8, 128, dtype=i32),
                vmem(2, 8, 128, dtype=i32),
                vmem(2, cy, cz),
                vmem(4, cx, cz),
                vmem(4, 8, 128),
                vmem(4, cx, cz),
                vmem(4, 8, 128),
                vmem(cx, 8, 128),
                vmem(cx, 8, 128, dtype=i32),
                vmem(cx, 8, 128),
                vmem(2, cx, cz),
                vmem(2 * nx, 128),
                vmem(ny * nz // 2, 2, 128),
                vmem(STEPS, 2 * nx, 6, 128),
                vmem(STEPS, ny * nz // 2, 9, 128),
                vmem(2 * nx, 128),
                vmem(ny * nz // 2, 128),
                pltpu.SemaphoreType.DMA((4,)),
                pltpu.SemaphoreType.DMA((4,)),
                pltpu.SemaphoreType.DMA((6, 6)),
                pltpu.SemaphoreType.DMA((6, 6)),
                pltpu.SemaphoreType.DMA((5, 2)),
                pltpu.SemaphoreType.DMA((5, 2)),
            ],
            compiler_params=pltpu.CompilerParams(
                collective_id=0, has_side_effects=True, vmem_limit_bytes=VMEM_BYTES
            ),
            name="deflated_cg",
        )(rhs, mobility, labels, coarse_inverse)
        return xs + alpha * p, rs - alpha * w

    spec = P("gx", "gz", "gy")
    return jax.shard_map(
        per_device,
        mesh=mesh,
        in_specs=(spec, spec, spec, P(("gx", "gy", "gz"), None)),
        out_specs=(spec, spec),
        check_vma=False,
    )
```

```python
import functools

import jax
import jax.numpy as jnp
from jax import lax
from jax.experimental import pallas as pl
from jax.experimental.pallas import tpu as pltpu
from jax.sharding import PartitionSpec as P

LOGICAL = pl.DeviceIdType.LOGICAL
F32 = jnp.float32
LOOP = 5
VMEM_BYTES = 64 * 1024 * 1024 - 256 * 1024

STEPS = 3
MOB, LAB, INV = range(STEPS, STEPS + 3)


def farthest_first(n):
    return sorted(range(n), key=lambda k: -min(k, n - k))


def kernel(
    nx,
    ny,
    nz,
    rhs_hbm,
    mob_hbm,
    lab_hbm,
    inv_hbm,
    x_hbm,
    p_hbm,
    r_hbm,
    w_hbm,
    step_out,
    mob,
    x0,
    field,
    direction,
    history,
    rhs_in,
    lab_in,
    mob_in,
    rhs,
    lab,
    inv_in,
    inv,
    inv_far,
    fx,
    fy,
    fz,
    dinv,
    rim,
    bits,
    fyb,
    fzp,
    ordered,
    rs,
    ws,
    xh,
    ys,
    yh,
    zs,
    zh,
    lxh,
    lys,
    lyh,
    lzs,
    lzh,
    lzf,
    yrim_x,
    yrim_y,
    yrim_z,
    prim_y,
    prim_z,
    zt,
    lt,
    et,
    ey,
    G1_first,
    G2_first,
    G1,
    G2,
    G1_last,
    G2_last,
    in_sem,
    out_sem,
    hs_sem,
    hr_sem,
    gs_sem,
    gr_sem,
):
    cx = rhs.shape[0]
    gx, gy, gz = lax.axis_index("gx"), lax.axis_index("gy"), lax.axis_index("gz")
    def logical(x, y, z):
        return (lax.rem(x, nx) * ny + lax.rem(y, ny)) * nz + lax.rem(z, nz)

    sides = (
        ("gx", gx > 0, logical(gx + nx - 1, gy, gz)),
        ("gx", gx < nx - 1, logical(gx + 1, gy, gz)),
        ("gz", gz > 0, logical(gx, gy, gz + nz - 1)),
        ("gz", gz < nz - 1, logical(gx, gy, gz + 1)),
        ("gy", gy > 0, logical(gx, gy + ny - 1, gz)),
        ("gy", gy < ny - 1, logical(gx, gy + 1, gz)),
    )

    loads = [
        pltpu.make_async_copy(rhs_hbm, rhs_in, in_sem.at[0]),
        pltpu.make_async_copy(lab_hbm, lab_in, in_sem.at[1]),
        pltpu.make_async_copy(mob_hbm, mob_in, in_sem.at[2]),
        pltpu.make_async_copy(inv_hbm, inv_in, in_sem.at[3]),
    ]
    for load in loads:
        load.start()

    barrier = pltpu.get_barrier_semaphore()
    chips = nz // 2
    chip, core = lax.div(gz, 2), lax.rem(gz, 2)
    line_peers = [
        logical(gx + k, gy, 2 * chip + lax.rem(core + c, 2))
        for k in farthest_first(nx)
        for c in (1, 0)
        if k or c
    ]
    plane_peers = [
        logical(gx, gy + j, gz + 2 * k)
        for j in farthest_first(ny)
        for k in farthest_first(chips)
        if j or k
    ]
    phases = ((core * nx + gx, line_peers), (gy * chips + chip, plane_peers))
    partners = line_peers + plane_peers + [logical(gx, gy, gz + nz - 1 + 2 * core)]
    for partner in partners:
        pl.semaphore_signal(barrier, inc=1, device_id=partner, device_id_type=LOGICAL)

    def clear(ref, *index):
        ref[index or Ellipsis] = jnp.zeros(ref.shape[len(index) :], ref.dtype)

    for low in range(2):

        @pl.when(gx == (nx - 1 if low else 0))
        def _():
            clear(mob, cx + 1 if low else 0)
            clear(lxh, low)
            for e in range(STEPS):
                clear(xh, e, low)

        @pl.when(gz == (nz - 1 if low else 0))
        def _():
            clear(lyh, low)
            for e in range(STEPS + 1):
                clear(yh, e, low)

        @pl.when(gy == (ny - 1 if low else 0))
        def _():
            clear(lzh, low)
            for e in range(STEPS + 1):
                clear(zh, e, low)

    clear(field, 0)
    clear(field, cx + 1)

    lane8 = lax.broadcasted_iota(jnp.int32, (8, 128), 1)
    row8 = lax.broadcasted_iota(jnp.int32, (8, 128), 0)
    lane16 = lax.broadcasted_iota(jnp.int32, (16, 128), 1)
    row16 = lax.broadcasted_iota(jnp.int32, (16, 128), 0)
    pair = ((lane8 + 1) >> 1) & 63
    ends = (lane8 == 0) | (lane8 == 127)
    even = (lane8 & 1) == 0
    zero = jnp.zeros((8, 128), F32)

    def interleaved(ref, x):
        return jnp.concatenate([ref[x, pl.ds(k, 8, stride=8), :] for k in range(8)], axis=0)

    def store_in_order(ref, x, plane):
        for k in range(8):
            ref[x, pl.ds(k, 8, stride=8), :] = plane[8 * k : 8 * k + 8]

    def next_row(plane):
        return jnp.concatenate([plane[8:], pltpu.roll(plane[:8], 7, 0)], axis=0)

    def last_row(plane):
        return jnp.concatenate([pltpu.roll(plane[56:], 1, 0), plane[:56]], axis=0)

    def fold(plane):
        tiles = [plane[k : k + 8] for k in range(0, plane.shape[0], 8)]
        while len(tiles) > 1:
            tiles = [a + b for a, b in zip(tiles[::2], tiles[1::2])]
        return tiles[0]

    def halo_copy(e, side):
        axis, _, index = sides[side]
        low, other = side & 1, 1 - (side & 1)
        kind = e if isinstance(e, int) else 0
        if kind == INV:
            src, dst = inv, inv_far.at[side ^ 1]
        elif kind == LAB:
            if axis == "gx":
                src, dst = lab.at[cx - 1 if low else 0], lxh.at[other]
            elif axis == "gz":
                src, dst = lys.at[low], lyh.at[other]
            else:
                src, dst = lzs, lzh.at[other]
        elif axis == "gx":
            src = (mob if kind == MOB else field).at[cx if low else 1]
            dst = mob.at[0 if low else cx + 1] if kind == MOB else xh.at[e, other]
        elif axis == "gz":
            src, dst = ys.at[e, low], yh.at[e, other]
        else:
            src, dst = zs.at[e], zh.at[e, other]
        return pltpu.make_async_remote_copy(
            src_ref=src,
            dst_ref=dst,
            send_sem=hs_sem.at[e, side],
            recv_sem=hr_sem.at[e, side ^ 1],
            device_id=index,
            device_id_type=LOGICAL,
        )

    def halo_landed(e, side):
        low = side & 1
        kind = e if isinstance(e, int) else 0
        if kind == INV:
            ref = inv_far.at[side]
        elif kind == LAB:
            ref = (lxh, lyh, lzh)[side // 2].at[low]
        elif side < 2:
            ref = mob.at[cx + 1 if low else 0] if kind == MOB else xh.at[e, low]
        else:
            ref = (yh, zh)[side // 2 - 1].at[e, low]
        return pltpu.make_async_copy(ref, ref, hr_sem.at[e, side])

    def exchange_start(e):
        for side in (0, 1, 4, 5, 2, 3):

            @pl.when(sides[side][1])
            def _():
                halo_copy(e, side).start()

    def exchange_wait(e):
        for side in range(6):

            @pl.when(sides[side][1])
            def _():
                halo_landed(e, side).wait()
                halo_copy(e, side).wait_send()

    def stage_rows(rows, x, plane):
        rows[0, pl.ds(x, 1), :] = plane[0:1]
        rows[1, pl.ds(x, 1), :] = plane[63:64]

    def pack_plane(plane):
        packed = plane[0:8]
        for k in range(1, 8):
            packed = jnp.where(pair == k, pltpu.roll(plane[8 * k : 8 * k + 8], 2 * k, 1), packed)
        return jnp.where(pair < 8, packed, jnp.zeros_like(packed))

    def pack_end(tiles, half):
        total = tiles[8 * half]
        for k in range(1, 8):
            total = total + pltpu.roll(tiles[8 * half + k], 16 * k, 1)
        return total

    def stage_plane(e, x, plane):
        stage_rows(ys.at[e], x, plane)
        zt[x] = pack_plane(plane)

    def stage_end(e):
        for half in range(2):
            zs[e, half] = pack_end(zt, half)

    def far(received, half):
        return jnp.where(
            even, pltpu.roll(received[0, half], 1, 1), pltpu.roll(received[1, half], 127, 1)
        )

    def spread(packed, half):
        et[8 * half] = packed
        for k in range(1, 8):
            et[8 * half + k] = pltpu.roll(packed, 128 - 16 * k, 1)

    def edge_tile(x, k):
        tile = et[x]
        tile = jnp.where(ends, pltpu.roll(tile, 128 - 2 * k, 1) if k else tile, 0.0)
        if k == 0:
            tile = tile + jnp.where(row8 == 0, ey[0, pl.ds(x, 1), :], 0.0)
        if k == 7:
            tile = tile + jnp.where(row8 == 7, ey[1, pl.ds(x, 1), :], 0.0)
        return tile

    def edge_part(x, k, v):
        return edge_tile(x, k)

    def edge_tiles(x):
        return jnp.concatenate([edge_tile(x, k) for k in range(8)], axis=0)

    def apply_all(values, body, init, outer, make=None, stage=None):
        def step(x, carry, above_v):
            below, v, rest = carry
            tiles = [v[8 * k : 8 * k + 8] for k in range(8)]
            last = fy[x, 56:64] * (pltpu.roll(tiles[0], 7, 0) - tiles[7])
            flux_below = pltpu.roll(last, 1, 0)
            aboves = []
            for k in range(8):
                rows = slice(8 * k, 8 * k + 8)
                tile = tiles[k]
                above = fx[x + 1, rows] * (above_v[rows] - tile)
                flux_y = fy[x, rows] * (tiles[k + 1] - tile) if k < 7 else last
                flux_z = fz[x, rows] * (pltpu.roll(tile, 127, 1) - tile)
                out = (
                    (below[rows] - above)
                    + (flux_below - flux_y)
                    + (pltpu.roll(flux_z, 1, 1) - flux_z)
                    + outer(x, k, tile)
                )
                flux_below = flux_y
                aboves.append(above)
                rest = body(x, k, tile, out, rest)
            if stage is not None:
                stage_plane(stage, x, field[x + 1])
            return jnp.concatenate(aboves, axis=0), above_v, rest

        if make is None:

            def make(x):
                return values[x + 1]

        v = make(0)
        carry = (fx[0] * (v - values[0]), v, init)
        carry = lax.fori_loop(
            0, cx - 1, lambda x, c: step(x, c, make(x + 1)), carry, unroll=LOOP
        )
        return step(cx - 1, carry, values[cx + 1])[2]

    def add_tile(sums, tile, tile_bits):
        terms = [tile]
        for bit in tile_bits:
            terms = terms + [term * bit for term in terms]
        return [total + term for total, term in zip(sums, terms)]

    def label_sums(sums):
        sums = list(sums)
        for i in range(4):
            for value in range(16):
                if not value >> i & 1:
                    sums[value] = sums[value] - sums[value | 1 << i]
        return sums

    def bits_of(labels):
        return [((labels >> i) & 1).astype(F32) for i in range(4)]

    def by_label(labels, values):
        sums = no_sums
        for k in range(0, values.shape[0], 8):
            sums = add_tile(sums, values[k : k + 8], bits_of(labels[k : k + 8]))
        return label_sums(sums)

    def restrict_tile(x, k, tile, sums):
        rows = slice(8 * k, 8 * k + 8)
        return tuple(add_tile(sums, tile, [bits[i, x, rows] for i in range(4)]))

    def restrict_rhs(x, sums):
        for k in range(8):
            labels = lab_in[x, pl.ds(k, 8, stride=8), :]
            values = rhs_in[x, pl.ds(k, 8, stride=8), :]
            tile_bits = bits_of(labels)
            rows = slice(8 * k, 8 * k + 8)
            lab[x, rows] = labels
            rhs[x, rows] = values
            for i in range(4):
                bits[i, x, rows] = tile_bits[i]
            sums = add_tile(sums, values, tile_bits)
        return tuple(sums)

    no_sums = (zero,) * 16

    def rows_of(tiles):
        for shift in (4, 2, 1):
            low = (row8 & shift) == 0
            half = len(tiles) // 2
            merged = []
            for a, b in zip(tiles[:half], tiles[half:]):
                kept, moved = jnp.where(low, a, b), jnp.where(low, b, a)
                if shift == 4:
                    moved = pltpu.roll(moved, 4, 0)
                else:
                    moved = jnp.where(
                        low, pltpu.roll(moved, 8 - shift, 0), pltpu.roll(moved, shift, 0)
                    )
                merged.append(kept + moved)
            tiles = merged
        return tiles[0]

    def placed(sums, block):
        rows = jnp.concatenate([rows_of(list(sums[:8])), rows_of(list(sums[8:]))], axis=0)
        column = jnp.sum(rows, axis=1, keepdims=True)
        return fold(jnp.where(lane16 == 16 * block + row16, column, 0.0))

    def message(sums, parts, dots):
        tiles = [placed(sums, gx) + placed(parts[0], gx - 1) + placed(parts[1], gx + 1)]
        for side in (4, 5, 2, 3):
            tiles.append(placed(parts[side], gx))
        joined = zero
        for k, dot in enumerate(dots):
            dot = dot + pltpu.roll(dot, 64, 1)
            joined = jnp.where(lane8 >> 5 == k, dot + pltpu.roll(dot, 32, 1), joined)
        return rows_of(tiles + [joined, zero, zero])[:6]

    def neighbour_parts(e):
        parts = [
            by_label(lxh[0], -(fx[0] * field[1])),
            by_label(lxh[1], -(fx[cx] * field[cx])),
        ]
        for low in range(2):
            parts.append(by_label(lyh[low], -(fyb[low] * ys[e, low])))
        for keep in (even, ~even):
            halves = [
                by_label(lzf[half], jnp.where(keep, -(fzp[half] * zs[e, half]), 0.0))
                for half in range(2)
            ]
            parts.append([a + b for a, b in zip(*halves)])
        return parts

    def coarse_right_side(e):
        sums = apply_all(
            field,
            lambda x, k, v, out, s: restrict_tile(x, k, out, s),
            no_sums,
            lambda x, k, v: rim[x, 8 * k : 8 * k + 8] * v,
        )
        return label_sums(sums), neighbour_parts(e)

    def slots_of(g, ph):
        if isinstance(g, int):
            return ((G1_first, G2_first), (G1_last, G2_last))[g != 0][ph]
        return (G1, G2)[ph].at[g - 1]

    def phase_slots(g, ph, first, count):
        slots = slots_of(g, ph)
        return slots.at[pl.ds(first, count)]

    def phase_start(g, ph):
        me, peers = phases[ph]
        slot = phase_slots(g, ph, me, 1)
        for peer in peers:
            pltpu.make_async_remote_copy(
                src_ref=slot,
                dst_ref=slot,
                send_sem=gs_sem.at[g, ph],
                recv_sem=gr_sem.at[g, ph],
                device_id=peer,
                device_id_type=LOGICAL,
            ).start()

    def phase_wait(g, ph):
        part = phase_slots(g, ph, 0, len(phases[ph][1]))
        pltpu.make_async_copy(part, part, gr_sem.at[g, ph]).wait()
        pltpu.make_async_copy(part, part, gs_sem.at[g, ph]).wait()

    def gather(g, tile, started, between):
        G1[g - 1, phases[0][0]] = tile
        phase_start(g, 0)
        started()
        phase_wait(g, 0)
        low, high = [jnp.sum(G1[g - 1, nx * c : nx * (c + 1)], axis=0) for c in range(2)]
        slot = phases[1][0]
        rows = [
            low[0:1] + high[3:4],
            high[0:1] + low[4:5],
            low[1:2],
            high[1:2],
            low[2:3],
            high[2:3],
            low[3:4],
            high[4:5],
            low[5:6] + high[5:6],
        ]
        for k, row in enumerate(rows):
            G2[g - 1, slot, k : k + 1] = row
        phase_start(g, 1)
        between()
        phase_wait(g, 1)

    def dots_of(g):
        row = jnp.sum(G2[g - 1, :, 8:9], axis=0)
        lane = lax.broadcasted_iota(jnp.int32, (1, 128), 1)
        return [
            jnp.broadcast_to(
                jnp.sum(jnp.where(lane >> 5 == k, row, 0.0), axis=1, keepdims=True), (1, 128)
            )
            for k in range(3)
        ]

    def right_side(g):
        def row(slot, k):
            if isinstance(g, int):
                return jnp.broadcast_to(G2_first[slot, k : k + 1], (8, 128))
            return jnp.broadcast_to(G2[g - 1, slot, k : k + 1], (8, 128))

        rows = [[None] * ny for _ in range(nz)]
        for j in range(ny):
            for k in range(chips):
                slot = j * chips + k
                for c in range(2):
                    total = row(slot, c)
                    if not isinstance(g, int):
                        if j + 1 < ny:
                            total = total + row(slot + chips, 2 + c)
                        if j > 0:
                            total = total + row(slot - chips, 4 + c)
                        if c == 0 and k > 0:
                            total = total + row(slot - 1, 7)
                        if c == 1 and k + 1 < chips:
                            total = total + row(slot + 1, 6)
                    rows[2 * k + c][j] = total
        return rows

    def coarse(g):
        accs = [jnp.zeros((16, 128), F32) for _ in range(7)]
        for i, rows in enumerate(right_side(g)):
            for j in range(ny):
                columns = slice((i * ny + j) * 128, (i * ny + j + 1) * 128)
                row = jnp.concatenate([rows[j], rows[j]], axis=0)
                accs[6] = accs[6] + inv[:, columns] * row
                for side in range(6):
                    accs[side] = accs[side] + inv_far[side, :, columns] * row
        values = []
        for side in range(7):
            total = jnp.broadcast_to(jnp.sum(accs[side], axis=1, keepdims=True), (16, 128))
            if side < 6:
                index = row16 * 0 + (gx, gz, gy)[side // 2]
                edge = (0, (nx, nz, ny)[side // 2] - 1)[side & 1]
                total = jnp.where(index == edge, 0.0, total)
            values.append(total)
        return values

    def splats_of(values):
        return [jnp.broadcast_to(values[m : m + 1], (8, 128)) for m in range(16)]

    def pick(splats, masks):
        if len(splats) == 1:
            return splats[0]
        half = len(splats) // 2
        return jnp.where(
            masks[-1], pick(splats[half:], masks[:-1]), pick(splats[:half], masks[:-1])
        )

    def masks_of(labels):
        return [labels & (1 << i) != 0 for i in range(4)]

    def take(splats, labels):
        tiles = [
            pick(splats, masks_of(labels[k : k + 8])) for k in range(0, labels.shape[0], 8)
        ]
        return jnp.concatenate(tiles, axis=0)

    def take_plane(splats, x):
        tiles = [
            pick(splats, [bits[i, x, k : k + 8] > 0.5 for i in range(4)]) for k in range(0, 64, 8)
        ]
        return jnp.concatenate(tiles, axis=0)

    def rim_of(values):
        splats = [splats_of(value) for value in values]
        x_far = [take(splats[low], lxh[low]) for low in range(2)]
        y_own = [take(splats[6], lys[low]) for low in range(2)]
        y_far = [take(splats[2 + low], lyh[low]) for low in range(2)]
        z_own = [take(splats[6], lzs[half]) for half in range(2)]
        z_far = [
            jnp.where(even, take(splats[4], lzf[half]), take(splats[5], lzf[half]))
            for half in range(2)
        ]
        return x_far, y_own, y_far, z_own, z_far

    def outer_faces(y_own, y_far, z_own, z_far):
        for low in range(2):
            ey[low] = fyb[low] * (y_own[low] - y_far[low])
        for half in range(2):
            spread(fzp[half] * (z_own[half] - z_far[half]), half)

    def order_columns():
        for top in (0, 8):
            for j in range(ny):
                tiles = [inv_in[top : top + 8, pl.ds((i * ny + j) * 128, 128)] for i in range(nx)]
                for s in (4, 2, 1):
                    clear_bit = (lane8 >> 4) & s == 0
                    for i in range(nx):
                        if not i & s:
                            a, b = tiles[i], tiles[i | s]
                            tiles[i] = jnp.where(clear_bit, a, pltpu.roll(b, 16 * s, 1))
                            tiles[i | s] = jnp.where(clear_bit, pltpu.roll(a, 128 - 16 * s, 1), b)
                for i in range(nz):
                    inv[top : top + 8, pl.ds((i * ny + j) * 128, 128)] = tiles[i]

    def stage_static(x, carry):
        mobility = interleaved(mob_in, x)
        mob[x + 1] = mobility
        stage_plane(MOB, x, mobility)
        labels = lab[x]
        stage_rows(lys, x, labels)
        lt[x] = pack_plane(labels)
        return carry

    loads[0].wait()
    loads[1].wait()
    sums = lax.fori_loop(0, cx, restrict_rhs, no_sums, unroll=4)
    line = jnp.sum(placed(label_sums(sums), gx), axis=0, keepdims=True)
    loads[3].wait()
    order_columns()
    loads[2].wait()
    lax.fori_loop(0, cx, stage_static, 0, unroll=4)
    stage_end(MOB)
    for half in range(2):
        lzs[half] = pack_end(lt, half)
    pl.semaphore_wait(barrier, len(partners))
    G1_first[pl.ds(phases[0][0], 1), :] = line
    phase_start(0, 0)
    exchange_start(MOB)
    exchange_start(LAB)
    exchange_start(INV)

    def faces():
        for ref in (direction, ws, yrim_x, yrim_y, yrim_z, prim_y, prim_z):
            clear(ref)
        exchange_wait(MOB)
        exchange_wait(LAB)
        for half in range(2):
            lzf[half] = far(lzh, half)
            fzp[half] = 0.5 * (zs[MOB, half] + far(zh.at[MOB], half))
            spread(fzp[half], half)
        for low in range(2):
            fyb[low] = 0.5 * (ys[MOB, low] + yh[MOB, low])
            ey[low] = fyb[low]
        fx[0] = 0.5 * (mob[1] + mob[0])
        row = lax.broadcasted_iota(jnp.int32, (64, 128), 0)
        lane = lax.broadcasted_iota(jnp.int32, (64, 128), 1)

        def step(x, below):
            m = mob[x + 1]
            above = 0.5 * (mob[x + 2] + m)
            face_y = jnp.where(row == 63, 0.0, 0.5 * (next_row(m) + m))
            face_z = jnp.where(lane == 127, 0.0, 0.5 * (pltpu.roll(m, 127, 1) + m))
            edges = edge_tiles(x)
            diag = (
                (below + above)
                + (last_row(face_y) + face_y)
                + (pltpu.roll(face_z, 1, 1) + face_z)
                + edges
            )
            rim[x] = edges
            fx[x + 1] = above
            fy[x] = face_y
            fz[x] = face_z
            dinv[x] = 1.0 / diag
            return above

        lax.fori_loop(0, cx, step, fx[0], unroll=4)

    phase_wait(0, 0)
    G2_first[phases[1][0]] = jnp.concatenate(
        [jnp.sum(G1_first[nx * c : nx * (c + 1)], axis=0, keepdims=True) for c in range(2)], axis=0
    )
    phase_start(0, 1)
    faces()
    phase_wait(0, 1)

    exchange_wait(INV)
    lines = coarse(0)

    own_splats = splats_of(lines[6])

    def first_iterate(x):
        plane = take_plane(own_splats, x)
        x0[x + 1] = plane
        return plane

    x_far, *rest = rim_of(lines)
    x0[0] = x_far[0]
    x0[cx + 1] = x_far[1]
    outer_faces(*rest)

    def first_residual(x, k, v, out, dot):
        rows = slice(8 * k, 8 * k + 8)
        residual = rhs[x, rows] - out
        precond = residual * dinv[x, rows]
        rs[x, rows] = residual
        field[x + 1, rows] = precond
        return dot + residual * precond

    ry_part = apply_all(x0, first_residual, zero, edge_part, first_iterate, 0)
    stage_end(0)

    def tall(row):
        return jnp.broadcast_to(row, (8, 128))

    def one_step(k, carry):
        ry, lines, dots, _, last_alpha = carry
        ry = ry[0:1]
        sums, parts = coarse_right_side(k)
        gather(
            k + 1,
            message(sums, parts, dots),
            lambda: exchange_start(k),
            lambda: exchange_wait(k),
        )
        more = coarse(k + 1)
        d0, d1, d2 = dots_of(k + 1)
        first = lax.broadcasted_iota(jnp.int32, (1, 128), 0) + k == 0
        alpha = jnp.where(first, 0.0, ry / d0)
        ry_next = jnp.where(first, d0, ry + alpha * (alpha * d2 - 2.0 * d1))
        beta = jnp.where(first, 0.0, ry_next / ry)
        gain = jnp.where(first, 1.0, -alpha)
        lines = [line + gain * extra for line, extra in zip(lines, more)]

        x_far, y_own, y_far, z_own, z_far = rim_of(lines)
        for low in range(2):
            outer = cx + 1 if low else 0
            layer = yrim_x[low] + gain * xh[k, low]
            yrim_x[low] = layer
            direction[outer] = (layer + beta * direction[outer]) - x_far[low]
        rows = [ys[k, 0], ys[k, 1], yh[k, 0], yh[k, 1]]
        packs = [zs[k, 0], zs[k, 1], far(zh.at[k], 0), far(zh.at[k], 1)]
        for i, (y_part, z_part) in enumerate(zip(y_own + y_far, z_own + z_far)):
            row = yrim_y[i] + gain * rows[i]
            pack = yrim_z[i] + gain * packs[i]
            yrim_y[i] = row
            yrim_z[i] = pack
            prim_y[i] = (row + beta * prim_y[i]) - y_part
            prim_z[i] = (pack + beta * prim_z[i]) - z_part
        outer_faces(
            [prim_y[0], prim_y[1]],
            [prim_y[2], prim_y[3]],
            [prim_z[0], prim_z[1]],
            [prim_z[2], prim_z[3]],
        )

        splats = splats_of(lines[6])

        def next_direction(x):
            residual = rs[x] - alpha * ws[x]
            rs[x] = residual
            plane = (residual * dinv[x] + beta * direction[x + 1]) - take_plane(splats, x)
            direction[x + 1] = plane
            history[k, x] = plane
            return plane

        def image(x, i, v, out, dots):
            rows = slice(8 * i, 8 * i + 8)
            z = out * dinv[x, rows]
            ws[x, rows] = out
            field[x + 1, rows] = z
            return dots[0] + v * out, dots[1] + rs[x, rows] * z, dots[2] + out * z

        dots = apply_all(direction, image, (zero, zero, zero), edge_part, next_direction, k + 1)
        stage_end(k + 1)
        return tall(ry_next), lines, dots, last_alpha, tall(alpha)

    ry, _, dots, *alphas = lax.fori_loop(
        0, STEPS, one_step, (zero + 1.0, [jnp.zeros((16, 128), F32)] * 7, (ry_part, zero, zero), zero, zero)
    )
    ry, alphas = ry[0:1], [alpha[0:1] for alpha in alphas]

    stores = [
        pltpu.make_async_copy(ordered.at[i], out, out_sem.at[i])
        for i, out in enumerate((x_hbm, p_hbm, r_hbm, w_hbm))
    ]
    G1_last[pl.ds(phases[0][0], 1), :] = jnp.sum(dots[0], axis=0, keepdims=True)
    phase_start(STEPS + 1, 0)

    def join_iterate(x, carry):
        joined = (x0[x + 1] + alphas[0] * history[0, x]) + alphas[1] * history[1, x]
        for i, plane in enumerate((joined, history[STEPS - 1, x], rs[x], ws[x])):
            store_in_order(ordered.at[i], x, plane)
        return carry

    lax.fori_loop(0, cx, join_iterate, 0, unroll=4)
    for store in stores:
        store.start()
    phase_wait(STEPS + 1, 0)
    G2_last[pl.ds(phases[1][0], 1), :] = jnp.sum(G1_last[...], axis=0, keepdims=True)
    phase_start(STEPS + 1, 1)
    phase_wait(STEPS + 1, 1)
    total = jnp.sum(jnp.sum(G2_last[...], axis=0, keepdims=True), axis=1, keepdims=True)
    step_out[...] = jnp.broadcast_to(ry / total, step_out.shape)
    for store in stores:
        store.wait()


def solution(mesh):
    nx, ny, nz = mesh.shape["gx"], mesh.shape["gy"], mesh.shape["gz"]

    def per_device(rhs, mobility, labels, coarse_inverse):
        cx, cy, cz = rhs.shape
        hbm = pl.BlockSpec(memory_space=pl.ANY)

        def vmem(*shape, dtype=F32):
            return pltpu.VMEM(shape, dtype)

        i32 = jnp.int32
        xs, p, rs, w, alpha = pl.pallas_call(
            functools.partial(kernel, nx, ny, nz),
            out_shape=[jax.ShapeDtypeStruct(rhs.shape, F32)] * 4
            + [jax.ShapeDtypeStruct((cy, cz), F32)],
            in_specs=[hbm] * 4,
            out_specs=[hbm] * 4 + [pl.BlockSpec(memory_space=pltpu.VMEM)],
            scratch_shapes=[
                *[vmem(cx + 2, cy, cz) for _ in range(4)],
                vmem(STEPS, cx, cy, cz),
                vmem(cx, cy, cz),
                vmem(cx, cy, cz, dtype=i32),
                vmem(cx, cy, cz),
                vmem(cx, cy, cz),
                vmem(cx, cy, cz, dtype=i32),
                vmem(*coarse_inverse.shape),
                vmem(*coarse_inverse.shape),
                vmem(6, *coarse_inverse.shape),
                vmem(cx + 1, cy, cz),
                *[vmem(cx, cy, cz) for _ in range(4)],
                vmem(4, cx, cy, cz),
                vmem(2, cx, cz),
                vmem(2, 8, 128),
                vmem(4, cx, cy, cz),
                *[vmem(cx, cy, cz) for _ in range(2)],
                vmem(STEPS, 2, cy, cz),
                vmem(4, 2, cx, cz),
                vmem(4, 2, cx, cz),
                vmem(4, 2, 8, 128),
                vmem(4, 2, 2, 8, 128),
                vmem(2, cy, cz, dtype=i32),
                vmem(2, cx, cz, dtype=i32),
                vmem(2, cx, cz, dtype=i32),
                vmem(2, 8, 128, dtype=i32),
                vmem(2, 2, 8, 128, dtype=i32),
                vmem(2, 8, 128, dtype=i32),
                vmem(2, cy, cz),
                vmem(4, cx, cz),
                vmem(4, 8, 128),
                vmem(4, cx, cz),
                vmem(4, 8, 128),
                vmem(cx, 8, 128),
                vmem(cx, 8, 128, dtype=i32),
                vmem(cx, 8, 128),
                vmem(2, cx, cz),
                vmem(2 * nx, 128),
                vmem(ny * nz // 2, 2, 128),
                vmem(STEPS, 2 * nx, 6, 128),
                vmem(STEPS, ny * nz // 2, 9, 128),
                vmem(2 * nx, 128),
                vmem(ny * nz // 2, 128),
                pltpu.SemaphoreType.DMA((4,)),
                pltpu.SemaphoreType.DMA((4,)),
                pltpu.SemaphoreType.DMA((6, 6)),
                pltpu.SemaphoreType.DMA((6, 6)),
                pltpu.SemaphoreType.DMA((5, 2)),
                pltpu.SemaphoreType.DMA((5, 2)),
            ],
            compiler_params=pltpu.CompilerParams(
                collective_id=0, has_side_effects=True, vmem_limit_bytes=VMEM_BYTES
            ),
            name="deflated_cg",
        )(rhs, mobility, labels, coarse_inverse)
        return xs + alpha * p, rs - alpha * w

    spec = P("gx", "gz", "gy")
    return jax.shard_map(
        per_device,
        mesh=mesh,
        in_specs=(spec, spec, spec, P(("gx", "gy", "gz"), None)),
        out_specs=(spec, spec),
        check_vma=False,
    )
```

```python
import functools

import jax
import jax.numpy as jnp
from jax import lax
from jax.experimental import pallas as pl
from jax.experimental.pallas import tpu as pltpu
from jax.sharding import PartitionSpec as P

LOGICAL = pl.DeviceIdType.LOGICAL
F32 = jnp.float32
LOOP = 3
VMEM_BYTES = 64 * 1024 * 1024 - 256 * 1024

STEPS = 3
MOB, LAB, INV = range(STEPS, STEPS + 3)


def farthest_first(n):
    return sorted(range(n), key=lambda k: -min(k, n - k))


def kernel(
    nx,
    ny,
    nz,
    rhs_hbm,
    mob_hbm,
    lab_hbm,
    inv_hbm,
    x_hbm,
    p_hbm,
    r_hbm,
    w_hbm,
    step_out,
    mob,
    x0,
    field,
    direction,
    history,
    rhs_in,
    lab_in,
    mob_in,
    rhs,
    lab,
    inv_in,
    inv,
    inv_far,
    fx,
    fy,
    fz,
    dinv,
    rim,
    bits,
    fyb,
    fzp,
    ordered,
    rs,
    ws,
    xh,
    ys,
    yh,
    zs,
    zh,
    lxh,
    lys,
    lyh,
    lzs,
    lzh,
    lzf,
    yrim_x,
    yrim_y,
    yrim_z,
    prim_y,
    prim_z,
    zt,
    lt,
    et,
    ey,
    G1_first,
    G2_first,
    G1,
    G2,
    G1_last,
    G2_last,
    in_sem,
    out_sem,
    hs_sem,
    hr_sem,
    gs_sem,
    gr_sem,
):
    cx = rhs.shape[0]
    gx, gy, gz = lax.axis_index("gx"), lax.axis_index("gy"), lax.axis_index("gz")
    def logical(x, y, z):
        return (lax.rem(x, nx) * ny + lax.rem(y, ny)) * nz + lax.rem(z, nz)

    sides = (
        ("gx", gx > 0, logical(gx + nx - 1, gy, gz)),
        ("gx", gx < nx - 1, logical(gx + 1, gy, gz)),
        ("gz", gz > 0, logical(gx, gy, gz + nz - 1)),
        ("gz", gz < nz - 1, logical(gx, gy, gz + 1)),
        ("gy", gy > 0, logical(gx, gy + ny - 1, gz)),
        ("gy", gy < ny - 1, logical(gx, gy + 1, gz)),
    )

    loads = [
        pltpu.make_async_copy(rhs_hbm, rhs_in, in_sem.at[0]),
        pltpu.make_async_copy(lab_hbm, lab_in, in_sem.at[1]),
        pltpu.make_async_copy(mob_hbm, mob_in, in_sem.at[2]),
        pltpu.make_async_copy(inv_hbm, inv_in, in_sem.at[3]),
    ]
    for load in loads:
        load.start()

    barrier = pltpu.get_barrier_semaphore()
    chips = nz // 2
    chip, core = lax.div(gz, 2), lax.rem(gz, 2)
    line_peers = [
        logical(gx + k, gy, 2 * chip + lax.rem(core + c, 2))
        for k in farthest_first(nx)
        for c in (1, 0)
        if k or c
    ]
    plane_peers = [
        logical(gx, gy + j, gz + 2 * k)
        for j in farthest_first(ny)
        for k in farthest_first(chips)
        if j or k
    ]
    phases = ((core * nx + gx, line_peers), (gy * chips + chip, plane_peers))
    partners = line_peers + plane_peers + [logical(gx, gy, gz + nz - 1 + 2 * core)]
    for partner in partners:
        pl.semaphore_signal(barrier, inc=1, device_id=partner, device_id_type=LOGICAL)

    def clear(ref, *index):
        ref[index or Ellipsis] = jnp.zeros(ref.shape[len(index) :], ref.dtype)

    for low in range(2):

        @pl.when(gx == (nx - 1 if low else 0))
        def _():
            clear(mob, cx + 1 if low else 0)
            clear(lxh, low)
            for e in range(STEPS):
                clear(xh, e, low)

        @pl.when(gz == (nz - 1 if low else 0))
        def _():
            clear(lyh, low)
            for e in range(STEPS + 1):
                clear(yh, e, low)

        @pl.when(gy == (ny - 1 if low else 0))
        def _():
            clear(lzh, low)
            for e in range(STEPS + 1):
                clear(zh, e, low)

    clear(field, 0)
    clear(field, cx + 1)

    lane8 = lax.broadcasted_iota(jnp.int32, (8, 128), 1)
    row8 = lax.broadcasted_iota(jnp.int32, (8, 128), 0)
    lane16 = lax.broadcasted_iota(jnp.int32, (16, 128), 1)
    row16 = lax.broadcasted_iota(jnp.int32, (16, 128), 0)
    pair = ((lane8 + 1) >> 1) & 63
    ends = (lane8 == 0) | (lane8 == 127)
    even = (lane8 & 1) == 0
    zero = jnp.zeros((8, 128), F32)

    def interleaved(ref, x):
        return jnp.concatenate([ref[x, pl.ds(k, 8, stride=8), :] for k in range(8)], axis=0)

    def store_in_order(ref, x, plane):
        for k in range(8):
            ref[x, pl.ds(k, 8, stride=8), :] = plane[8 * k : 8 * k + 8]

    def next_row(plane):
        return jnp.concatenate([plane[8:], pltpu.roll(plane[:8], 7, 0)], axis=0)

    def last_row(plane):
        return jnp.concatenate([pltpu.roll(plane[56:], 1, 0), plane[:56]], axis=0)

    def fold(plane):
        tiles = [plane[k : k + 8] for k in range(0, plane.shape[0], 8)]
        while len(tiles) > 1:
            tiles = [a + b for a, b in zip(tiles[::2], tiles[1::2])]
        return tiles[0]

    def halo_copy(e, side):
        axis, _, index = sides[side]
        low, other = side & 1, 1 - (side & 1)
        kind = e if isinstance(e, int) else 0
        if kind == INV:
            src, dst = inv, inv_far.at[side ^ 1]
        elif kind == LAB:
            if axis == "gx":
                src, dst = lab.at[cx - 1 if low else 0], lxh.at[other]
            elif axis == "gz":
                src, dst = lys.at[low], lyh.at[other]
            else:
                src, dst = lzs, lzh.at[other]
        elif axis == "gx":
            src = (mob if kind == MOB else field).at[cx if low else 1]
            dst = mob.at[0 if low else cx + 1] if kind == MOB else xh.at[e, other]
        elif axis == "gz":
            src, dst = ys.at[e, low], yh.at[e, other]
        else:
            src, dst = zs.at[e], zh.at[e, other]
        return pltpu.make_async_remote_copy(
            src_ref=src,
            dst_ref=dst,
            send_sem=hs_sem.at[e, side],
            recv_sem=hr_sem.at[e, side ^ 1],
            device_id=index,
            device_id_type=LOGICAL,
        )

    def halo_landed(e, side):
        low = side & 1
        kind = e if isinstance(e, int) else 0
        if kind == INV:
            ref = inv_far.at[side]
        elif kind == LAB:
            ref = (lxh, lyh, lzh)[side // 2].at[low]
        elif side < 2:
            ref = mob.at[cx + 1 if low else 0] if kind == MOB else xh.at[e, low]
        else:
            ref = (yh, zh)[side // 2 - 1].at[e, low]
        return pltpu.make_async_copy(ref, ref, hr_sem.at[e, side])

    def exchange_start(e):
        for side in (0, 1, 4, 5, 2, 3):

            @pl.when(sides[side][1])
            def _():
                halo_copy(e, side).start()

    def exchange_wait(e):
        for side in range(6):

            @pl.when(sides[side][1])
            def _():
                halo_landed(e, side).wait()
                halo_copy(e, side).wait_send()

    def stage_rows(rows, x, plane):
        rows[0, pl.ds(x, 1), :] = plane[0:1]
        rows[1, pl.ds(x, 1), :] = plane[63:64]

    def pack_plane(plane):
        packed = plane[0:8]
        for k in range(1, 8):
            packed = jnp.where(pair == k, pltpu.roll(plane[8 * k : 8 * k + 8], 2 * k, 1), packed)
        return jnp.where(pair < 8, packed, jnp.zeros_like(packed))

    def pack_end(tiles, half):
        total = tiles[8 * half]
        for k in range(1, 8):
            total = total + pltpu.roll(tiles[8 * half + k], 16 * k, 1)
        return total

    def stage_plane(e, x, plane):
        stage_rows(ys.at[e], x, plane)
        zt[x] = pack_plane(plane)

    def stage_end(e):
        for half in range(2):
            zs[e, half] = pack_end(zt, half)

    def far(received, half):
        return jnp.where(
            even, pltpu.roll(received[0, half], 1, 1), pltpu.roll(received[1, half], 127, 1)
        )

    def spread(packed, half):
        et[8 * half] = packed
        for k in range(1, 8):
            et[8 * half + k] = pltpu.roll(packed, 128 - 16 * k, 1)

    def edge_tile(x, k):
        tile = et[x]
        tile = jnp.where(ends, pltpu.roll(tile, 128 - 2 * k, 1) if k else tile, 0.0)
        if k == 0:
            tile = tile + jnp.where(row8 == 0, ey[0, pl.ds(x, 1), :], 0.0)
        if k == 7:
            tile = tile + jnp.where(row8 == 7, ey[1, pl.ds(x, 1), :], 0.0)
        return tile

    def edge_part(x, k, v):
        return edge_tile(x, k)

    def edge_tiles(x):
        return jnp.concatenate([edge_tile(x, k) for k in range(8)], axis=0)

    def apply_all(values, body, init, outer, make=None, stage=None):
        def step(x, carry, above_v):
            below, v, rest = carry
            tiles = [v[8 * k : 8 * k + 8] for k in range(8)]
            last = fy[x, 56:64] * (pltpu.roll(tiles[0], 7, 0) - tiles[7])
            flux_below = pltpu.roll(last, 1, 0)
            aboves = []
            for k in range(8):
                rows = slice(8 * k, 8 * k + 8)
                tile = tiles[k]
                above = fx[x + 1, rows] * (above_v[rows] - tile)
                flux_y = fy[x, rows] * (tiles[k + 1] - tile) if k < 7 else last
                flux_z = fz[x, rows] * (pltpu.roll(tile, 127, 1) - tile)
                out = (
                    (below[rows] - above)
                    + (flux_below - flux_y)
                    + (pltpu.roll(flux_z, 1, 1) - flux_z)
                    + outer(x, k, tile)
                )
                flux_below = flux_y
                aboves.append(above)
                rest = body(x, k, tile, out, rest)
            if stage is not None:
                stage_plane(stage, x, field[x + 1])
            return jnp.concatenate(aboves, axis=0), above_v, rest

        if make is None:

            def make(x):
                return values[x + 1]

        v = make(0)
        carry = (fx[0] * (v - values[0]), v, init)
        carry = lax.fori_loop(
            0, cx - 1, lambda x, c: step(x, c, make(x + 1)), carry, unroll=LOOP
        )
        return step(cx - 1, carry, values[cx + 1])[2]

    def add_tile(sums, tile, tile_bits):
        terms = [tile]
        for bit in tile_bits:
            terms = terms + [term * bit for term in terms]
        return [total + term for total, term in zip(sums, terms)]

    def label_sums(sums):
        sums = list(sums)
        for i in range(4):
            for value in range(16):
                if not value >> i & 1:
                    sums[value] = sums[value] - sums[value | 1 << i]
        return sums

    def bits_of(labels):
        return [((labels >> i) & 1).astype(F32) for i in range(4)]

    def by_label(labels, values):
        sums = no_sums
        for k in range(0, values.shape[0], 8):
            sums = add_tile(sums, values[k : k + 8], bits_of(labels[k : k + 8]))
        return label_sums(sums)

    def restrict_tile(x, k, tile, sums):
        rows = slice(8 * k, 8 * k + 8)
        return tuple(add_tile(sums, tile, [bits[i, x, rows] for i in range(4)]))

    def restrict_rhs(x, sums):
        for k in range(8):
            labels = lab_in[x, pl.ds(k, 8, stride=8), :]
            values = rhs_in[x, pl.ds(k, 8, stride=8), :]
            tile_bits = bits_of(labels)
            rows = slice(8 * k, 8 * k + 8)
            lab[x, rows] = labels
            rhs[x, rows] = values
            for i in range(4):
                bits[i, x, rows] = tile_bits[i]
            sums = add_tile(sums, values, tile_bits)
        return tuple(sums)

    no_sums = (zero,) * 16

    def rows_of(tiles):
        for shift in (4, 2, 1):
            low = (row8 & shift) == 0
            half = len(tiles) // 2
            merged = []
            for a, b in zip(tiles[:half], tiles[half:]):
                kept, moved = jnp.where(low, a, b), jnp.where(low, b, a)
                if shift == 4:
                    moved = pltpu.roll(moved, 4, 0)
                else:
                    moved = jnp.where(
                        low, pltpu.roll(moved, 8 - shift, 0), pltpu.roll(moved, shift, 0)
                    )
                merged.append(kept + moved)
            tiles = merged
        return tiles[0]

    def placed(sums, block):
        rows = jnp.concatenate([rows_of(list(sums[:8])), rows_of(list(sums[8:]))], axis=0)
        column = jnp.sum(rows, axis=1, keepdims=True)
        return fold(jnp.where(lane16 == 16 * block + row16, column, 0.0))

    def message(sums, parts, dots):
        tiles = [placed(sums, gx) + placed(parts[0], gx - 1) + placed(parts[1], gx + 1)]
        for side in (4, 5, 2, 3):
            tiles.append(placed(parts[side], gx))
        joined = zero
        for k, dot in enumerate(dots):
            dot = dot + pltpu.roll(dot, 64, 1)
            joined = jnp.where(lane8 >> 5 == k, dot + pltpu.roll(dot, 32, 1), joined)
        return rows_of(tiles + [joined, zero, zero])[:6]

    def neighbour_parts(e):
        parts = [
            by_label(lxh[0], -(fx[0] * field[1])),
            by_label(lxh[1], -(fx[cx] * field[cx])),
        ]
        for low in range(2):
            parts.append(by_label(lyh[low], -(fyb[low] * ys[e, low])))
        for keep in (even, ~even):
            halves = [
                by_label(lzf[half], jnp.where(keep, -(fzp[half] * zs[e, half]), 0.0))
                for half in range(2)
            ]
            parts.append([a + b for a, b in zip(*halves)])
        return parts

    def coarse_right_side(e):
        sums = apply_all(
            field,
            lambda x, k, v, out, s: restrict_tile(x, k, out, s),
            no_sums,
            lambda x, k, v: rim[x, 8 * k : 8 * k + 8] * v,
        )
        return label_sums(sums), neighbour_parts(e)

    def slots_of(g, ph):
        if isinstance(g, int):
            return ((G1_first, G2_first), (G1_last, G2_last))[g != 0][ph]
        return (G1, G2)[ph].at[g - 1]

    def phase_slots(g, ph, first, count):
        slots = slots_of(g, ph)
        return slots.at[pl.ds(first, count)]

    def phase_start(g, ph):
        me, peers = phases[ph]
        slot = phase_slots(g, ph, me, 1)
        for peer in peers:
            pltpu.make_async_remote_copy(
                src_ref=slot,
                dst_ref=slot,
                send_sem=gs_sem.at[g, ph],
                recv_sem=gr_sem.at[g, ph],
                device_id=peer,
                device_id_type=LOGICAL,
            ).start()

    def phase_wait(g, ph):
        part = phase_slots(g, ph, 0, len(phases[ph][1]))
        pltpu.make_async_copy(part, part, gr_sem.at[g, ph]).wait()
        pltpu.make_async_copy(part, part, gs_sem.at[g, ph]).wait()

    def gather(g, tile, started, between):
        G1[g - 1, phases[0][0]] = tile
        phase_start(g, 0)
        started()
        phase_wait(g, 0)
        low, high = [jnp.sum(G1[g - 1, nx * c : nx * (c + 1)], axis=0) for c in range(2)]
        slot = phases[1][0]
        rows = [
            low[0:1] + high[3:4],
            high[0:1] + low[4:5],
            low[1:2],
            high[1:2],
            low[2:3],
            high[2:3],
            low[3:4],
            high[4:5],
            low[5:6] + high[5:6],
        ]
        for k, row in enumerate(rows):
            G2[g - 1, slot, k : k + 1] = row
        phase_start(g, 1)
        between()
        phase_wait(g, 1)

    def dots_of(g):
        row = jnp.sum(G2[g - 1, :, 8:9], axis=0)
        lane = lax.broadcasted_iota(jnp.int32, (1, 128), 1)
        return [
            jnp.broadcast_to(
                jnp.sum(jnp.where(lane >> 5 == k, row, 0.0), axis=1, keepdims=True), (1, 128)
            )
            for k in range(3)
        ]

    def right_side(g):
        def row(slot, k):
            if isinstance(g, int):
                return jnp.broadcast_to(G2_first[slot, k : k + 1], (8, 128))
            return jnp.broadcast_to(G2[g - 1, slot, k : k + 1], (8, 128))

        rows = [[None] * ny for _ in range(nz)]
        for j in range(ny):
            for k in range(chips):
                slot = j * chips + k
                for c in range(2):
                    total = row(slot, c)
                    if not isinstance(g, int):
                        if j + 1 < ny:
                            total = total + row(slot + chips, 2 + c)
                        if j > 0:
                            total = total + row(slot - chips, 4 + c)
                        if c == 0 and k > 0:
                            total = total + row(slot - 1, 7)
                        if c == 1 and k + 1 < chips:
                            total = total + row(slot + 1, 6)
                    rows[2 * k + c][j] = total
        return rows

    def coarse(g):
        accs = [jnp.zeros((16, 128), F32) for _ in range(7)]
        for i, rows in enumerate(right_side(g)):
            for j in range(ny):
                columns = slice((i * ny + j) * 128, (i * ny + j + 1) * 128)
                row = jnp.concatenate([rows[j], rows[j]], axis=0)
                accs[6] = accs[6] + inv[:, columns] * row
                for side in range(6):
                    accs[side] = accs[side] + inv_far[side, :, columns] * row
        values = []
        for side in range(7):
            total = jnp.broadcast_to(jnp.sum(accs[side], axis=1, keepdims=True), (16, 128))
            if side < 6:
                index = row16 * 0 + (gx, gz, gy)[side // 2]
                edge = (0, (nx, nz, ny)[side // 2] - 1)[side & 1]
                total = jnp.where(index == edge, 0.0, total)
            values.append(total)
        return values

    def splats_of(values):
        return [jnp.broadcast_to(values[m : m + 1], (8, 128)) for m in range(16)]

    def pick(splats, masks):
        if len(splats) == 1:
            return splats[0]
        half = len(splats) // 2
        return jnp.where(
            masks[-1], pick(splats[half:], masks[:-1]), pick(splats[:half], masks[:-1])
        )

    def masks_of(labels):
        return [labels & (1 << i) != 0 for i in range(4)]

    def take(splats, labels):
        tiles = [
            pick(splats, masks_of(labels[k : k + 8])) for k in range(0, labels.shape[0], 8)
        ]
        return jnp.concatenate(tiles, axis=0)

    def take_plane(splats, x):
        tiles = [
            pick(splats, [bits[i, x, k : k + 8] > 0.5 for i in range(4)]) for k in range(0, 64, 8)
        ]
        return jnp.concatenate(tiles, axis=0)

    def rim_of(values):
        splats = [splats_of(value) for value in values]
        x_far = [take(splats[low], lxh[low]) for low in range(2)]
        y_own = [take(splats[6], lys[low]) for low in range(2)]
        y_far = [take(splats[2 + low], lyh[low]) for low in range(2)]
        z_own = [take(splats[6], lzs[half]) for half in range(2)]
        z_far = [
            jnp.where(even, take(splats[4], lzf[half]), take(splats[5], lzf[half]))
            for half in range(2)
        ]
        return x_far, y_own, y_far, z_own, z_far

    def outer_faces(y_own, y_far, z_own, z_far):
        for low in range(2):
            ey[low] = fyb[low] * (y_own[low] - y_far[low])
        for half in range(2):
            spread(fzp[half] * (z_own[half] - z_far[half]), half)

    def order_columns():
        for top in (0, 8):
            for j in range(ny):
                tiles = [inv_in[top : top + 8, pl.ds((i * ny + j) * 128, 128)] for i in range(nx)]
                for s in (4, 2, 1):
                    clear_bit = (lane8 >> 4) & s == 0
                    for i in range(nx):
                        if not i & s:
                            a, b = tiles[i], tiles[i | s]
                            tiles[i] = jnp.where(clear_bit, a, pltpu.roll(b, 16 * s, 1))
                            tiles[i | s] = jnp.where(clear_bit, pltpu.roll(a, 128 - 16 * s, 1), b)
                for i in range(nz):
                    inv[top : top + 8, pl.ds((i * ny + j) * 128, 128)] = tiles[i]

    def stage_static(x, carry):
        mobility = interleaved(mob_in, x)
        mob[x + 1] = mobility
        stage_plane(MOB, x, mobility)
        labels = lab[x]
        stage_rows(lys, x, labels)
        lt[x] = pack_plane(labels)
        return carry

    loads[0].wait()
    loads[1].wait()
    sums = lax.fori_loop(0, cx, restrict_rhs, no_sums, unroll=4)
    line = jnp.sum(placed(label_sums(sums), gx), axis=0, keepdims=True)
    loads[3].wait()
    order_columns()
    loads[2].wait()
    lax.fori_loop(0, cx, stage_static, 0, unroll=4)
    stage_end(MOB)
    for half in range(2):
        lzs[half] = pack_end(lt, half)
    pl.semaphore_wait(barrier, len(partners))
    G1_first[pl.ds(phases[0][0], 1), :] = line
    phase_start(0, 0)
    exchange_start(MOB)
    exchange_start(LAB)
    exchange_start(INV)

    def faces():
        exchange_wait(MOB)
        for half in range(2):
            fzp[half] = 0.5 * (zs[MOB, half] + far(zh.at[MOB], half))
            spread(fzp[half], half)
        for low in range(2):
            fyb[low] = 0.5 * (ys[MOB, low] + yh[MOB, low])
            ey[low] = fyb[low]
        fx[0] = 0.5 * (mob[1] + mob[0])
        row = lax.broadcasted_iota(jnp.int32, (64, 128), 0)
        lane = lax.broadcasted_iota(jnp.int32, (64, 128), 1)

        def step(x, below):
            m = mob[x + 1]
            above = 0.5 * (mob[x + 2] + m)
            face_y = jnp.where(row == 63, 0.0, 0.5 * (next_row(m) + m))
            face_z = jnp.where(lane == 127, 0.0, 0.5 * (pltpu.roll(m, 127, 1) + m))
            edges = edge_tiles(x)
            diag = (
                (below + above)
                + (last_row(face_y) + face_y)
                + (pltpu.roll(face_z, 1, 1) + face_z)
                + edges
            )
            rim[x] = edges
            fx[x + 1] = above
            fy[x] = face_y
            fz[x] = face_z
            dinv[x] = 1.0 / diag
            return above

        lax.fori_loop(0, cx, step, fx[0], unroll=4)
        exchange_wait(LAB)
        for half in range(2):
            lzf[half] = far(lzh, half)

    for ref in (direction, ws, yrim_x, yrim_y, yrim_z, prim_y, prim_z):
        clear(ref)
    phase_wait(0, 0)
    G2_first[phases[1][0]] = jnp.concatenate(
        [jnp.sum(G1_first[nx * c : nx * (c + 1)], axis=0, keepdims=True) for c in range(2)], axis=0
    )
    phase_start(0, 1)
    faces()
    phase_wait(0, 1)

    exchange_wait(INV)
    lines = coarse(0)

    own_splats = splats_of(lines[6])

    def first_iterate(x):
        plane = take_plane(own_splats, x)
        x0[x + 1] = plane
        return plane

    x_far, *rest = rim_of(lines)
    x0[0] = x_far[0]
    x0[cx + 1] = x_far[1]
    outer_faces(*rest)

    def first_residual(x, k, v, out, dot):
        rows = slice(8 * k, 8 * k + 8)
        residual = rhs[x, rows] - out
        precond = residual * dinv[x, rows]
        rs[x, rows] = residual
        field[x + 1, rows] = precond
        return dot + residual * precond

    ry_part = apply_all(x0, first_residual, zero, edge_part, first_iterate, 0)
    stage_end(0)

    def tall(row):
        return jnp.broadcast_to(row, (8, 128))

    def one_step(k, carry):
        ry, lines, dots, _, last_alpha = carry
        ry = ry[0:1]
        sums, parts = coarse_right_side(k)
        gather(
            k + 1,
            message(sums, parts, dots),
            lambda: exchange_start(k),
            lambda: exchange_wait(k),
        )
        more = coarse(k + 1)
        d0, d1, d2 = dots_of(k + 1)
        first = lax.broadcasted_iota(jnp.int32, (1, 128), 0) + k == 0
        alpha = jnp.where(first, 0.0, ry / d0)
        ry_next = jnp.where(first, d0, ry + alpha * (alpha * d2 - 2.0 * d1))
        beta = jnp.where(first, 0.0, ry_next / ry)
        gain = jnp.where(first, 1.0, -alpha)
        lines = [line + gain * extra for line, extra in zip(lines, more)]

        x_far, y_own, y_far, z_own, z_far = rim_of(lines)
        for low in range(2):
            outer = cx + 1 if low else 0
            layer = yrim_x[low] + gain * xh[k, low]
            yrim_x[low] = layer
            direction[outer] = (layer + beta * direction[outer]) - x_far[low]
        rows = [ys[k, 0], ys[k, 1], yh[k, 0], yh[k, 1]]
        packs = [zs[k, 0], zs[k, 1], far(zh.at[k], 0), far(zh.at[k], 1)]
        for i, (y_part, z_part) in enumerate(zip(y_own + y_far, z_own + z_far)):
            row = yrim_y[i] + gain * rows[i]
            pack = yrim_z[i] + gain * packs[i]
            yrim_y[i] = row
            yrim_z[i] = pack
            prim_y[i] = (row + beta * prim_y[i]) - y_part
            prim_z[i] = (pack + beta * prim_z[i]) - z_part
        outer_faces(
            [prim_y[0], prim_y[1]],
            [prim_y[2], prim_y[3]],
            [prim_z[0], prim_z[1]],
            [prim_z[2], prim_z[3]],
        )

        splats = splats_of(lines[6])

        def next_direction(x):
            residual = rs[x] - alpha * ws[x]
            rs[x] = residual
            plane = (residual * dinv[x] + beta * direction[x + 1]) - take_plane(splats, x)
            direction[x + 1] = plane
            history[k, x] = plane
            return plane

        def image(x, i, v, out, dots):
            rows = slice(8 * i, 8 * i + 8)
            z = out * dinv[x, rows]
            ws[x, rows] = out
            field[x + 1, rows] = z
            return dots[0] + v * out, dots[1] + rs[x, rows] * z, dots[2] + out * z

        dots = apply_all(direction, image, (zero, zero, zero), edge_part, next_direction, k + 1)
        stage_end(k + 1)
        return tall(ry_next), lines, dots, last_alpha, tall(alpha)

    ry, _, dots, *alphas = lax.fori_loop(
        0, STEPS, one_step, (zero + 1.0, [jnp.zeros((16, 128), F32)] * 7, (ry_part, zero, zero), zero, zero)
    )
    ry, alphas = ry[0:1], [alpha[0:1] for alpha in alphas]

    stores = [
        pltpu.make_async_copy(ordered.at[i], out, out_sem.at[i])
        for i, out in enumerate((x_hbm, p_hbm, r_hbm, w_hbm))
    ]
    G1_last[pl.ds(phases[0][0], 1), :] = jnp.sum(dots[0], axis=0, keepdims=True)
    phase_start(STEPS + 1, 0)

    def join_iterate(x, carry):
        joined = (x0[x + 1] + alphas[0] * history[0, x]) + alphas[1] * history[1, x]
        for i, plane in enumerate((joined, history[STEPS - 1, x], rs[x], ws[x])):
            store_in_order(ordered.at[i], x, plane)
        return carry

    lax.fori_loop(0, cx, join_iterate, 0, unroll=4)
    for store in stores:
        store.start()
    phase_wait(STEPS + 1, 0)
    G2_last[pl.ds(phases[1][0], 1), :] = jnp.sum(G1_last[...], axis=0, keepdims=True)
    phase_start(STEPS + 1, 1)
    phase_wait(STEPS + 1, 1)
    total = jnp.sum(jnp.sum(G2_last[...], axis=0, keepdims=True), axis=1, keepdims=True)
    step_out[...] = jnp.broadcast_to(ry / total, step_out.shape)
    for store in stores:
        store.wait()


def solution(mesh):
    nx, ny, nz = mesh.shape["gx"], mesh.shape["gy"], mesh.shape["gz"]

    def per_device(rhs, mobility, labels, coarse_inverse):
        cx, cy, cz = rhs.shape
        hbm = pl.BlockSpec(memory_space=pl.ANY)

        def vmem(*shape, dtype=F32):
            return pltpu.VMEM(shape, dtype)

        i32 = jnp.int32
        xs, p, rs, w, alpha = pl.pallas_call(
            functools.partial(kernel, nx, ny, nz),
            out_shape=[jax.ShapeDtypeStruct(rhs.shape, F32)] * 4
            + [jax.ShapeDtypeStruct((cy, cz), F32)],
            in_specs=[hbm] * 4,
            out_specs=[hbm] * 4 + [pl.BlockSpec(memory_space=pltpu.VMEM)],
            scratch_shapes=[
                *[vmem(cx + 2, cy, cz) for _ in range(4)],
                vmem(STEPS, cx, cy, cz),
                vmem(cx, cy, cz),
                vmem(cx, cy, cz, dtype=i32),
                vmem(cx, cy, cz),
                vmem(cx, cy, cz),
                vmem(cx, cy, cz, dtype=i32),
                vmem(*coarse_inverse.shape),
                vmem(*coarse_inverse.shape),
                vmem(6, *coarse_inverse.shape),
                vmem(cx + 1, cy, cz),
                *[vmem(cx, cy, cz) for _ in range(4)],
                vmem(4, cx, cy, cz),
                vmem(2, cx, cz),
                vmem(2, 8, 128),
                vmem(4, cx, cy, cz),
                *[vmem(cx, cy, cz) for _ in range(2)],
                vmem(STEPS, 2, cy, cz),
                vmem(4, 2, cx, cz),
                vmem(4, 2, cx, cz),
                vmem(4, 2, 8, 128),
                vmem(4, 2, 2, 8, 128),
                vmem(2, cy, cz, dtype=i32),
                vmem(2, cx, cz, dtype=i32),
                vmem(2, cx, cz, dtype=i32),
                vmem(2, 8, 128, dtype=i32),
                vmem(2, 2, 8, 128, dtype=i32),
                vmem(2, 8, 128, dtype=i32),
                vmem(2, cy, cz),
                vmem(4, cx, cz),
                vmem(4, 8, 128),
                vmem(4, cx, cz),
                vmem(4, 8, 128),
                vmem(cx, 8, 128),
                vmem(cx, 8, 128, dtype=i32),
                vmem(cx, 8, 128),
                vmem(2, cx, cz),
                vmem(2 * nx, 128),
                vmem(ny * nz // 2, 2, 128),
                vmem(STEPS, 2 * nx, 6, 128),
                vmem(STEPS, ny * nz // 2, 9, 128),
                vmem(2 * nx, 128),
                vmem(ny * nz // 2, 128),
                pltpu.SemaphoreType.DMA((4,)),
                pltpu.SemaphoreType.DMA((4,)),
                pltpu.SemaphoreType.DMA((6, 6)),
                pltpu.SemaphoreType.DMA((6, 6)),
                pltpu.SemaphoreType.DMA((5, 2)),
                pltpu.SemaphoreType.DMA((5, 2)),
            ],
            compiler_params=pltpu.CompilerParams(
                collective_id=0, has_side_effects=True, vmem_limit_bytes=VMEM_BYTES
            ),
            name="deflated_cg",
        )(rhs, mobility, labels, coarse_inverse)
        return xs + alpha * p, rs - alpha * w

    spec = P("gx", "gz", "gy")
    return jax.shard_map(
        per_device,
        mesh=mesh,
        in_specs=(spec, spec, spec, P(("gx", "gy", "gz"), None)),
        out_specs=(spec, spec),
        check_vma=False,
    )
```

```python
import functools

import jax
import jax.numpy as jnp
from jax import lax
from jax.experimental import pallas as pl
from jax.experimental.pallas import tpu as pltpu
from jax.sharding import PartitionSpec as P

LOGICAL = pl.DeviceIdType.LOGICAL
F32 = jnp.float32
LOOP = 15
VMEM_BYTES = 64 * 1024 * 1024 - 256 * 1024

STEPS = 3
MOB, LAB, INV = range(STEPS, STEPS + 3)


def farthest_first(n):
    return sorted(range(n), key=lambda k: -min(k, n - k))


def kernel(
    nx,
    ny,
    nz,
    rhs_hbm,
    mob_hbm,
    lab_hbm,
    inv_hbm,
    x_hbm,
    p_hbm,
    r_hbm,
    w_hbm,
    step_out,
    mob,
    x0,
    field,
    direction,
    history,
    rhs_in,
    lab_in,
    mob_in,
    rhs,
    lab,
    inv_in,
    inv,
    inv_far,
    fx,
    fy,
    fz,
    dinv,
    rim,
    bits,
    fyb,
    fzp,
    ordered,
    rs,
    ws,
    xh,
    ys,
    yh,
    zs,
    zh,
    lxh,
    lys,
    lyh,
    lzs,
    lzh,
    lzf,
    yrim_x,
    yrim_y,
    yrim_z,
    prim_y,
    prim_z,
    zt,
    lt,
    et,
    ey,
    G1_first,
    G2_first,
    G1,
    G2,
    G1_last,
    G2_last,
    in_sem,
    out_sem,
    hs_sem,
    hr_sem,
    gs_sem,
    gr_sem,
):
    cx = rhs.shape[0]
    gx, gy, gz = lax.axis_index("gx"), lax.axis_index("gy"), lax.axis_index("gz")
    def logical(x, y, z):
        return (lax.rem(x, nx) * ny + lax.rem(y, ny)) * nz + lax.rem(z, nz)

    sides = (
        ("gx", gx > 0, logical(gx + nx - 1, gy, gz)),
        ("gx", gx < nx - 1, logical(gx + 1, gy, gz)),
        ("gz", gz > 0, logical(gx, gy, gz + nz - 1)),
        ("gz", gz < nz - 1, logical(gx, gy, gz + 1)),
        ("gy", gy > 0, logical(gx, gy + ny - 1, gz)),
        ("gy", gy < ny - 1, logical(gx, gy + 1, gz)),
    )

    loads = [
        pltpu.make_async_copy(rhs_hbm, rhs_in, in_sem.at[0]),
        pltpu.make_async_copy(lab_hbm, lab_in, in_sem.at[1]),
        pltpu.make_async_copy(mob_hbm, mob_in, in_sem.at[2]),
        pltpu.make_async_copy(inv_hbm, inv_in, in_sem.at[3]),
    ]
    for load in loads:
        load.start()

    barrier = pltpu.get_barrier_semaphore()
    chips = nz // 2
    chip, core = lax.div(gz, 2), lax.rem(gz, 2)
    line_peers = [
        logical(gx + k, gy, 2 * chip + lax.rem(core + c, 2))
        for k in farthest_first(nx)
        for c in (1, 0)
        if k or c
    ]
    plane_peers = [
        logical(gx, gy + j, gz + 2 * k)
        for j in farthest_first(ny)
        for k in farthest_first(chips)
        if j or k
    ]
    phases = ((core * nx + gx, line_peers), (gy * chips + chip, plane_peers))
    partners = line_peers + plane_peers + [logical(gx, gy, gz + nz - 1 + 2 * core)]
    for partner in partners:
        pl.semaphore_signal(barrier, inc=1, device_id=partner, device_id_type=LOGICAL)

    def clear(ref, *index):
        ref[index or Ellipsis] = jnp.zeros(ref.shape[len(index) :], ref.dtype)

    for low in range(2):

        @pl.when(gx == (nx - 1 if low else 0))
        def _():
            clear(mob, cx + 1 if low else 0)
            clear(lxh, low)
            for e in range(STEPS):
                clear(xh, e, low)

        @pl.when(gz == (nz - 1 if low else 0))
        def _():
            clear(lyh, low)
            for e in range(STEPS + 1):
                clear(yh, e, low)

        @pl.when(gy == (ny - 1 if low else 0))
        def _():
            clear(lzh, low)
            for e in range(STEPS + 1):
                clear(zh, e, low)

    clear(field, 0)
    clear(field, cx + 1)

    lane8 = lax.broadcasted_iota(jnp.int32, (8, 128), 1)
    row8 = lax.broadcasted_iota(jnp.int32, (8, 128), 0)
    lane16 = lax.broadcasted_iota(jnp.int32, (16, 128), 1)
    row16 = lax.broadcasted_iota(jnp.int32, (16, 128), 0)
    pair = ((lane8 + 1) >> 1) & 63
    ends = (lane8 == 0) | (lane8 == 127)
    even = (lane8 & 1) == 0
    zero = jnp.zeros((8, 128), F32)

    def interleaved(ref, x):
        return jnp.concatenate([ref[x, pl.ds(k, 8, stride=8), :] for k in range(8)], axis=0)

    def store_in_order(ref, x, plane):
        for k in range(8):
            ref[x, pl.ds(k, 8, stride=8), :] = plane[8 * k : 8 * k + 8]

    def next_row(plane):
        return jnp.concatenate([plane[8:], pltpu.roll(plane[:8], 7, 0)], axis=0)

    def last_row(plane):
        return jnp.concatenate([pltpu.roll(plane[56:], 1, 0), plane[:56]], axis=0)

    def fold(plane):
        tiles = [plane[k : k + 8] for k in range(0, plane.shape[0], 8)]
        while len(tiles) > 1:
            tiles = [a + b for a, b in zip(tiles[::2], tiles[1::2])]
        return tiles[0]

    def halo_copy(e, side):
        axis, _, index = sides[side]
        low, other = side & 1, 1 - (side & 1)
        kind = e if isinstance(e, int) else 0
        if kind == INV:
            src, dst = inv, inv_far.at[side ^ 1]
        elif kind == LAB:
            if axis == "gx":
                src, dst = lab.at[cx - 1 if low else 0], lxh.at[other]
            elif axis == "gz":
                src, dst = lys.at[low], lyh.at[other]
            else:
                src, dst = lzs, lzh.at[other]
        elif axis == "gx":
            src = (mob if kind == MOB else field).at[cx if low else 1]
            dst = mob.at[0 if low else cx + 1] if kind == MOB else xh.at[e, other]
        elif axis == "gz":
            src, dst = ys.at[e, low], yh.at[e, other]
        else:
            src, dst = zs.at[e], zh.at[e, other]
        return pltpu.make_async_remote_copy(
            src_ref=src,
            dst_ref=dst,
            send_sem=hs_sem.at[e, side],
            recv_sem=hr_sem.at[e, side ^ 1],
            device_id=index,
            device_id_type=LOGICAL,
        )

    def halo_landed(e, side):
        low = side & 1
        kind = e if isinstance(e, int) else 0
        if kind == INV:
            ref = inv_far.at[side]
        elif kind == LAB:
            ref = (lxh, lyh, lzh)[side // 2].at[low]
        elif side < 2:
            ref = mob.at[cx + 1 if low else 0] if kind == MOB else xh.at[e, low]
        else:
            ref = (yh, zh)[side // 2 - 1].at[e, low]
        return pltpu.make_async_copy(ref, ref, hr_sem.at[e, side])

    def exchange_start(e):
        for side in (0, 1, 4, 5, 2, 3):

            @pl.when(sides[side][1])
            def _():
                halo_copy(e, side).start()

    def exchange_wait(e):
        for side in range(6):

            @pl.when(sides[side][1])
            def _():
                halo_landed(e, side).wait()
                halo_copy(e, side).wait_send()

    def stage_rows(rows, x, plane):
        rows[0, pl.ds(x, 1), :] = plane[0:1]
        rows[1, pl.ds(x, 1), :] = plane[63:64]

    def pack_plane(plane):
        packed = plane[0:8]
        for k in range(1, 8):
            packed = jnp.where(pair == k, pltpu.roll(plane[8 * k : 8 * k + 8], 2 * k, 1), packed)
        return jnp.where(pair < 8, packed, jnp.zeros_like(packed))

    def pack_end(tiles, half):
        total = tiles[8 * half]
        for k in range(1, 8):
            total = total + pltpu.roll(tiles[8 * half + k], 16 * k, 1)
        return total

    def stage_plane(e, x, plane):
        stage_rows(ys.at[e], x, plane)
        zt[x] = pack_plane(plane)

    def stage_end(e):
        for half in range(2):
            zs[e, half] = pack_end(zt, half)

    def far(received, half):
        return jnp.where(
            even, pltpu.roll(received[0, half], 1, 1), pltpu.roll(received[1, half], 127, 1)
        )

    def spread(packed, half):
        et[8 * half] = packed
        for k in range(1, 8):
            et[8 * half + k] = pltpu.roll(packed, 128 - 16 * k, 1)

    def edge_part(x, v):
        return edge_tiles(x)

    def edge_tiles(x):
        tile = et[x]
        tiles = [
            jnp.where(ends, tile if k == 0 else pltpu.roll(tile, 128 - 2 * k, 1), 0.0)
            for k in range(8)
        ]
        first, last = ey[0, pl.ds(x, 1), :], ey[1, pl.ds(x, 1), :]
        tiles[0] = tiles[0] + jnp.where(row8 == 0, first, 0.0)
        tiles[7] = tiles[7] + jnp.where(row8 == 7, last, 0.0)
        return jnp.concatenate(tiles, axis=0)

    def apply_all(values, body, init, outer, make=None):
        def step(x, carry, above_v):
            below, v, rest = carry
            above = fx[x + 1] * (above_v - v)
            flux_y = fy[x] * (next_row(v) - v)
            flux_z = fz[x] * (pltpu.roll(v, 127, 1) - v)
            out = (
                (below - above)
                + (last_row(flux_y) - flux_y)
                + (pltpu.roll(flux_z, 1, 1) - flux_z)
                + outer(x, v)
            )
            return above, above_v, body(x, v, out, rest)

        if make is None:

            def make(x):
                return values[x + 1]

        v = make(0)
        carry = (fx[0] * (v - values[0]), v, init)
        carry = lax.fori_loop(
            0, cx - 1, lambda x, c: step(x, c, make(x + 1)), carry, unroll=LOOP
        )
        return step(cx - 1, carry, values[cx + 1])[2]

    def add_tile(sums, tile, tile_bits):
        terms = [tile]
        for bit in tile_bits:
            terms = terms + [term * bit for term in terms]
        return [total + term for total, term in zip(sums, terms)]

    def label_sums(sums):
        sums = list(sums)
        for i in range(4):
            for value in range(16):
                if not value >> i & 1:
                    sums[value] = sums[value] - sums[value | 1 << i]
        return sums

    def bits_of(labels):
        return [((labels >> i) & 1).astype(F32) for i in range(4)]

    def by_label(labels, values):
        sums = no_sums
        for k in range(0, values.shape[0], 8):
            sums = add_tile(sums, values[k : k + 8], bits_of(labels[k : k + 8]))
        return label_sums(sums)

    def restrict_plane(x, plane, sums):
        for k in range(0, 64, 8):
            tile_bits = [bits[i, x, k : k + 8] for i in range(4)]
            sums = add_tile(sums, plane[k : k + 8], tile_bits)
        return tuple(sums)

    def restrict_rhs(x, sums):
        for k in range(8):
            labels = lab_in[x, pl.ds(k, 8, stride=8), :]
            values = rhs_in[x, pl.ds(k, 8, stride=8), :]
            tile_bits = bits_of(labels)
            rows = slice(8 * k, 8 * k + 8)
            lab[x, rows] = labels
            rhs[x, rows] = values
            for i in range(4):
                bits[i, x, rows] = tile_bits[i]
            sums = add_tile(sums, values, tile_bits)
        return tuple(sums)

    no_sums = (zero,) * 16

    def rows_of(tiles):
        for shift in (4, 2, 1):
            low = (row8 & shift) == 0
            half = len(tiles) // 2
            merged = []
            for a, b in zip(tiles[:half], tiles[half:]):
                kept, moved = jnp.where(low, a, b), jnp.where(low, b, a)
                if shift == 4:
                    moved = pltpu.roll(moved, 4, 0)
                else:
                    moved = jnp.where(
                        low, pltpu.roll(moved, 8 - shift, 0), pltpu.roll(moved, shift, 0)
                    )
                merged.append(kept + moved)
            tiles = merged
        return tiles[0]

    def placed(sums, block):
        rows = jnp.concatenate([rows_of(list(sums[:8])), rows_of(list(sums[8:]))], axis=0)
        column = jnp.sum(rows, axis=1, keepdims=True)
        return fold(jnp.where(lane16 == 16 * block + row16, column, 0.0))

    def message(sums, parts, dots):
        tiles = [placed(sums, gx) + placed(parts[0], gx - 1) + placed(parts[1], gx + 1)]
        for side in (4, 5, 2, 3):
            tiles.append(placed(parts[side], gx))
        joined = zero
        for k, dot in enumerate(dots):
            dot = dot + pltpu.roll(dot, 64, 1)
            joined = jnp.where(lane8 >> 5 == k, dot + pltpu.roll(dot, 32, 1), joined)
        return rows_of(tiles + [joined, zero, zero])[:6]

    def neighbour_parts(e):
        parts = [
            by_label(lxh[0], -(fx[0] * field[1])),
            by_label(lxh[1], -(fx[cx] * field[cx])),
        ]
        for low in range(2):
            parts.append(by_label(lyh[low], -(fyb[low] * ys[e, low])))
        for keep in (even, ~even):
            halves = [
                by_label(lzf[half], jnp.where(keep, -(fzp[half] * zs[e, half]), 0.0))
                for half in range(2)
            ]
            parts.append([a + b for a, b in zip(*halves)])
        return parts

    def coarse_right_side(e):
        sums = apply_all(
            field, lambda x, v, out, s: restrict_plane(x, out, s), no_sums, lambda x, v: rim[x] * v
        )
        return label_sums(sums), neighbour_parts(e)

    def slots_of(g, ph):
        if isinstance(g, int):
            return ((G1_first, G2_first), (G1_last, G2_last))[g != 0][ph]
        return (G1, G2)[ph].at[g - 1]

    def phase_slots(g, ph, first, count):
        slots = slots_of(g, ph)
        return slots.at[pl.ds(first, count)]

    def phase_start(g, ph):
        me, peers = phases[ph]
        slot = phase_slots(g, ph, me, 1)
        for peer in peers:
            pltpu.make_async_remote_copy(
                src_ref=slot,
                dst_ref=slot,
                send_sem=gs_sem.at[g, ph],
                recv_sem=gr_sem.at[g, ph],
                device_id=peer,
                device_id_type=LOGICAL,
            ).start()

    def phase_wait(g, ph):
        part = phase_slots(g, ph, 0, len(phases[ph][1]))
        pltpu.make_async_copy(part, part, gr_sem.at[g, ph]).wait()
        pltpu.make_async_copy(part, part, gs_sem.at[g, ph]).wait()

    def gather(g, tile, started, between):
        G1[g - 1, phases[0][0]] = tile
        phase_start(g, 0)
        started()
        phase_wait(g, 0)
        low, high = [jnp.sum(G1[g - 1, nx * c : nx * (c + 1)], axis=0) for c in range(2)]
        slot = phases[1][0]
        rows = [
            low[0:1] + high[3:4],
            high[0:1] + low[4:5],
            low[1:2],
            high[1:2],
            low[2:3],
            high[2:3],
            low[3:4],
            high[4:5],
            low[5:6] + high[5:6],
        ]
        for k, row in enumerate(rows):
            G2[g - 1, slot, k : k + 1] = row
        phase_start(g, 1)
        between()
        phase_wait(g, 1)

    def dots_of(g):
        row = jnp.sum(G2[g - 1, :, 8:9], axis=0)
        lane = lax.broadcasted_iota(jnp.int32, (1, 128), 1)
        return [
            jnp.broadcast_to(
                jnp.sum(jnp.where(lane >> 5 == k, row, 0.0), axis=1, keepdims=True), (1, 128)
            )
            for k in range(3)
        ]

    def right_side(g):
        def row(slot, k):
            if isinstance(g, int):
                return jnp.broadcast_to(G2_first[slot, k : k + 1], (8, 128))
            return jnp.broadcast_to(G2[g - 1, slot, k : k + 1], (8, 128))

        rows = [[None] * ny for _ in range(nz)]
        for j in range(ny):
            for k in range(chips):
                slot = j * chips + k
                for c in range(2):
                    total = row(slot, c)
                    if not isinstance(g, int):
                        if j + 1 < ny:
                            total = total + row(slot + chips, 2 + c)
                        if j > 0:
                            total = total + row(slot - chips, 4 + c)
                        if c == 0 and k > 0:
                            total = total + row(slot - 1, 7)
                        if c == 1 and k + 1 < chips:
                            total = total + row(slot + 1, 6)
                    rows[2 * k + c][j] = total
        return rows

    def coarse(g):
        accs = [jnp.zeros((16, 128), F32) for _ in range(7)]
        for i, rows in enumerate(right_side(g)):
            for j in range(ny):
                columns = slice((i * ny + j) * 128, (i * ny + j + 1) * 128)
                row = jnp.concatenate([rows[j], rows[j]], axis=0)
                accs[6] = accs[6] + inv[:, columns] * row
                for side in range(6):
                    accs[side] = accs[side] + inv_far[side, :, columns] * row
        values = []
        for side in range(7):
            total = jnp.broadcast_to(jnp.sum(accs[side], axis=1, keepdims=True), (16, 128))
            if side < 6:
                index = row16 * 0 + (gx, gz, gy)[side // 2]
                edge = (0, (nx, nz, ny)[side // 2] - 1)[side & 1]
                total = jnp.where(index == edge, 0.0, total)
            values.append(total)
        return values

    def splats_of(values):
        return [jnp.broadcast_to(values[m : m + 1], (8, 128)) for m in range(16)]

    def pick(splats, masks):
        if len(splats) == 1:
            return splats[0]
        half = len(splats) // 2
        return jnp.where(
            masks[-1], pick(splats[half:], masks[:-1]), pick(splats[:half], masks[:-1])
        )

    def masks_of(labels):
        return [labels & (1 << i) != 0 for i in range(4)]

    def take(splats, labels):
        tiles = [
            pick(splats, masks_of(labels[k : k + 8])) for k in range(0, labels.shape[0], 8)
        ]
        return jnp.concatenate(tiles, axis=0)

    def take_plane(splats, x):
        tiles = [
            pick(splats, [bits[i, x, k : k + 8] > 0.5 for i in range(4)]) for k in range(0, 64, 8)
        ]
        return jnp.concatenate(tiles, axis=0)

    def rim_of(values):
        splats = [splats_of(value) for value in values]
        x_far = [take(splats[low], lxh[low]) for low in range(2)]
        y_own = [take(splats[6], lys[low]) for low in range(2)]
        y_far = [take(splats[2 + low], lyh[low]) for low in range(2)]
        z_own = [take(splats[6], lzs[half]) for half in range(2)]
        z_far = [
            jnp.where(even, take(splats[4], lzf[half]), take(splats[5], lzf[half]))
            for half in range(2)
        ]
        return x_far, y_own, y_far, z_own, z_far

    def outer_faces(y_own, y_far, z_own, z_far):
        for low in range(2):
            ey[low] = fyb[low] * (y_own[low] - y_far[low])
        for half in range(2):
            spread(fzp[half] * (z_own[half] - z_far[half]), half)

    def order_columns():
        for top in (0, 8):
            for j in range(ny):
                tiles = [inv_in[top : top + 8, pl.ds((i * ny + j) * 128, 128)] for i in range(nx)]
                for s in (4, 2, 1):
                    clear_bit = (lane8 >> 4) & s == 0
                    for i in range(nx):
                        if not i & s:
                            a, b = tiles[i], tiles[i | s]
                            tiles[i] = jnp.where(clear_bit, a, pltpu.roll(b, 16 * s, 1))
                            tiles[i | s] = jnp.where(clear_bit, pltpu.roll(a, 128 - 16 * s, 1), b)
                for i in range(nz):
                    inv[top : top + 8, pl.ds((i * ny + j) * 128, 128)] = tiles[i]

    def stage_static(x, carry):
        mobility = interleaved(mob_in, x)
        mob[x + 1] = mobility
        stage_plane(MOB, x, mobility)
        labels = lab[x]
        stage_rows(lys, x, labels)
        lt[x] = pack_plane(labels)
        return carry

    loads[0].wait()
    loads[1].wait()
    sums = lax.fori_loop(0, cx, restrict_rhs, no_sums, unroll=4)
    line = jnp.sum(placed(label_sums(sums), gx), axis=0, keepdims=True)
    loads[3].wait()
    order_columns()
    loads[2].wait()
    lax.fori_loop(0, cx, stage_static, 0, unroll=4)
    stage_end(MOB)
    for half in range(2):
        lzs[half] = pack_end(lt, half)
    pl.semaphore_wait(barrier, len(partners))
    G1_first[pl.ds(phases[0][0], 1), :] = line
    phase_start(0, 0)
    exchange_start(MOB)
    exchange_start(LAB)
    exchange_start(INV)

    def faces():
        for ref in (direction, ws, yrim_x, yrim_y, yrim_z, prim_y, prim_z):
            clear(ref)
        exchange_wait(MOB)
        exchange_wait(LAB)
        for half in range(2):
            lzf[half] = far(lzh, half)
            fzp[half] = 0.5 * (zs[MOB, half] + far(zh.at[MOB], half))
            spread(fzp[half], half)
        for low in range(2):
            fyb[low] = 0.5 * (ys[MOB, low] + yh[MOB, low])
            ey[low] = fyb[low]
        fx[0] = 0.5 * (mob[1] + mob[0])
        row = lax.broadcasted_iota(jnp.int32, (64, 128), 0)
        lane = lax.broadcasted_iota(jnp.int32, (64, 128), 1)

        def step(x, below):
            m = mob[x + 1]
            above = 0.5 * (mob[x + 2] + m)
            face_y = jnp.where(row == 63, 0.0, 0.5 * (next_row(m) + m))
            face_z = jnp.where(lane == 127, 0.0, 0.5 * (pltpu.roll(m, 127, 1) + m))
            edges = edge_tiles(x)
            diag = (
                (below + above)
                + (last_row(face_y) + face_y)
                + (pltpu.roll(face_z, 1, 1) + face_z)
                + edges
            )
            rim[x] = edges
            fx[x + 1] = above
            fy[x] = face_y
            fz[x] = face_z
            dinv[x] = 1.0 / diag
            return above

        lax.fori_loop(0, cx, step, fx[0], unroll=4)

    phase_wait(0, 0)
    G2_first[phases[1][0]] = jnp.concatenate(
        [jnp.sum(G1_first[nx * c : nx * (c + 1)], axis=0, keepdims=True) for c in range(2)], axis=0
    )
    phase_start(0, 1)
    faces()
    phase_wait(0, 1)

    exchange_wait(INV)
    lines = coarse(0)

    own_splats = splats_of(lines[6])

    def first_iterate(x):
        plane = take_plane(own_splats, x)
        x0[x + 1] = plane
        return plane

    x_far, *rest = rim_of(lines)
    x0[0] = x_far[0]
    x0[cx + 1] = x_far[1]
    outer_faces(*rest)

    def first_residual(x, v, out, dot):
        residual = rhs[x] - out
        precond = residual * dinv[x]
        rs[x] = residual
        field[x + 1] = precond
        stage_plane(0, x, precond)
        return dot + fold(residual * precond)

    ry_part = apply_all(x0, first_residual, zero, edge_part, first_iterate)
    stage_end(0)

    def tall(row):
        return jnp.broadcast_to(row, (8, 128))

    def one_step(k, carry):
        ry, lines, dots, _, last_alpha = carry
        ry = ry[0:1]
        sums, parts = coarse_right_side(k)
        gather(
            k + 1,
            message(sums, parts, dots),
            lambda: exchange_start(k),
            lambda: exchange_wait(k),
        )
        more = coarse(k + 1)
        d0, d1, d2 = dots_of(k + 1)
        first = lax.broadcasted_iota(jnp.int32, (1, 128), 0) + k == 0
        alpha = jnp.where(first, 0.0, ry / d0)
        ry_next = jnp.where(first, d0, ry + alpha * (alpha * d2 - 2.0 * d1))
        beta = jnp.where(first, 0.0, ry_next / ry)
        gain = jnp.where(first, 1.0, -alpha)
        lines = [line + gain * extra for line, extra in zip(lines, more)]

        x_far, y_own, y_far, z_own, z_far = rim_of(lines)
        for low in range(2):
            outer = cx + 1 if low else 0
            layer = yrim_x[low] + gain * xh[k, low]
            yrim_x[low] = layer
            direction[outer] = (layer + beta * direction[outer]) - x_far[low]
        rows = [ys[k, 0], ys[k, 1], yh[k, 0], yh[k, 1]]
        packs = [zs[k, 0], zs[k, 1], far(zh.at[k], 0), far(zh.at[k], 1)]
        for i, (y_part, z_part) in enumerate(zip(y_own + y_far, z_own + z_far)):
            row = yrim_y[i] + gain * rows[i]
            pack = yrim_z[i] + gain * packs[i]
            yrim_y[i] = row
            yrim_z[i] = pack
            prim_y[i] = (row + beta * prim_y[i]) - y_part
            prim_z[i] = (pack + beta * prim_z[i]) - z_part
        outer_faces(
            [prim_y[0], prim_y[1]],
            [prim_y[2], prim_y[3]],
            [prim_z[0], prim_z[1]],
            [prim_z[2], prim_z[3]],
        )

        splats = splats_of(lines[6])

        def next_direction(x):
            residual = rs[x] - alpha * ws[x]
            rs[x] = residual
            plane = (residual * dinv[x] + beta * direction[x + 1]) - take_plane(splats, x)
            direction[x + 1] = plane
            history[k, x] = plane
            return plane

        def image(x, v, out, dots):
            z = out * dinv[x]
            ws[x] = out
            field[x + 1] = z
            stage_plane(k + 1, x, z)
            return (
                dots[0] + fold(v * out),
                dots[1] + fold(rs[x] * z),
                dots[2] + fold(out * z),
            )

        dots = apply_all(direction, image, (zero, zero, zero), edge_part, next_direction)
        stage_end(k + 1)
        return tall(ry_next), lines, dots, last_alpha, tall(alpha)

    ry, _, dots, *alphas = lax.fori_loop(
        0, STEPS, one_step, (zero + 1.0, [jnp.zeros((16, 128), F32)] * 7, (ry_part, zero, zero), zero, zero)
    )
    ry, alphas = ry[0:1], [alpha[0:1] for alpha in alphas]

    stores = [
        pltpu.make_async_copy(ordered.at[i], out, out_sem.at[i])
        for i, out in enumerate((x_hbm, p_hbm, r_hbm, w_hbm))
    ]
    G1_last[pl.ds(phases[0][0], 1), :] = jnp.sum(dots[0], axis=0, keepdims=True)
    phase_start(STEPS + 1, 0)

    def join_iterate(x, carry):
        joined = (x0[x + 1] + alphas[0] * history[0, x]) + alphas[1] * history[1, x]
        for i, plane in enumerate((joined, history[STEPS - 1, x], rs[x], ws[x])):
            store_in_order(ordered.at[i], x, plane)
        return carry

    lax.fori_loop(0, cx, join_iterate, 0, unroll=4)
    for store in stores:
        store.start()
    phase_wait(STEPS + 1, 0)
    G2_last[pl.ds(phases[1][0], 1), :] = jnp.sum(G1_last[...], axis=0, keepdims=True)
    phase_start(STEPS + 1, 1)
    phase_wait(STEPS + 1, 1)
    total = jnp.sum(jnp.sum(G2_last[...], axis=0, keepdims=True), axis=1, keepdims=True)
    step_out[...] = jnp.broadcast_to(ry / total, step_out.shape)
    for store in stores:
        store.wait()


def solution(mesh):
    nx, ny, nz = mesh.shape["gx"], mesh.shape["gy"], mesh.shape["gz"]

    def per_device(rhs, mobility, labels, coarse_inverse):
        cx, cy, cz = rhs.shape
        hbm = pl.BlockSpec(memory_space=pl.ANY)

        def vmem(*shape, dtype=F32):
            return pltpu.VMEM(shape, dtype)

        i32 = jnp.int32
        xs, p, rs, w, alpha = pl.pallas_call(
            functools.partial(kernel, nx, ny, nz),
            out_shape=[jax.ShapeDtypeStruct(rhs.shape, F32)] * 4
            + [jax.ShapeDtypeStruct((cy, cz), F32)],
            in_specs=[hbm] * 4,
            out_specs=[hbm] * 4 + [pl.BlockSpec(memory_space=pltpu.VMEM)],
            scratch_shapes=[
                *[vmem(cx + 2, cy, cz) for _ in range(4)],
                vmem(STEPS, cx, cy, cz),
                vmem(cx, cy, cz),
                vmem(cx, cy, cz, dtype=i32),
                vmem(cx, cy, cz),
                vmem(cx, cy, cz),
                vmem(cx, cy, cz, dtype=i32),
                vmem(*coarse_inverse.shape),
                vmem(*coarse_inverse.shape),
                vmem(6, *coarse_inverse.shape),
                vmem(cx + 1, cy, cz),
                *[vmem(cx, cy, cz) for _ in range(4)],
                vmem(4, cx, cy, cz),
                vmem(2, cx, cz),
                vmem(2, 8, 128),
                vmem(4, cx, cy, cz),
                *[vmem(cx, cy, cz) for _ in range(2)],
                vmem(STEPS, 2, cy, cz),
                vmem(4, 2, cx, cz),
                vmem(4, 2, cx, cz),
                vmem(4, 2, 8, 128),
                vmem(4, 2, 2, 8, 128),
                vmem(2, cy, cz, dtype=i32),
                vmem(2, cx, cz, dtype=i32),
                vmem(2, cx, cz, dtype=i32),
                vmem(2, 8, 128, dtype=i32),
                vmem(2, 2, 8, 128, dtype=i32),
                vmem(2, 8, 128, dtype=i32),
                vmem(2, cy, cz),
                vmem(4, cx, cz),
                vmem(4, 8, 128),
                vmem(4, cx, cz),
                vmem(4, 8, 128),
                vmem(cx, 8, 128),
                vmem(cx, 8, 128, dtype=i32),
                vmem(cx, 8, 128),
                vmem(2, cx, cz),
                vmem(2 * nx, 128),
                vmem(ny * nz // 2, 2, 128),
                vmem(STEPS, 2 * nx, 6, 128),
                vmem(STEPS, ny * nz // 2, 9, 128),
                vmem(2 * nx, 128),
                vmem(ny * nz // 2, 128),
                pltpu.SemaphoreType.DMA((4,)),
                pltpu.SemaphoreType.DMA((4,)),
                pltpu.SemaphoreType.DMA((6, 6)),
                pltpu.SemaphoreType.DMA((6, 6)),
                pltpu.SemaphoreType.DMA((5, 2)),
                pltpu.SemaphoreType.DMA((5, 2)),
            ],
            compiler_params=pltpu.CompilerParams(
                collective_id=0, has_side_effects=True, vmem_limit_bytes=VMEM_BYTES
            ),
            name="deflated_cg",
        )(rhs, mobility, labels, coarse_inverse)
        return xs + alpha * p, rs - alpha * w

    spec = P("gx", "gz", "gy")
    return jax.shard_map(
        per_device,
        mesh=mesh,
        in_specs=(spec, spec, spec, P(("gx", "gy", "gz"), None)),
        out_specs=(spec, spec),
        check_vma=False,
    )
```
